32 devices in a mesh: ctx: 16 (over z, y, core), fsdp: 2 (over x).
Axes of the slice: x: 2, y: 2, z: 4, core: 2. Of those that a mesh axis runs over, the one named last changes fastest.
Arguments:
- tokens_in: bfloat16 [4, 2048, 1024], P('fsdp', 'ctx'), may hold values from -6 to 6
- gain_attn: bfloat16 [1024], P('fsdp'), may hold values from 0.5 to 1.5
- shift_attn: bfloat16 [1024], P('fsdp'), may hold values from -4 to 4
- w_heads: bfloat16 [1024, 3072], P('fsdp'), may hold values from -0.1875 to 0.1875
- bias_query: bfloat16 [1024], P('fsdp'), may hold values from -4 to 4
- bias_value: bfloat16 [1024], P('fsdp'), may hold values from -0.75 to 0.75
- w_merge: bfloat16 [1024, 1024], P('fsdp'), may hold values from -0.75 to 0.75
- bias_merge: bfloat16 [1024], P('fsdp'), may hold values from -4 to 4
- gain_mlp: bfloat16 [1024], P('fsdp'), may hold values from 0.5 to 1.5
- shift_mlp: bfloat16 [1024], P('fsdp'), may hold values from -4 to 4
- w_expand: bfloat16 [1024, 4096], P('fsdp'), may hold values from -0.1875 to 0.1875
- bias_expand: bfloat16 [4096], P('fsdp'), may hold values from -4 to 4
- w_contract: bfloat16 [4096, 1024], P('fsdp'), may hold values from -0.09375 to 0.09375
- bias_contract: bfloat16 [1024], P('fsdp'), may hold values from -4 to 4
- cotangent: bfloat16 [4, 2048, 1024], P('fsdp', 'ctx'), may hold values from -6 to 6
Outputs:
- block_out: bfloat16 [4, 2048, 1024], P('fsdp', 'ctx')
- grad_tokens: float32 [4, 2048, 1024], P('fsdp', 'ctx')
- grad_gain_attn: float32 [1024], P('fsdp')
- grad_shift_attn: float32 [1024], P('fsdp')
- grad_w_heads: float32 [1024, 3072], P('fsdp')
- grad_bias_query: float32 [1024], P('fsdp')
- grad_bias_value: float32 [1024], P('fsdp')
- grad_w_merge: float32 [1024, 1024], P('fsdp')
- grad_bias_merge: float32 [1024], P('fsdp')
- grad_gain_mlp: float32 [1024], P('fsdp')
- grad_shift_mlp: float32 [1024], P('fsdp')
- grad_w_expand: float32 [1024, 4096], P('fsdp')
- grad_bias_expand: float32 [4096], P('fsdp')
- grad_w_contract: float32 [4096, 1024], P('fsdp')
- grad_bias_contract: float32 [1024], P('fsdp')
The draws below stay inside these ranges and needn't reach their ends.
All inputs are finite; a program needn't handle non-finite values.
Results may differ from the reference program's by a relative error of at most 0.018.
Values may be sent and summed in bfloat16 or wider, within the bound.
No kernel may reach another device: no remote copies, remote signals or barrier semaphores. Data moves between devices by JAX's collectives and lax.ppermute only.
A program may use at most 384 MiB of HBM per device.

```python
import math
import jax
import jax.numpy as jnp
from jax import lax

D = 1024
HEADS = 16
HEAD = 64
FF = 4096
LENGTH = 2048
SEQS = 4


def block_scale(rng, shape, shards, low, high):
    gain = 1.0
    for dim, shards_of in shards:
        draws = jax.random.uniform(jax.random.fold_in(jax.random.fold_in(rng, 6), dim), (shards_of,), jnp.float32, low / len(shards), high / len(shards))
        gain = gain * jnp.repeat(jnp.exp(draws), shape[dim] // shards_of).reshape((-1,) + (1,) * (len(shape) - 1 - dim))
    return gain


def gaussian(key, extent, deviation, reach, cuts=(), held_as=jnp.bfloat16):
    level = block_scale(key, extent, cuts, -0.22, 0.18) if cuts else 1.0
    drawn = jax.random.normal(key, extent, jnp.float32) * deviation * level
    return jnp.minimum(jnp.maximum(drawn, -reach), reach).astype(held_as)


def setup_inputs(seed: int = 0) -> dict:
    splits = jax.random.split(jax.random.key(seed), 16)
    return {
        "tokens_in": gaussian(splits[0], (SEQS, LENGTH, D), 1.0, 6.0, ((0, 2), (1, 16))),
        "gain_attn": jnp.clip(1.0 + 0.1 * jax.random.normal(splits[1], (D,), jnp.float32), 0.5, 1.5).astype(jnp.bfloat16),
        "shift_attn": gaussian(splits[2], (D,), 0.3, 4.0, ((0, 2),)),
        "w_heads": gaussian(splits[3], (D, 3 * D), D ** -0.5, 0.1875, ((0, 2),)),
        "bias_query": gaussian(splits[4], (D,), 0.3, 4.0, ((0, 2),)),
        "bias_value": gaussian(splits[5], (D,), 0.05, 0.75, ((0, 2),)),
        "w_merge": gaussian(splits[6], (D, D), (D // 16) ** -0.5, 0.75, ((0, 2),)),
        "bias_merge": gaussian(splits[7], (D,), 0.3, 4.0, ((0, 2),)),
        "gain_mlp": jnp.clip(1.0 + 0.1 * jax.random.normal(splits[8], (D,), jnp.float32), 0.5, 1.5).astype(jnp.bfloat16),
        "shift_mlp": gaussian(splits[9], (D,), 0.3, 4.0, ((0, 2),)),
        "w_expand": gaussian(splits[10], (D, FF), D ** -0.5, 0.1875, ((0, 2),)),
        "bias_expand": gaussian(splits[11], (FF,), 0.3, 4.0, ((0, 2),)),
        "w_contract": gaussian(splits[12], (FF, D), FF ** -0.5, 0.09375, ((0, 2),)),
        "bias_contract": gaussian(splits[13], (D,), 0.3, 4.0, ((0, 2),)),
        "cotangent": gaussian(splits[14], (SEQS, LENGTH, D), 1.0, 6.0, ((0, 2), (1, 16))),
    }


@jax.custom_vjp
def low(v):
    return lax.optimization_barrier(v.astype(jnp.bfloat16)).astype(jnp.float32)

@jax.custom_vjp
def low_back(v):
    return v

def low_keep(v):
    return (low(v), None)

def low_pass(kept, grad):
    return (grad,)

def back_keep(v):
    return (v, None)

def back_low(kept, grad):
    return (low(grad),)
low.defvjp(low_keep, low_pass)
low_back.defvjp(back_keep, back_low)
epsilon = 1e-05
highest = lax.Precision.HIGHEST
masked_score = -1e+30

def layer_norm(inputs, gain_vec, shift_vec):
    row_mean = lax.optimization_barrier(jnp.mean(inputs, axis=-1, keepdims=True))
    centered = inputs - row_mean
    variance = lax.optimization_barrier(jnp.mean(centered * centered, axis=-1, keepdims=True))
    return centered * lax.rsqrt(variance + epsilon) * gain_vec + shift_vec

def attend_sequence(operands):
    queries, key_rows, value_rows = operands
    length = queries.shape[0]
    block_rows = min(512, length)
    nblocks = length // block_rows
    scale_now = 1.0 / math.sqrt(HEAD)
    q_blocks = queries.reshape(nblocks, block_rows, HEADS, HEAD)
    firsts = jnp.arange(nblocks, dtype=jnp.int32) * block_rows
    positions = jnp.arange(length, dtype=jnp.int32)

    def one_block(inputs):
        q_part, first_row = inputs
        scores = jnp.einsum('qhe,khe->hqk', q_part, key_rows, precision=highest) * scale_now
        scores = low_back(scores)
        q_pos = first_row + jnp.arange(block_rows, dtype=jnp.int32)
        allowed = (positions[None, :] <= q_pos[:, None])[None]
        masked = jnp.where(allowed, scores, masked_score)
        row_top = lax.optimization_barrier(jnp.max(masked, axis=-1, keepdims=True))
        weights = jnp.where(allowed, jnp.exp(masked - row_top), 0.0)
        totals = lax.optimization_barrier(jnp.sum(weights, axis=-1, keepdims=True))
        mixed = jnp.einsum('hqk,khe->hqe', low(weights), value_rows, precision=highest) / totals
        return jnp.transpose(mixed, (1, 0, 2))
    output = lax.map(jax.checkpoint(one_block), (q_blocks, firsts))
    return output.reshape(length, HEADS * HEAD)

def forward(tokens_in, gain_attn, shift_attn, w_heads, bias_query, bias_value, w_merge, bias_merge, gain_mlp, shift_mlp, w_expand, bias_expand, w_contract, bias_contract):
    seq_count, length, model_width = tokens_in.shape
    flat_rows = tokens_in.reshape(seq_count * length, model_width)
    normed = low(layer_norm(flat_rows, gain_attn, shift_attn))
    projected = jnp.dot(normed, w_heads, precision=highest)
    queries = low(low_back(projected[:, :model_width] + bias_query))
    key_all = low(low_back(projected[:, model_width:2 * model_width]))
    value_all = low(low_back(projected[:, 2 * model_width:] + bias_value))

    def as_heads(member):
        return member.reshape(seq_count, length, HEADS, HEAD)
    mixed = lax.map(attend_sequence, (as_heads(queries), as_heads(key_all), as_heads(value_all)))
    mixed = low(low_back(mixed.reshape(seq_count * length, model_width)))
    branch = low_back(jnp.dot(mixed, w_merge, precision=highest) + bias_merge)
    middle = flat_rows + branch
    normed_two = low(layer_norm(middle, gain_mlp, shift_mlp))
    inner_pre = low_back(jnp.dot(normed_two, w_expand, precision=highest) + bias_expand)
    active = low(jax.nn.gelu(inner_pre, approximate=True))
    branch_two = low_back(jnp.dot(active, w_contract, precision=highest) + bias_contract)
    return (middle + branch_two).reshape(seq_count, length, model_width)

def reference(tokens_in, gain_attn, shift_attn, w_heads, bias_query, bias_value, w_merge, bias_merge, gain_mlp, shift_mlp, w_expand, bias_expand, w_contract, bias_contract, cotangent):
    floats = tuple((member.astype(jnp.float32) for member in (tokens_in, gain_attn, shift_attn, w_heads, bias_query, bias_value, w_merge, bias_merge, gain_mlp, shift_mlp, w_expand, bias_expand, w_contract, bias_contract)))
    result, pull_back = jax.vjp(forward, *floats)
    gradients = pull_back(cotangent.astype(jnp.float32))
    return (result.astype(jnp.bfloat16), gradients[0], gradients[1], gradients[2], gradients[3], gradients[4], gradients[5], gradients[6], gradients[7], gradients[8], gradients[9], gradients[10], gradients[11], gradients[12], gradients[13])
```

```python
import functools
import math

import jax
import jax.numpy as jnp
from jax import lax
from jax.experimental import pallas as pl
from jax.experimental.pallas import tpu as pltpu
from jax.sharding import PartitionSpec as P

HEAD = 64
EPS = 1e-05
LOWEST = -1e30
GELU_A = math.sqrt(2.0 / math.pi)
GELU_B = 0.044715
F32 = jnp.float32
BF16 = jnp.bfloat16
VMEM_BYTES = 52 * 1024 * 1024
GAIN_ATTN, SHIFT_ATTN, BIAS_QUERY, BIAS_VALUE = 0, 1, 2, 3
BIAS_MERGE, GAIN_MLP, SHIFT_MLP, BIAS_CONTRACT = 4, 5, 6, 7
BIAS_EXPAND = 8


def mm(left, right):
    return jnp.dot(left, right, preferred_element_type=F32)


def mm_nt(left, right):
    return lax.dot_general(left, right, (((1,), (1,)), ((), ())), preferred_element_type=F32)


def mm_tn(left, right):
    return lax.dot_general(left, right, (((0,), (0,)), ((), ())), preferred_element_type=F32)


def params(**extra):
    return pltpu.CompilerParams(vmem_limit_bytes=VMEM_BYTES, **extra)


def cost(flops, nbytes, trans=0):
    return pl.CostEstimate(flops=int(flops), bytes_accessed=int(nbytes), transcendentals=int(trans))


def whole(shape):
    return pl.BlockSpec(shape, lambda *_: (0,) * len(shape))


def full_row(at, mine_ref, theirs_ref, row):
    mine = mine_ref[row : row + 1, :].astype(F32)
    theirs = theirs_ref[row : row + 1, :].astype(F32)
    low = jnp.where(at == 0, mine, theirs)
    high = jnp.where(at == 0, theirs, mine)
    return jnp.concatenate([low, high], axis=1)


def normalise(rows):
    mean = jnp.mean(rows, axis=-1, keepdims=True)
    centered = rows - mean
    variance = jnp.mean(centered * centered, axis=-1, keepdims=True)
    inverse = lax.rsqrt(variance + EPS)
    return centered * inverse, inverse


def normalise_back(grad, unit, inverse, gain):
    scaled = grad * gain
    mean = jnp.mean(scaled, axis=-1, keepdims=True)
    along = jnp.mean(scaled * unit, axis=-1, keepdims=True)
    return inverse * (scaled - mean - unit * along)


def piece_starts(at, core, half):
    other = (1 - at) * half
    quarter = half // 2
    return (
        (pl.multiple_of(at * half, quarter), half),
        (pl.multiple_of(other + core * quarter, quarter), quarter),
        (pl.multiple_of(other + (1 - core) * quarter, quarter), quarter),
    )


def front_body(place, x_ref, mine_ref, theirs_ref, *rest):
    weights, (out_ref, h_ref, bias_ref) = rest[:9], rest[9:]
    at, core = place[0], place[1]
    step = pl.program_id(0)
    half = weights[0].shape[0]
    wide = weights[0].shape[1]

    @pl.when(step == 0)
    def _():
        unit, _ = normalise(x_ref[...].astype(F32))
        gain = full_row(at, mine_ref, theirs_ref, GAIN_ATTN)
        shift = full_row(at, mine_ref, theirs_ref, SHIFT_ATTN)
        h_ref[...] = (unit * gain + shift).astype(BF16)
        bias_ref[0:1, :] = full_row(at, mine_ref, theirs_ref, BIAS_QUERY)
        bias_ref[1:2, :] = jnp.zeros_like(bias_ref[1:2, :])
        bias_ref[2:3, :] = full_row(at, mine_ref, theirs_ref, BIAS_VALUE)

    starts = piece_starts(at, core, half)
    pieces = [h_ref[:, pl.ds(begin, size)] for begin, size in starts]
    columns = pl.ds(pl.multiple_of(step * wide, wide), wide)
    for part in range(3):
        total = bias_ref[part : part + 1, columns]
        for index in range(3):
            total = total + mm(pieces[index], weights[part * 3 + index][...])
        turned = total.T.astype(BF16)
        for head in range(wide // HEAD):
            out_ref[head, part] = turned[head * HEAD : (head + 1) * HEAD, :]


def front(place, x, mine, theirs, own, near, far):
    rows, width = x.shape
    heads = width // HEAD
    wide = 256
    steps = width // wide
    specs = []
    for part in range(3):
        for member in (own, near, far):
            specs.append(
                pl.BlockSpec(
                    (member.shape[0], wide), lambda i, _, part=part: (0, part * steps + i)
                )
            )
    return pl.pallas_call(
        front_body,
        grid_spec=pltpu.PrefetchScalarGridSpec(
            num_scalar_prefetch=1,
            grid=(steps,),
            in_specs=[whole(x.shape), whole(mine.shape), whole(theirs.shape)] + specs,
            out_specs=[
                pl.BlockSpec((wide // HEAD, 3, HEAD, rows), lambda i, _: (i, 0, 0, 0)),
                whole((rows, width)),
            ],
            scratch_shapes=[pltpu.VMEM((8, width), F32)],
        ),
        out_shape=[
            jax.ShapeDtypeStruct((heads, 3, HEAD, rows), BF16),
            jax.ShapeDtypeStruct((rows, width), BF16),
        ],
        compiler_params=params(),
        cost_estimate=cost(6 * rows * width * width, 6 * width * width + 10 * rows * width),
        name="front",
    )(place, x, mine, theirs, *([own, near, far] * 3))


def lay_out(source, target, part, per, tokens, sources, block, turned, scale):
    for src in range(sources):
        for pair in range(per):
            piece = source[src, part, :, pair * tokens : (pair + 1) * tokens]
            if scale is not None:
                piece = piece * jnp.asarray(scale, BF16)
            begin = src * tokens
            if turned:
                rows = piece.astype(F32).T.astype(BF16)
                target[pair, begin : begin + tokens, :] = rows
            else:
                inner = begin % block
                target[pair, begin // block, :, inner : inner + tokens] = piece


def attend_body(per, tokens, block, qkv_ref, out_ref, outf_ref, lse_ref, q_ref, k_ref, v_ref):
    sources = qkv_ref.shape[0]
    step = pl.program_id(0)

    @pl.when(step == 0)
    def _():
        lay_out(qkv_ref, q_ref, 0, per, tokens, sources, block, False, HEAD**-0.5)
        lay_out(qkv_ref, k_ref, 1, per, tokens, sources, block, True, None)
        lay_out(qkv_ref, v_ref, 2, per, tokens, sources, block, False, None)

    queries = [q_ref[pair, step] for pair in range(per)]

    def scores(pair, index):
        keys = k_ref[pair, pl.ds(pl.multiple_of(index * block, block), block), :]
        return mm(keys, queries[pair])

    key_at = lax.broadcasted_iota(jnp.int32, (block, block), 0)
    query_at = lax.broadcasted_iota(jnp.int32, (block, block), 1)
    carried = []
    for pair in range(per):
        masked = jnp.where(key_at <= query_at, scores(pair, step), LOWEST)
        top = jnp.max(masked, axis=0, keepdims=True)
        weights = jnp.exp(masked - top)
        total = jnp.sum(weights, axis=0, keepdims=True)
        mixed = mm(v_ref[pair, step], weights.astype(BF16))
        carried += [top, total, mixed]

    def one(index, state):
        fresh = []
        for pair in range(per):
            top, total, mixed = state[3 * pair : 3 * pair + 3]
            here = scores(pair, index)
            new_top = jnp.maximum(top, jnp.max(here, axis=0, keepdims=True))
            weights = jnp.exp(here - new_top)
            factor = jnp.exp(top - new_top)
            total = total * factor + jnp.sum(weights, axis=0, keepdims=True)
            mixed = mixed * factor + mm(v_ref[pair, index], weights.astype(BF16))
            fresh += [new_top, total, mixed]
        return tuple(fresh)

    final = lax.fori_loop(0, step, one, tuple(carried))
    for pair in range(per):
        top, total, mixed = final[3 * pair : 3 * pair + 3]
        mixed = mixed / total
        lse_ref[0, pair : pair + 1, :] = top + jnp.log(total)
        for dst in range(block // tokens):
            piece = mixed[:, dst * tokens : (dst + 1) * tokens]
            lanes = slice(pair * tokens, (pair + 1) * tokens)
            outf_ref[dst, :, lanes] = piece
            out_ref[dst, :, lanes] = piece.astype(BF16)


def attend(qkv, per):
    sources, _, _, lanes = qkv.shape
    tokens = lanes // per
    length = sources * tokens
    block = max(256, tokens)
    steps = length // block
    here = pl.BlockSpec((block // tokens, HEAD, lanes), lambda i: (i, 0, 0))
    return pl.pallas_call(
        functools.partial(attend_body, per, tokens, block),
        grid=(steps,),
        in_specs=[whole(qkv.shape)],
        out_specs=[here, here, pl.BlockSpec((1, 8, block), lambda i: (i, 0, 0))],
        out_shape=[
            jax.ShapeDtypeStruct((sources, HEAD, lanes), BF16),
            jax.ShapeDtypeStruct((sources, HEAD, lanes), F32),
            jax.ShapeDtypeStruct((steps, 8, block), F32),
        ],
        scratch_shapes=[
            pltpu.VMEM((per, steps, HEAD, block), BF16),
            pltpu.VMEM((per, length, HEAD), BF16),
            pltpu.VMEM((per, steps, HEAD, block), BF16),
        ],
        compiler_params=params(),
        cost_estimate=cost(
            8 * per * length * length * HEAD, 16 * qkv.size, per * length * length
        ),
        name="attend",
    )(qkv)


def attend_back_body(
    per, tokens, block, qkv_ref, go_ref, of_ref, lse_ref, out_ref, qt_ref, q_ref, kt_ref, k_ref, v_ref, g_ref,
    dk_ref, dv_ref,
):
    sources = qkv_ref.shape[0]
    step = pl.program_id(0)
    last = pl.num_programs(0) - 1

    @pl.when(step == 0)
    def _():
        lay_out(qkv_ref, qt_ref, 0, per, tokens, sources, block, False, HEAD**-0.5)
        lay_out(qkv_ref, q_ref, 0, per, tokens, sources, block, True, HEAD**-0.5)
        lay_out(qkv_ref, kt_ref, 1, per, tokens, sources, block, False, HEAD**-0.5)
        lay_out(qkv_ref, k_ref, 1, per, tokens, sources, block, True, None)
        lay_out(qkv_ref, v_ref, 2, per, tokens, sources, block, True, None)
        dk_ref[...] = jnp.zeros_like(dk_ref)
        dv_ref[...] = jnp.zeros_like(dv_ref)

    inner = block // tokens
    grads, deltas, lses, turned_grads, turned_queries, queries = [], [], [], [], [], []
    for pair in range(per):
        lanes = slice(pair * tokens, (pair + 1) * tokens)
        grad = jnp.concatenate([go_ref[dst, :, lanes] for dst in range(inner)], axis=1)
        mixed = jnp.concatenate([of_ref[dst, :, lanes] for dst in range(inner)], axis=1)
        wide = grad.astype(F32)
        grads.append(grad)
        deltas.append(jnp.sum(wide * mixed, axis=0, keepdims=True))
        turned_grads.append(wide.T.astype(BF16))
        lses.append(lse_ref[0, pair : pair + 1, :])
        queries.append(qt_ref[pair, step])
        turned_queries.append(q_ref[pair, pl.ds(pl.multiple_of(step * block, block), block), :])

    def one(index, state, diagonal):
        rows = pl.ds(pl.multiple_of(index * block, block), block)
        fresh = []
        for pair in range(per):
            weights = jnp.exp(mm(k_ref[pair, rows, :], queries[pair]) - lses[pair])
            if diagonal:
                key_at = lax.broadcasted_iota(jnp.int32, (block, block), 0)
                query_at = lax.broadcasted_iota(jnp.int32, (block, block), 1)
                weights = jnp.where(key_at <= query_at, weights, 0.0)
            back = mm(v_ref[pair, rows, :], grads[pair])
            dscore = (weights * (back - deltas[pair])).astype(BF16)
            dv_ref[pair, rows, :] += mm(weights.astype(BF16), turned_grads[pair])
            dk_ref[pair, rows, :] += mm(dscore, turned_queries[pair])
            fresh.append(state[pair] + mm(kt_ref[pair, index], dscore))
        return tuple(fresh)

    start = tuple(jnp.zeros((HEAD, block), F32) for _ in range(per))
    state = lax.fori_loop(0, step, lambda i, s: one(i, s, False), start)
    state = one(step, state, True)
    for pair in range(per):
        lanes = slice(pair * tokens, (pair + 1) * tokens)
        for dst in range(inner):
            out_ref[step * inner + dst, 0, :, lanes] = state[pair][
                :, dst * tokens : (dst + 1) * tokens
            ].astype(BF16)

    @pl.when(step == last)
    def _():
        for pair in range(per):
            lanes = slice(pair * tokens, (pair + 1) * tokens)
            for src in range(sources):
                rows = slice(src * tokens, (src + 1) * tokens)
                out_ref[src, 1, :, lanes] = dk_ref[pair, rows, :].T.astype(BF16)
                out_ref[src, 2, :, lanes] = dv_ref[pair, rows, :].T.astype(BF16)


def attend_back(qkv, grad, mixed, lse, per):
    sources, _, _, lanes = qkv.shape
    tokens = lanes // per
    length = sources * tokens
    block = max(256, tokens)
    steps = length // block
    here = pl.BlockSpec((block // tokens, HEAD, lanes), lambda i: (i, 0, 0))
    return pl.pallas_call(
        functools.partial(attend_back_body, per, tokens, block),
        grid=(steps,),
        in_specs=[whole(qkv.shape), here, here, pl.BlockSpec((1, 8, block), lambda i: (i, 0, 0))],
        out_specs=whole(qkv.shape),
        out_shape=jax.ShapeDtypeStruct(qkv.shape, BF16),
        scratch_shapes=[
            pltpu.VMEM((per, steps, HEAD, block), BF16),
            pltpu.VMEM((per, length, HEAD), BF16),
            pltpu.VMEM((per, steps, HEAD, block), BF16),
            pltpu.VMEM((per, length, HEAD), BF16),
            pltpu.VMEM((per, length, HEAD), BF16),
            pltpu.VMEM((8, 128), BF16),
            pltpu.VMEM((per, length, HEAD), F32),
            pltpu.VMEM((per, length, HEAD), F32),
        ],
        compiler_params=params(),
        cost_estimate=cost(
            20 * per * length * length * HEAD, 16 * qkv.size, per * length * length
        ),
        name="attend_back",
    )(qkv, grad, mixed, lse)


def middle_body(
    own_steps, place, x_ref, ot_ref, dy_ref, mine_ref, theirs_ref, mo_ref, mn_ref, mf_ref, eo_ref, en_ref, ef_ref,
    co_ref, cn_ref, cf_ref, out_ref, dx_ref, act_ref, du_ref, h_ref, da_ref, o_ref, dot_ref, sums_ref, be_ref,
    x1_ref, total_ref, dh_ref, bias_ref,
):
    at, core = place[0], place[1]
    step = pl.program_id(0)
    half = mo_ref.shape[0]
    starts = piece_starts(at, core, half)
    wide = act_ref.shape[1]
    near_steps = own_steps // 2
    block = expand_block(step, at, core, own_steps)

    @pl.when(step == 0)
    def _():
        mixed = ot_ref[...].astype(F32).T.astype(BF16)
        o_ref[...] = mixed
        merged = full_row(at, mine_ref, theirs_ref, BIAS_MERGE)
        for (begin, size), weight in zip(starts, (mo_ref, mn_ref, mf_ref)):
            merged = merged + mm(o_ref[:, pl.ds(begin, size)], weight[...])
        x1 = x_ref[...].astype(F32) + merged
        x1_ref[...] = x1
        unit, _ = normalise(x1)
        gain = full_row(at, mine_ref, theirs_ref, GAIN_MLP)
        shift = full_row(at, mine_ref, theirs_ref, SHIFT_MLP)
        h_ref[...] = (unit * gain + shift).astype(BF16)
        total_ref[...] = jnp.zeros_like(total_ref)
        dh_ref[...] = jnp.zeros_like(dh_ref)
        for row in range(own_steps):
            mine = mine_ref[BIAS_EXPAND + row : BIAS_EXPAND + row + 1, :].astype(F32)
            theirs = theirs_ref[BIAS_EXPAND + row : BIAS_EXPAND + row + 1, :].astype(F32)
            bias_ref[row : row + 1, :] = jnp.where(at == 0, mine, theirs)
            bias_ref[own_steps + row : own_steps + row + 1, :] = jnp.where(at == 0, theirs, mine)

    def work(contract):
        inner = bias_ref[pl.ds(block, 1), :]
        for (begin, size), weight in zip(starts, (eo_ref, en_ref, ef_ref)):
            inner = inner + mm(h_ref[:, pl.ds(begin, size)], weight[...])
        square = inner * inner
        bend = jnp.tanh(GELU_A * (inner + GELU_B * (inner * square)))
        active = (0.5 * inner * (1.0 + bend)).astype(BF16)
        slope = 0.5 * (1.0 + bend) + 0.5 * inner * (1.0 - bend * bend) * (
            GELU_A * (1.0 + 3.0 * GELU_B * square)
        )
        act_ref[...] = active
        total_ref[...] += mm(active, contract[...])
        grad = (mm_nt(dy_ref[...], contract[...]) * slope).astype(BF16)
        du_ref[...] = grad
        be_ref[pl.ds(block, 1), :] = jnp.sum(grad.astype(F32), axis=0, keepdims=True)
        for (begin, size), weight in zip(starts, (eo_ref, en_ref, ef_ref)):
            dh_ref[:, pl.ds(begin, size)] += mm_nt(grad, weight[...])

    @pl.when(step < own_steps)
    def _():
        work(co_ref)

    @pl.when(jnp.logical_and(step >= own_steps, step < own_steps + near_steps))
    def _():
        work(cn_ref)

    @pl.when(step >= own_steps + near_steps)
    def _():
        work(cf_ref)

    @pl.when(step == pl.num_programs(0) - 1)
    def _():
        x1 = x1_ref[...]
        bias = full_row(at, mine_ref, theirs_ref, BIAS_CONTRACT)
        out_ref[...] = (x1 + total_ref[...] + bias).astype(BF16)
        gain = full_row(at, mine_ref, theirs_ref, GAIN_MLP)
        unit, inverse = normalise(x1)
        grad = dh_ref[...]
        dy = dy_ref[...].astype(F32)
        dx = dy + normalise_back(grad, unit, inverse, gain)
        dx_ref[...] = dx
        da = dx.astype(BF16)
        da_ref[...] = da
        sums_ref[0:1, :] = jnp.sum(dy, axis=0, keepdims=True)
        sums_ref[1:2, :] = jnp.sum(grad * unit, axis=0, keepdims=True)
        sums_ref[2:3, :] = jnp.sum(grad, axis=0, keepdims=True)
        sums_ref[3:4, :] = jnp.sum(da.astype(F32), axis=0, keepdims=True)
        sums_ref[4:8, :] = jnp.zeros_like(sums_ref[4:8, :])
        for (begin, size), weight in zip(starts, (mo_ref, mn_ref, mf_ref)):
            dot_ref[pl.ds(begin, size), :] = mm_nt(weight[...], da).astype(BF16)


def expand_block(step, at, core, own_steps):
    near_steps = own_steps // 2
    other = (1 - at) * own_steps
    return jnp.where(
        step < own_steps,
        at * own_steps + step,
        jnp.where(
            step < own_steps + near_steps,
            other + core * near_steps + step - own_steps,
            other + (1 - core) * near_steps + step - own_steps - near_steps,
        ),
    )


def middle(place, x, ot, dy, mine, theirs, merge, expand, contract):
    rows, width = x.shape
    hidden = expand[0].shape[1]
    wide = 512
    own_steps = contract[0].shape[0] // wide
    near_steps = own_steps // 2
    steps = 2 * own_steps

    def column(i, place):
        return (0, expand_block(i, place[0], place[1], own_steps))

    def held(first, count):
        return lambda i, _: (jnp.clip(i - first, 0, count - 1), 0)

    in_specs = [whole(x.shape), whole(ot.shape), whole(dy.shape), whole(mine.shape), whole(theirs.shape)]
    in_specs += [whole(member.shape) for member in merge]
    in_specs += [pl.BlockSpec((member.shape[0], wide), column) for member in expand]
    in_specs += [
        pl.BlockSpec((wide, width), held(0, own_steps)),
        pl.BlockSpec((wide, width), held(own_steps, near_steps)),
        pl.BlockSpec((wide, width), held(own_steps + near_steps, near_steps)),
    ]
    shapes = [
        ((rows, width), BF16, None),
        ((rows, width), F32, None),
        ((rows, hidden), BF16, wide),
        ((rows, hidden), BF16, wide),
        ((rows, width), BF16, None),
        ((rows, width), BF16, None),
        ((rows, width), BF16, None),
        ((width, rows), BF16, None),
        ((8, width), F32, None),
        ((steps, wide), F32, None),
    ]
    return pl.pallas_call(
        functools.partial(middle_body, own_steps),
        grid_spec=pltpu.PrefetchScalarGridSpec(
            num_scalar_prefetch=1,
            grid=(steps,),
            in_specs=in_specs,
            out_specs=[
                whole(shape) if block is None else pl.BlockSpec((rows, block), column)
                for shape, _, block in shapes
            ],
            scratch_shapes=[
                pltpu.VMEM((rows, width), F32),
                pltpu.VMEM((rows, width), F32),
                pltpu.VMEM((rows, width), F32),
                pltpu.VMEM((steps, wide), F32),
            ],
        ),
        out_shape=[jax.ShapeDtypeStruct(shape, dtype) for shape, dtype, _ in shapes],
        compiler_params=params(),
        cost_estimate=cost(
            8 * rows * width * hidden + 4 * rows * width * width,
            4 * width * hidden + 2 * width * width + 30 * rows * width,
            rows * hidden,
        ),
        name="middle",
    )(place, x, ot, dy, mine, theirs, *merge, *expand, *contract)


def gram_body(aq, ax, ac, bq, bx, bc, out_ref):
    total = mm_tn(aq[...], bq[...])
    total = total + mm_tn(ax[...], bx[...])
    total = total + mm_tn(ac[0], bc[0])
    total = total + mm_tn(ac[1], bc[1])
    out_ref[0] = total.astype(BF16)


def gram(place, left, right, name):
    (aq, ax, ac), (bq, bx, bc) = left, right
    rows, columns = bq.shape
    quarter = ac.shape[2]
    high = min(quarter, 512)
    wide = 1024
    per = quarter // high
    return pl.pallas_call(
        lambda place, *refs: gram_body(*refs),
        grid_spec=pltpu.PrefetchScalarGridSpec(
            num_scalar_prefetch=1,
            grid=(columns // wide, per),
            in_specs=[
                pl.BlockSpec((rows, high), lambda j, i, s: (0, (s[0] * 2 + s[1]) * per + i)),
                pl.BlockSpec((rows, high), lambda j, i, s: (0, s[1] * per + i)),
                pl.BlockSpec((2, rows, high), lambda j, i, s: (0, 0, i)),
                pl.BlockSpec((rows, wide), lambda j, i, s: (0, j)),
                pl.BlockSpec((rows, wide), lambda j, i, s: (0, j)),
                pl.BlockSpec((2, rows, wide), lambda j, i, s: (0, 0, j)),
            ],
            out_specs=pl.BlockSpec((1, high, wide), lambda j, i, s: (j, i, 0)),
        ),
        out_shape=jax.ShapeDtypeStruct((columns // wide, quarter, wide), BF16),
        compiler_params=params(),
        cost_estimate=cost(
            8 * rows * quarter * columns, 8 * rows * (quarter + columns) + 2 * quarter * columns
        ),
        name=name,
    )(place, aq, ax, ac, bq, bx, bc)


def heads_body(dp_ref, h_ref, out_ref):
    @pl.when(pl.program_id(0) == 0)
    def _():
        out_ref[...] = jnp.zeros_like(out_ref)

    _, parts, head, lanes = dp_ref.shape
    out_ref[...] += mm(dp_ref[0].reshape(parts * head, lanes), h_ref[0])


def heads_gradient(dp, normed):
    sources, parts, head, lanes = dp.shape
    width = normed.shape[2]
    return pl.pallas_call(
        heads_body,
        grid=(sources,),
        in_specs=[
            pl.BlockSpec((1, parts, head, lanes), lambda i: (i, 0, 0, 0)),
            pl.BlockSpec((1, lanes, width), lambda i: (i, 0, 0)),
        ],
        out_specs=whole((parts * head, width)),
        out_shape=jax.ShapeDtypeStruct((parts * head, width), F32),
        compiler_params=params(),
        cost_estimate=cost(
            2 * sources * parts * head * lanes * width, 2 * sources * lanes * (width + parts * head)
        ),
        name="heads_gradient",
    )(dp, normed)


def spread_body(in_ref, out_ref):
    heads, _, head, half = in_ref.shape
    out_ref[...] = in_ref[...].reshape(heads * head, half).astype(F32).T


def spread_heads(gathered):
    heads, parts, head, half = gathered.shape
    some = 4
    steps = heads // some
    return pl.pallas_call(
        spread_body,
        grid=(parts, steps),
        in_specs=[pl.BlockSpec((some, 1, head, half), lambda t, i: (i, t, 0, 0))],
        out_specs=pl.BlockSpec((half, some * head), lambda t, i: (0, t * steps + i)),
        out_shape=jax.ShapeDtypeStruct((half, parts * heads * head), F32),
        compiler_params=params(),
        cost_estimate=cost(0, 6 * gathered.size),
        name="spread_heads",
    )(gathered)


def back_body(place, dp_ref, x_ref, dx_ref, mine_ref, theirs_ref, wo_ref, wn_ref, wf_ref, out_ref, sums_ref, dh_ref):
    at, core = place[0], place[1]
    part = pl.program_id(0)
    starts = piece_starts(at, core, wo_ref.shape[0])
    heads, _, head, rows = dp_ref.shape
    grad = dp_ref[...].reshape(heads * head, rows)

    @pl.when(part == 0)
    def _():
        dh_ref[...] = jnp.zeros_like(dh_ref)
        sums_ref[...] = jnp.zeros_like(sums_ref)

    for (begin, size), weight in zip(starts, (wo_ref, wn_ref, wf_ref)):
        dh_ref[pl.ds(begin, size), :] += mm(weight[...], grad)
    total = mm_nt(jnp.ones((8, rows), BF16), grad)

    @pl.when(part == 0)
    def _():
        sums_ref[2:3, :] = total[0:1, :]

    @pl.when(part == 2)
    def _():
        sums_ref[3:4, :] = total[0:1, :]
        dh = dh_ref[...].T
        unit, inverse = normalise(x_ref[...].astype(F32))
        gain = full_row(at, mine_ref, theirs_ref, GAIN_ATTN)
        out_ref[...] = dx_ref[...] + normalise_back(dh, unit, inverse, gain)
        sums_ref[0:1, :] = jnp.sum(dh * unit, axis=0, keepdims=True)
        sums_ref[1:2, :] = jnp.sum(dh, axis=0, keepdims=True)


def back(place, dp, x, dx, mine, theirs, weights):
    rows, width = x.shape
    heads, parts, head, _ = dp.shape
    return pl.pallas_call(
        back_body,
        grid_spec=pltpu.PrefetchScalarGridSpec(
            num_scalar_prefetch=1,
            grid=(parts,),
            in_specs=[
                pl.BlockSpec((heads, 1, head, rows), lambda t, _: (0, t, 0, 0)),
                whole(x.shape),
                whole(dx.shape),
                whole(mine.shape),
                whole(theirs.shape),
            ]
            + [pl.BlockSpec((member.shape[0], width), lambda t, _: (0, t)) for member in weights],
            out_specs=[whole((rows, width)), whole((8, width))],
            scratch_shapes=[pltpu.VMEM((width, rows), F32)],
        ),
        out_shape=[
            jax.ShapeDtypeStruct((rows, width), F32),
            jax.ShapeDtypeStruct((8, width), F32),
        ],
        compiler_params=params(),
        cost_estimate=cost(6 * rows * width * width, 6 * width * width + 14 * rows * width),
        name="back",
    )(place, dp, x, dx, mine, theirs, *weights)


def after(value, *others):
    return lax.optimization_barrier((value,) + others)[0]


def per_device(
    nctx, tokens_in, gain_attn, shift_attn, w_heads, bias_query, bias_value, w_merge, bias_merge, gain_mlp, shift_mlp,
    w_expand, bias_expand, w_contract, bias_contract, cotangent,
):
    seqs, tokens, width = tokens_in.shape
    rows = seqs * tokens
    half = width // 2
    heads = width // HEAD
    hidden = w_expand.shape[1]
    pairs = seqs * heads
    same = max(1, nctx // pairs)
    per = max(1, pairs // nctx)
    groups = seqs // per
    ctx = lax.axis_index("ctx")
    at = lax.axis_index("fsdp")
    core = ctx % 2
    place = jnp.stack([at, core]).astype(jnp.int32)
    chips = [[2 * chip + one for chip in range(nctx // 2)] for one in range(2)]

    def over_x(value):
        return lax.ppermute(value, "fsdp", [(0, 1), (1, 0)])

    def over_core(value):
        return lax.ppermute(value, "ctx", [(i, i ^ 1) for i in range(nctx)])

    def exchange(value):
        return lax.all_to_all(value, "ctx", 0, 0)

    def gather_weight(weight, *first):
        quarter = weight.shape[0] // 2
        mine = lax.dynamic_slice_in_dim(weight, core * quarter, quarter, 0)
        near = over_x(after(mine, *first))
        return weight, near, over_core(near)

    mine = jnp.concatenate(
        [
            member.reshape(-1, half)
            for member in (
                gain_attn, shift_attn, bias_query, bias_value, bias_merge, gain_mlp, shift_mlp, bias_contract,
                bias_expand, jnp.zeros(((-8 - bias_expand.shape[0] // half) % 16 * half,), BF16),
            )
        ]
    )
    theirs = over_x(mine)
    heads_w = gather_weight(w_heads)
    merge_w = gather_weight(w_merge, heads_w[1])
    expand_w = gather_weight(w_expand, heads_w[1])

    x = tokens_in.reshape(rows, width)
    dy = cotangent.reshape(rows, width)

    def to_send(value):
        lead = value.shape[1:-1]
        value = value.reshape((heads,) + lead + (groups, per * tokens))
        value = jnp.moveaxis(value, -2, 1).reshape((nctx // same,) + lead + (per * tokens,))
        return value if same == 1 else jnp.repeat(value, same, axis=0)

    def received(value):
        value = value[::same]
        lead = value.shape[1:-1]
        value = value.reshape((heads, groups) + lead + (per * tokens,))
        return jnp.moveaxis(value, 1, -2).reshape((heads,) + lead + (rows,))

    projected, normed = front(place, x, mine, theirs, *heads_w)
    normed_all = lax.all_gather(normed, "ctx", axis=0, tiled=False)
    qkv = exchange(to_send(projected))
    contract_w = gather_weight(w_contract, expand_w[1], qkv)
    mixed_b, mixed_f, lse = attend(qkv, per)
    mixed = received(exchange(mixed_b)).reshape(width, rows)
    block_out, dx1, active, du, normed_two, da, mixed_rows, grad_mixed, sums_mlp, sums_expand = middle(
        place, x, mixed, dy, mine, theirs, merge_w, expand_w, contract_w
    )

    def columns_of_four(value, first=()):
        two = value.shape[1] // 2
        one = two // 2
        there = over_x(after(lax.dynamic_slice_in_dim(value, (1 - at) * two, two, 1), *first))
        sent = jnp.stack(
            [
                lax.dynamic_slice_in_dim(value, at * two + (1 - core) * one, one, 1),
                lax.dynamic_slice_in_dim(there, (1 - core) * one, one, 1),
            ]
        )
        return value, there, over_core(sent)

    def tokens_of_four(value, *first):
        there = over_x(after(value, *first))
        return value, there, over_core(jnp.stack([value, there]))

    dy_four = tokens_of_four(dy, contract_w[1])
    grad_contract = gram(place, columns_of_four(active), dy_four, "grad_contract")
    grad_expand = gram(place, columns_of_four(normed_two), tokens_of_four(du), "grad_expand")
    grad_merge = gram(place, columns_of_four(mixed_rows), tokens_of_four(da), "grad_merge")

    grad_out = exchange(to_send(grad_mixed.reshape(heads, HEAD, rows)))
    dqkv = attend_back(qkv, grad_out, mixed_f, lse, per)
    dp = received(exchange(dqkv))

    def summed(value):
        part = lax.psum_scatter(
            value, "ctx", scatter_dimension=1, tiled=True, axis_index_groups=chips
        )
        whole_of = lax.all_gather(part, "ctx", axis=0, tiled=False)
        whole_of = whole_of.reshape((nctx // 2, 2) + part.shape)
        return jnp.transpose(whole_of, (1, 0, 3, 2, 4)).astype(F32)

    contract_sum = summed(grad_contract).reshape(w_contract.shape)
    others = summed(jnp.concatenate([grad_expand, grad_merge]))
    expand_sum = others[:, :, :, : hidden // width].reshape(w_expand.shape)
    merge_sum = others[:, :, :, hidden // width :].reshape(w_merge.shape)

    if groups > 1:
        normed_here = lax.dynamic_slice_in_dim(normed_all, (ctx // same % groups) * tokens * per, tokens * per, 1)
    else:
        normed_here = normed_all
    grad_heads = heads_gradient(dqkv, normed_here)
    if groups > 1:
        members = [
            [first + one + same * group for group in range(groups)]
            for first in range(0, nctx, groups * same)
            for one in range(same)
        ]
        grad_heads = lax.psum(grad_heads, "ctx", axis_index_groups=members)
    kept = lax.dynamic_slice_in_dim(grad_heads, at * half, half, 1)
    sent = lax.dynamic_slice_in_dim(grad_heads, (1 - at) * half, half, 1)
    kept = (kept + over_x(sent.astype(BF16)).astype(F32)).astype(BF16)
    spread = lax.all_gather(kept, "ctx", axis=0, tiled=False)[:: groups * same]
    heads_sum = spread_heads(spread.reshape(heads, 3, HEAD, half))

    grad_tokens, sums_attn = back(place, dp, x, dx1, mine, theirs, heads_w)

    vectors = jnp.concatenate(
        [
            jnp.concatenate([sums_mlp[:4], sums_attn[:4]]).reshape(8, 2, half),
            sums_expand.reshape(2, -1, half).swapaxes(0, 1),
        ]
    ).swapaxes(0, 1)
    mine_v = lax.dynamic_index_in_dim(vectors, at, 0, keepdims=False)
    vector = mine_v + over_x(lax.dynamic_index_in_dim(vectors, 1 - at, 0, keepdims=False))
    vector = jnp.sum(exchange(jnp.broadcast_to(vector, (nctx,) + vector.shape)), axis=0)
    return (
        block_out.reshape(tokens_in.shape),
        grad_tokens.reshape(tokens_in.shape),
        vector[4],
        vector[5],
        heads_sum,
        vector[6],
        vector[7],
        merge_sum,
        vector[3],
        vector[1],
        vector[2],
        expand_sum,
        vector[8:].reshape(-1),
        contract_sum,
        vector[0],
    )


def solution(mesh):
    rows, vec, mat = P("fsdp", "ctx", None), P("fsdp"), P("fsdp", None)
    return jax.shard_map(
        functools.partial(per_device, mesh.shape["ctx"]),
        mesh=mesh,
        in_specs=(rows, vec, vec, mat, vec, vec, mat, vec, vec, vec, mat, vec, mat, vec, rows),
        out_specs=(rows, rows, vec, vec, mat, vec, vec, mat, vec, vec, vec, mat, vec, mat, vec),
        check_vma=False,
    )
```

```python
import functools
import math

import jax
import jax.numpy as jnp
from jax import lax
from jax.experimental import pallas as pl
from jax.experimental.pallas import tpu as pltpu
from jax.sharding import PartitionSpec as P

HEAD = 64
EPS = 1e-05
LOWEST = -1e30
GELU_A = math.sqrt(2.0 / math.pi)
GELU_B = 0.044715
F32 = jnp.float32
BF16 = jnp.bfloat16
VMEM_BYTES = 52 * 1024 * 1024
GAIN_ATTN, SHIFT_ATTN, BIAS_QUERY, BIAS_VALUE = 0, 1, 2, 3
BIAS_MERGE, GAIN_MLP, SHIFT_MLP, BIAS_CONTRACT = 4, 5, 6, 7
BIAS_EXPAND = 8


def mm(left, right):
    return jnp.dot(left, right, preferred_element_type=F32)


def mm_nt(left, right):
    return lax.dot_general(left, right, (((1,), (1,)), ((), ())), preferred_element_type=F32)


def mm_tn(left, right):
    return lax.dot_general(left, right, (((0,), (0,)), ((), ())), preferred_element_type=F32)


def params(**extra):
    return pltpu.CompilerParams(vmem_limit_bytes=VMEM_BYTES, **extra)


def about(us):
    return pl.CostEstimate(flops=int(us * 1.15e9), bytes_accessed=0, transcendentals=0)


def whole(shape):
    return pl.BlockSpec(shape, lambda *_: (0,) * len(shape))


def full_row(at, mine_ref, theirs_ref, row):
    mine = mine_ref[row : row + 1, :].astype(F32)
    theirs = theirs_ref[row : row + 1, :].astype(F32)
    low = jnp.where(at == 0, mine, theirs)
    high = jnp.where(at == 0, theirs, mine)
    return jnp.concatenate([low, high], axis=1)


def normalise(rows):
    mean = jnp.mean(rows, axis=-1, keepdims=True)
    centered = rows - mean
    variance = jnp.mean(centered * centered, axis=-1, keepdims=True)
    inverse = lax.rsqrt(variance + EPS)
    return centered * inverse, inverse


def normalise_back(grad, unit, inverse, gain):
    scaled = grad * gain
    mean = jnp.mean(scaled, axis=-1, keepdims=True)
    along = jnp.mean(scaled * unit, axis=-1, keepdims=True)
    return inverse * (scaled - mean - unit * along)


def piece_starts(at, core, half):
    other = (1 - at) * half
    quarter = half // 2
    return (
        (pl.multiple_of(at * half, quarter), half),
        (pl.multiple_of(other + core * quarter, quarter), quarter),
        (pl.multiple_of(other + (1 - core) * quarter, quarter), quarter),
    )


def project(at, core, normed, bias, own, near, far, out_ref, part):
    total = bias
    for (begin, size), weight in zip(piece_starts(at, core, own.shape[0]), (own, near, far)):
        total = total + mm(normed[:, pl.ds(begin, size)], weight[...])
    turned = total.T.astype(BF16)
    for head in range(turned.shape[0] // HEAD):
        piece = turned[head * HEAD : (head + 1) * HEAD, :]
        if part is None:
            out_ref[head] = piece
        else:
            out_ref[head, part] = piece


def front_query_body(place, x_ref, mine_ref, theirs_ref, own, near, far, out_ref, h_ref, bias_ref):
    at, core = place[0], place[1]
    step = pl.program_id(0)
    wide = own.shape[1]

    @pl.when(step == 0)
    def _():
        unit, _ = normalise(x_ref[...].astype(F32))
        gain = full_row(at, mine_ref, theirs_ref, GAIN_ATTN)
        shift = full_row(at, mine_ref, theirs_ref, SHIFT_ATTN)
        h_ref[...] = (unit * gain + shift).astype(BF16)
        bias_ref[0:1, :] = full_row(at, mine_ref, theirs_ref, BIAS_QUERY)

    columns = pl.ds(pl.multiple_of(step * wide, wide), wide)
    project(at, core, h_ref, bias_ref[0:1, columns], own, near, far, out_ref, None)


def front_query(place, x, mine, theirs, own, near, far):
    rows, width = x.shape
    heads = width // HEAD
    wide = 256
    return pl.pallas_call(
        front_query_body,
        grid_spec=pltpu.PrefetchScalarGridSpec(
            num_scalar_prefetch=1,
            grid=(width // wide,),
            in_specs=[whole(x.shape), whole(mine.shape), whole(theirs.shape)]
            + [pl.BlockSpec((member.shape[0], wide), lambda i, _: (0, i)) for member in (own, near, far)],
            out_specs=[
                pl.BlockSpec((wide // HEAD, HEAD, rows), lambda i, _: (i, 0, 0)),
                whole((rows, width)),
            ],
            scratch_shapes=[pltpu.VMEM((8, width), F32)],
        ),
        out_shape=[
            jax.ShapeDtypeStruct((heads, HEAD, rows), BF16),
            jax.ShapeDtypeStruct((rows, width), BF16),
        ],
        compiler_params=params(),
        cost_estimate=about(4),
        name="front_query",
    )(place, x, mine, theirs, own, near, far)


def front_rest_body(place, h_ref, mine_ref, theirs_ref, *rest):
    weights, (out_ref, bias_ref) = rest[:6], rest[6:]
    at, core = place[0], place[1]
    step = pl.program_id(0)
    wide = weights[0].shape[1]

    @pl.when(step == 0)
    def _():
        bias_ref[0:1, :] = jnp.zeros_like(bias_ref[0:1, :])
        bias_ref[1:2, :] = full_row(at, mine_ref, theirs_ref, BIAS_VALUE)

    columns = pl.ds(pl.multiple_of(step * wide, wide), wide)
    for part in range(2):
        bias = bias_ref[part : part + 1, columns]
        project(at, core, h_ref, bias, *weights[3 * part : 3 * part + 3], out_ref, part)


def front_rest(place, normed, mine, theirs, own, near, far):
    rows, width = normed.shape
    heads = width // HEAD
    wide = 256
    steps = width // wide
    specs = []
    for part in range(2):
        for member, skip in ((own, 1), (near, 0), (far, 0)):
            first = (part + skip) * steps
            specs.append(pl.BlockSpec((member.shape[0], wide), lambda i, _, first=first: (0, first + i)))
    return pl.pallas_call(
        front_rest_body,
        grid_spec=pltpu.PrefetchScalarGridSpec(
            num_scalar_prefetch=1,
            grid=(steps,),
            in_specs=[whole(normed.shape), whole(mine.shape), whole(theirs.shape)] + specs,
            out_specs=pl.BlockSpec((wide // HEAD, 2, HEAD, rows), lambda i, _: (i, 0, 0, 0)),
            scratch_shapes=[pltpu.VMEM((8, width), F32)],
        ),
        out_shape=jax.ShapeDtypeStruct((heads, 2, HEAD, rows), BF16),
        compiler_params=params(),
        cost_estimate=about(5),
        name="front_rest",
    )(place, normed, mine, theirs, *([own, near, far] * 2))


def lay_out(source, target, per, tokens, block, turned=False, scale=None):
    for src in range(source.shape[0]):
        for pair in range(per):
            piece = source[src, :, pair * tokens : (pair + 1) * tokens]
            if scale is not None:
                piece = piece * jnp.asarray(scale, BF16)
            begin = src * tokens
            if turned:
                target[pair, begin : begin + tokens, :] = piece.astype(F32).T.astype(BF16)
            else:
                inner = begin % block
                target[pair, begin // block, :, inner : inner + tokens] = piece


def allowed_at(first_key, first_query, keys, queries):
    key_at = first_key + lax.broadcasted_iota(jnp.int32, (keys, queries), 0)
    query_at = first_query + lax.broadcasted_iota(jnp.int32, (keys, queries), 1)
    return key_at <= query_at


def attend_body(per, tokens, block, chunk, query_ref, kv_ref, out_ref, outf_ref, lse_ref, q_ref, k_ref, v_ref):
    step = pl.program_id(0)

    @pl.when(step == 0)
    def _():
        lay_out(query_ref, q_ref, per, tokens, block, scale=HEAD**-0.5)
        lay_out(kv_ref.at[:, 0], k_ref, per, tokens, chunk, turned=True)
        lay_out(kv_ref.at[:, 1], v_ref, per, tokens, chunk)

    queries = [q_ref[pair, step] for pair in range(per)]

    def scores(pair, index):
        keys = k_ref[pair, pl.ds(pl.multiple_of(index * chunk, chunk), chunk), :]
        return mm(keys, queries[pair])

    last = (step * block) // chunk
    allowed = allowed_at(last * chunk, step * block, chunk, block)
    carried = []
    for pair in range(per):
        masked = jnp.where(allowed, scores(pair, last), LOWEST)
        top = jnp.max(masked, axis=0, keepdims=True)
        weights = jnp.exp(masked - top)
        total = jnp.sum(weights, axis=0, keepdims=True)
        mixed = mm(v_ref[pair, last], weights.astype(BF16))
        carried += [top, total, mixed]

    def one(index, state):
        fresh = []
        for pair in range(per):
            top, total, mixed = state[3 * pair : 3 * pair + 3]
            here = scores(pair, index)
            new_top = jnp.maximum(top, jnp.max(here, axis=0, keepdims=True))
            weights = jnp.exp(here - new_top)
            factor = jnp.exp(top - new_top)
            total = total * factor + jnp.sum(weights, axis=0, keepdims=True)
            mixed = mixed * factor + mm(v_ref[pair, index], weights.astype(BF16))
            fresh += [new_top, total, mixed]
        return tuple(fresh)

    final = lax.fori_loop(0, last, one, tuple(carried))
    for pair in range(per):
        top, total, mixed = final[3 * pair : 3 * pair + 3]
        mixed = mixed / total
        lse_ref[0, pair : pair + 1, :] = top + jnp.log(total)
        for dst in range(block // tokens):
            piece = mixed[:, dst * tokens : (dst + 1) * tokens]
            lanes = slice(pair * tokens, (pair + 1) * tokens)
            outf_ref[dst, :, lanes] = piece
            out_ref[dst, :, lanes] = piece.astype(BF16)


def attend(query, kv, per, block=512, chunk=512):
    sources, _, lanes = query.shape
    tokens = lanes // per
    length = sources * tokens
    steps = length // block
    here = pl.BlockSpec((block // tokens, HEAD, lanes), lambda i: (i, 0, 0))
    return pl.pallas_call(
        functools.partial(attend_body, per, tokens, block, chunk),
        grid=(steps,),
        in_specs=[whole(query.shape), whole(kv.shape)],
        out_specs=[here, here, pl.BlockSpec((1, 8, block), lambda i: (i, 0, 0))],
        out_shape=[
            jax.ShapeDtypeStruct((sources, HEAD, lanes), BF16),
            jax.ShapeDtypeStruct((sources, HEAD, lanes), F32),
            jax.ShapeDtypeStruct((steps, 8, block), F32),
        ],
        scratch_shapes=[
            pltpu.VMEM((per, steps, HEAD, block), BF16),
            pltpu.VMEM((per, length, HEAD), BF16),
            pltpu.VMEM((per, length // chunk, HEAD, chunk), BF16),
        ],
        compiler_params=params(),
        cost_estimate=about(20),
        name="attend",
    )(query, kv)


def attend_back_body(
    per, tokens, block, chunk, query_ref, kv_ref, go_ref, of_ref, lse_ref, out_ref, qt_ref, q_ref, kt_ref, k_ref, v_ref,
    dk_ref, dv_ref,
):
    sources = query_ref.shape[0]
    step = pl.program_id(0)

    @pl.when(step == 0)
    def _():
        lay_out(query_ref, qt_ref, per, tokens, block, scale=HEAD**-0.5)
        lay_out(query_ref, q_ref, per, tokens, block, turned=True, scale=HEAD**-0.5)
        lay_out(kv_ref.at[:, 0], kt_ref, per, tokens, chunk, scale=HEAD**-0.5)
        lay_out(kv_ref.at[:, 0], k_ref, per, tokens, chunk, turned=True)
        lay_out(kv_ref.at[:, 1], v_ref, per, tokens, chunk, turned=True)
        dk_ref[...] = jnp.zeros_like(dk_ref)
        dv_ref[...] = jnp.zeros_like(dv_ref)

    inner = block // tokens
    grads, deltas, lses, turned_grads, turned_queries, queries = [], [], [], [], [], []
    for pair in range(per):
        lanes = slice(pair * tokens, (pair + 1) * tokens)
        grad = jnp.concatenate([go_ref[dst, :, lanes] for dst in range(inner)], axis=1)
        mixed = jnp.concatenate([of_ref[dst, :, lanes] for dst in range(inner)], axis=1)
        wide = grad.astype(F32)
        grads.append(grad)
        deltas.append(jnp.sum(wide * mixed, axis=0, keepdims=True))
        turned_grads.append(wide.T.astype(BF16))
        lses.append(lse_ref[0, pair : pair + 1, :])
        queries.append(qt_ref[pair, step])
        turned_queries.append(q_ref[pair, pl.ds(pl.multiple_of(step * block, block), block), :])

    def one(index, state, allowed):
        rows = pl.ds(pl.multiple_of(index * chunk, chunk), chunk)
        fresh = []
        for pair in range(per):
            weights = jnp.exp(mm(k_ref[pair, rows, :], queries[pair]) - lses[pair])
            if allowed is not None:
                weights = jnp.where(allowed, weights, 0.0)
            back = mm(v_ref[pair, rows, :], grads[pair])
            dscore = (weights * (back - deltas[pair])).astype(BF16)
            dv_ref[pair, rows, :] += mm(weights.astype(BF16), turned_grads[pair])
            dk_ref[pair, rows, :] += mm(dscore, turned_queries[pair])
            fresh.append(state[pair] + mm(kt_ref[pair, index], dscore))
        return tuple(fresh)

    last = (step * block) // chunk
    start = tuple(jnp.zeros((HEAD, block), F32) for _ in range(per))
    state = lax.fori_loop(0, last, lambda i, s: one(i, s, None), start)
    state = one(last, state, allowed_at(last * chunk, step * block, chunk, block))
    for pair in range(per):
        lanes = slice(pair * tokens, (pair + 1) * tokens)
        for dst in range(inner):
            out_ref[step * inner + dst, 0, :, lanes] = state[pair][
                :, dst * tokens : (dst + 1) * tokens
            ].astype(BF16)

    @pl.when(step == pl.num_programs(0) - 1)
    def _():
        for pair in range(per):
            lanes = slice(pair * tokens, (pair + 1) * tokens)
            for src in range(sources):
                rows = slice(src * tokens, (src + 1) * tokens)
                out_ref[src, 1, :, lanes] = dk_ref[pair, rows, :].T.astype(BF16)
                out_ref[src, 2, :, lanes] = dv_ref[pair, rows, :].T.astype(BF16)


def attend_back(query, kv, grad, mixed, lse, per, chunk=512):
    sources, _, lanes = query.shape
    tokens = lanes // per
    length = sources * tokens
    steps, _, block = lse.shape
    here = pl.BlockSpec((block // tokens, HEAD, lanes), lambda i: (i, 0, 0))
    shape = (sources, 3, HEAD, lanes)
    return pl.pallas_call(
        functools.partial(attend_back_body, per, tokens, block, chunk),
        grid=(steps,),
        in_specs=[
            whole(query.shape), whole(kv.shape), here, here, pl.BlockSpec((1, 8, block), lambda i: (i, 0, 0)),
        ],
        out_specs=whole(shape),
        out_shape=jax.ShapeDtypeStruct(shape, BF16),
        scratch_shapes=[
            pltpu.VMEM((per, steps, HEAD, block), BF16),
            pltpu.VMEM((per, length, HEAD), BF16),
            pltpu.VMEM((per, length // chunk, HEAD, chunk), BF16),
            pltpu.VMEM((per, length, HEAD), BF16),
            pltpu.VMEM((per, length, HEAD), BF16),
            pltpu.VMEM((per, length, HEAD), F32),
            pltpu.VMEM((per, length, HEAD), F32),
        ],
        compiler_params=params(),
        cost_estimate=about(25),
        name="attend_back",
    )(query, kv, grad, mixed, lse)


def merge_body(place, x_ref, ot_ref, mine_ref, theirs_ref, mo_ref, mn_ref, mf_ref, x1_ref, h_ref, o_ref):
    at, core = place[0], place[1]
    starts = piece_starts(at, core, mo_ref.shape[0])
    o_ref[...] = ot_ref[...].astype(F32).T.astype(BF16)
    merged = full_row(at, mine_ref, theirs_ref, BIAS_MERGE)
    for (begin, size), weight in zip(starts, (mo_ref, mn_ref, mf_ref)):
        merged = merged + mm(o_ref[:, pl.ds(begin, size)], weight[...])
    x1 = x_ref[...].astype(F32) + merged
    x1_ref[...] = x1
    unit, _ = normalise(x1)
    gain = full_row(at, mine_ref, theirs_ref, GAIN_MLP)
    shift = full_row(at, mine_ref, theirs_ref, SHIFT_MLP)
    h_ref[...] = (unit * gain + shift).astype(BF16)


def merge(place, x, ot, mine, theirs, weights):
    shape = x.shape
    operands = (x, ot, mine, theirs, *weights)
    return pl.pallas_call(
        merge_body,
        grid_spec=pltpu.PrefetchScalarGridSpec(
            num_scalar_prefetch=1,
            grid=(1,),
            in_specs=[whole(member.shape) for member in operands],
            out_specs=[whole(shape)] * 3,
        ),
        out_shape=[
            jax.ShapeDtypeStruct(shape, F32),
            jax.ShapeDtypeStruct(shape, BF16),
            jax.ShapeDtypeStruct(shape, BF16),
        ],
        compiler_params=params(),
        cost_estimate=about(5),
        name="merge",
    )(place, *operands)


def gelu_pair(inner):
    square = inner * inner
    bend = jnp.tanh(GELU_A * (inner + GELU_B * (inner * square)))
    active = 0.5 * inner * (1.0 + bend)
    slope = 0.5 * (1.0 + bend) + 0.5 * inner * (1.0 - bend * bend) * (GELU_A * (1.0 + 3.0 * GELU_B * square))
    return active, slope


def read_expand_bias(at, mine_ref, theirs_ref, bias_ref):
    count = bias_ref.shape[0] // 2
    for row in range(count):
        mine = mine_ref[BIAS_EXPAND + row : BIAS_EXPAND + row + 1, :].astype(F32)
        theirs = theirs_ref[BIAS_EXPAND + row : BIAS_EXPAND + row + 1, :].astype(F32)
        bias_ref[row : row + 1, :] = jnp.where(at == 0, mine, theirs)
        bias_ref[count + row : count + row + 1, :] = jnp.where(at == 0, theirs, mine)


def mlp_body(
    own_steps, place, x1_ref, h_ref, dy_ref, mine_ref, theirs_ref, mo_ref, mn_ref, mf_ref, eo_ref, en_ref, ef_ref,
    co_ref, cr_ref, out_ref, dx_ref, da_ref, dot_ref, sums_ref, be_ref, total_ref, dh_ref, bias_ref,
):
    at, core = place[0], place[1]
    step = pl.program_id(0)
    starts = piece_starts(at, core, mo_ref.shape[0])
    block = hidden_block(step, at, own_steps)

    @pl.when(step == 0)
    def _():
        total_ref[...] = jnp.zeros_like(total_ref)
        dh_ref[...] = jnp.zeros_like(dh_ref)
        read_expand_bias(at, mine_ref, theirs_ref, bias_ref)

    def work(contract_ref):
        contract = contract_ref[...].reshape(-1, contract_ref.shape[-1])
        inner = bias_ref[pl.ds(block, 1), :]
        for (begin, size), weight in zip(starts, (eo_ref, en_ref, ef_ref)):
            inner = inner + mm(h_ref[:, pl.ds(begin, size)], weight[...])
        active, slope = gelu_pair(inner)
        total_ref[...] += mm(active.astype(BF16), contract)
        grad = (mm_nt(dy_ref[...], contract) * slope).astype(BF16)
        be_ref[pl.ds(block, 1), :] = jnp.sum(grad.astype(F32), axis=0, keepdims=True)
        for (begin, size), weight in zip(starts, (eo_ref, en_ref, ef_ref)):
            dh_ref[:, pl.ds(begin, size)] += mm_nt(grad, weight[...])

    @pl.when(step < own_steps)
    def _():
        work(co_ref)

    @pl.when(step >= own_steps)
    def _():
        work(cr_ref)

    @pl.when(step == pl.num_programs(0) - 1)
    def _():
        x1 = x1_ref[...]
        bias = full_row(at, mine_ref, theirs_ref, BIAS_CONTRACT)
        out_ref[...] = (x1 + total_ref[...] + bias).astype(BF16)
        gain = full_row(at, mine_ref, theirs_ref, GAIN_MLP)
        unit, inverse = normalise(x1)
        grad = dh_ref[...]
        dy = dy_ref[...].astype(F32)
        dx = dy + normalise_back(grad, unit, inverse, gain)
        dx_ref[...] = dx
        da = dx.astype(BF16)
        da_ref[...] = da
        sums_ref[0:1, :] = jnp.sum(dy, axis=0, keepdims=True)
        sums_ref[1:2, :] = jnp.sum(grad * unit, axis=0, keepdims=True)
        sums_ref[2:3, :] = jnp.sum(grad, axis=0, keepdims=True)
        sums_ref[3:4, :] = jnp.sum(da.astype(F32), axis=0, keepdims=True)
        sums_ref[4:8, :] = jnp.zeros_like(sums_ref[4:8, :])
        for (begin, size), weight in zip(starts, (mo_ref, mn_ref, mf_ref)):
            dot_ref[pl.ds(begin, size), :] = mm_nt(weight[...], da).astype(BF16)


def hidden_block(step, at, own_steps):
    return jnp.where(step < own_steps, at * own_steps + step, (1 - at) * own_steps + step - own_steps)


def mlp(place, x1, normed, dy, mine, theirs, merge_w, expand, contract, contract_rest):
    rows, width = x1.shape
    wide = 512
    own_steps = contract.shape[0] // wide
    shards = wide // contract_rest.shape[1]
    steps = 2 * own_steps
    operands = (x1, normed, dy, mine, theirs, *merge_w)
    in_specs = [whole(member.shape) for member in operands]
    in_specs += [
        pl.BlockSpec((member.shape[0], wide), lambda i, s: (0, hidden_block(i, s[0], own_steps)))
        for member in expand
    ]
    in_specs += [
        pl.BlockSpec((wide, width), lambda i, _: (jnp.minimum(i, own_steps - 1), 0)),
        pl.BlockSpec(
            (shards, contract_rest.shape[1], width), lambda i, _: (jnp.maximum(i - own_steps, 0), 0, 0)
        ),
    ]
    shapes = [
        ((rows, width), BF16),
        ((rows, width), F32),
        ((rows, width), BF16),
        ((width, rows), BF16),
        ((8, width), F32),
        ((steps, wide), F32),
    ]
    return pl.pallas_call(
        functools.partial(mlp_body, own_steps),
        grid_spec=pltpu.PrefetchScalarGridSpec(
            num_scalar_prefetch=1,
            grid=(steps,),
            in_specs=in_specs,
            out_specs=[whole(shape) for shape, _ in shapes],
            scratch_shapes=[
                pltpu.VMEM((rows, width), F32),
                pltpu.VMEM((rows, width), F32),
                pltpu.VMEM((steps, wide), F32),
            ],
        ),
        out_shape=[jax.ShapeDtypeStruct(shape, dtype) for shape, dtype in shapes],
        compiler_params=params(),
        cost_estimate=about(18),
        name="mlp",
    )(place, *operands, *expand, contract, contract_rest)


def hidden_part(step, at, core, own_steps):
    part = own_steps // 2
    return jnp.where(
        step < part, at * own_steps + core * part + step, (1 - at) * own_steps + core * part + step - part
    )


def weights_body(own_steps, place, *refs):
    h_refs, dy_refs = refs[:4], refs[4:8]
    mine_ref, theirs_ref, eo_ref, en_ref, ef_ref, co_ref, cr_ref, out_ref, bias_ref, contract_ref, expand_ref = refs[8:]
    at, core = place[0], place[1]
    step = pl.program_id(0)
    part = own_steps // 2
    half = eo_ref.shape[0]
    starts = piece_starts(at, core, half)
    block = hidden_part(step, at, core, own_steps)
    wide = eo_ref.shape[1]
    chips, _, width = out_ref.shape
    contract_rows = part * wide // chips
    expand_rows = half // chips

    @pl.when(step == 0)
    def _():
        read_expand_bias(at, mine_ref, theirs_ref, bias_ref)

    def work(weight_ref, forward):
        contract = weight_ref[...].reshape(wide, width)
        bias = bias_ref[pl.ds(block, 1), :]
        for index, (h_ref, dy_ref) in enumerate(zip(h_refs, dy_refs)):
            inner = bias
            for (begin, size), weight in zip(starts, (eo_ref, en_ref, ef_ref)):
                inner = inner + mm(h_ref[:, pl.ds(begin, size)], weight[...])
            active, slope = gelu_pair(inner)
            grad = (mm_nt(dy_ref[...], contract) * slope).astype(BF16)
            own = mm_tn(h_ref[:, pl.ds(pl.multiple_of(at * half, half), half)], grad)
            if index == 0:
                expand_ref[...] = own
            else:
                expand_ref[...] += own
            if forward:
                own = mm_tn(active.astype(BF16), dy_ref[...])
                if index == 0:
                    contract_ref[...] = own
                else:
                    contract_ref[...] += own

    def store_expand(column):
        for turn in range(2):
            place_of = jnp.where(turn == 0, at, 1 - at)
            rows = pl.ds(pl.multiple_of(contract_rows + place_of * expand_rows, expand_rows), expand_rows)

            @pl.when(step // part == turn)
            def _():
                for chip in range(chips):
                    out_ref[chip, rows, column * wide : (column + 1) * wide] = expand_ref[
                        chip * expand_rows : (chip + 1) * expand_rows, :
                    ].astype(BF16)

    for now in range(part):

        @pl.when(step == now)
        def _():
            work(co_ref, True)
            some = wide // contract_rows
            for chip in range(some):
                out_ref[now * some + chip, :contract_rows, :] = contract_ref[
                    chip * contract_rows : (chip + 1) * contract_rows, :
                ].astype(BF16)

    @pl.when(step >= part)
    def _():
        work(cr_ref, False)

    for column in range(part):

        @pl.when(step % part == column)
        def _():
            store_expand(column)


def mlp_weights(place, chips, normed, dy, mine, theirs, expand, contract, contract_rest):
    rows, width = dy[0].shape
    wide = 512
    half = expand[0].shape[0]
    own_steps = contract.shape[0] // wide
    part = own_steps // 2
    shards = wide // contract_rest.shape[1]
    operands = (*normed, *dy, mine, theirs)
    in_specs = [whole(member.shape) for member in operands]
    in_specs += [
        pl.BlockSpec((member.shape[0], wide), lambda i, s: (0, hidden_part(i, s[0], s[1], own_steps)))
        for member in expand
    ]
    in_specs += [
        pl.BlockSpec((wide, width), lambda i, s: (s[1] * part + jnp.minimum(i, part - 1), 0)),
        pl.BlockSpec(
            (shards, contract_rest.shape[1], width),
            lambda i, s: (s[1] * part + jnp.maximum(i - part, 0), 0, 0),
        ),
    ]
    shape = (chips, part * wide // chips + 2 * (half // chips), width)
    return pl.pallas_call(
        functools.partial(weights_body, own_steps),
        grid_spec=pltpu.PrefetchScalarGridSpec(
            num_scalar_prefetch=1,
            grid=(own_steps,),
            in_specs=in_specs,
            out_specs=whole(shape),
            scratch_shapes=[
                pltpu.VMEM((2 * own_steps, wide), F32),
                pltpu.VMEM((wide, width), F32),
                pltpu.VMEM((half, wide), F32),
            ],
        ),
        out_shape=jax.ShapeDtypeStruct(shape, BF16),
        compiler_params=params(),
        cost_estimate=about(20),
        name="mlp_weights",
    )(place, *operands, *expand, contract, contract_rest)


def spread_mlp_body(in_ref, contract_ref, expand_ref):
    _, _, contract_rows, width = contract_ref.shape
    expand_rows = expand_ref.shape[0]
    for core in range(2):
        contract_ref[core, 0] = in_ref[core, :contract_rows, :].astype(F32)
        for part in range(2):
            first = contract_rows + part * expand_rows
            begin = (2 * part + core) * width
            expand_ref[:, begin : begin + width] = in_ref[core, first : first + expand_rows, :].astype(F32)


def spread_mlp(gathered, contract_shape, expand_shape):
    devices, rows, width = gathered.shape
    chips = devices // 2
    contract_rows = contract_shape[0] // devices
    expand_rows = expand_shape[0] // chips
    contract, expand = pl.pallas_call(
        spread_mlp_body,
        grid=(chips,),
        in_specs=[pl.BlockSpec((2, rows, width), lambda i: (i, 0, 0))],
        out_specs=[
            pl.BlockSpec((2, 1, contract_rows, width), lambda i: (0, i, 0, 0)),
            pl.BlockSpec((expand_rows, expand_shape[1]), lambda i: (i, 0)),
        ],
        out_shape=[
            jax.ShapeDtypeStruct((2, chips, contract_rows, width), F32),
            jax.ShapeDtypeStruct(expand_shape, F32),
        ],
        compiler_params=params(),
        cost_estimate=about(8),
        name="spread_mlp",
    )(gathered)
    return contract.reshape(contract_shape), expand


def merge_weights_body(place, oo_ref, ox_ref, ao_ref, ax_ref, out_ref):
    out_ref[...] = (mm_tn(oo_ref[...], ao_ref[...]) + mm_tn(ox_ref[...], ax_ref[...])).astype(BF16)


def merge_weights(place, mixed, grad):
    rows, width = mixed[0].shape
    half = width // 2
    return pl.pallas_call(
        merge_weights_body,
        grid_spec=pltpu.PrefetchScalarGridSpec(
            num_scalar_prefetch=1,
            grid=(1,),
            in_specs=[pl.BlockSpec((rows, half), lambda i, s: (0, s[0]))] * 2 + [whole((rows, width))] * 2,
            out_specs=whole((half, width)),
        ),
        out_shape=jax.ShapeDtypeStruct((half, width), BF16),
        compiler_params=params(),
        cost_estimate=about(4),
        name="merge_weights",
    )(place, *mixed, *grad)


def heads_body(dp_ref, h_ref, out_ref):
    @pl.when(pl.program_id(0) == 0)
    def _():
        out_ref[...] = jnp.zeros_like(out_ref)

    _, parts, head, lanes = dp_ref.shape
    out_ref[...] += mm(dp_ref[0].reshape(parts * head, lanes), h_ref[0])


def heads_gradient(dp, normed):
    sources, parts, head, lanes = dp.shape
    width = normed.shape[2]
    return pl.pallas_call(
        heads_body,
        grid=(sources,),
        in_specs=[
            pl.BlockSpec((1, parts, head, lanes), lambda i: (i, 0, 0, 0)),
            pl.BlockSpec((1, lanes, width), lambda i: (i, 0, 0)),
        ],
        out_specs=whole((parts * head, width)),
        out_shape=jax.ShapeDtypeStruct((parts * head, width), F32),
        compiler_params=params(),
        cost_estimate=about(11),
        name="heads_gradient",
    )(dp, normed)


def spread_body(in_ref, heads_ref, merge_ref):
    heads, rows, half = in_ref.shape
    parts = heads_ref.shape[1] // (heads * HEAD)
    some = 4
    for part in range(parts):
        for first in range(0, heads, some):
            piece = in_ref[first : first + some, part * HEAD : (part + 1) * HEAD, :]
            column = (part * heads + first) * HEAD
            heads_ref[:, column : column + some * HEAD] = piece.reshape(some * HEAD, half).astype(F32).T
    merge_rows = merge_ref.shape[0] // heads
    for head in range(heads):
        for side in range(2):
            first = parts * HEAD + side * merge_rows
            merge_ref[head * merge_rows : (head + 1) * merge_rows, side * half : (side + 1) * half] = in_ref[
                head, first : first + merge_rows, :
            ].astype(F32)


def spread_heads(gathered, heads_shape, merge_shape):
    return pl.pallas_call(
        spread_body,
        out_shape=[jax.ShapeDtypeStruct(heads_shape, F32), jax.ShapeDtypeStruct(merge_shape, F32)],
        compiler_params=params(),
        cost_estimate=about(9),
        name="spread_heads",
    )(gathered)


def back_body(
    place, dp_ref, x_ref, dx_ref, mine_ref, theirs_ref, own_ref, qn_ref, qf_ref, rn_ref, rf_ref, out_ref, sums_ref, dh_ref
):
    at, core = place[0], place[1]
    part = pl.program_id(0)
    starts = piece_starts(at, core, own_ref.shape[0])
    heads, _, head, rows = dp_ref.shape

    @pl.when(part == 0)
    def _():
        dh_ref[...] = jnp.zeros_like(dh_ref)
        sums_ref[...] = jnp.zeros_like(sums_ref)

    def work(weights):
        grad = dp_ref[...].reshape(heads * head, rows)
        for (begin, size), weight in zip(starts, weights):
            dh_ref[pl.ds(begin, size), :] += mm(weight[...], grad)
        return mm_nt(jnp.ones((8, rows), BF16), grad)[0:1, :]

    @pl.when(part == 0)
    def _():
        sums_ref[2:3, :] = work((own_ref, qn_ref, qf_ref))

    @pl.when(part == 1)
    def _():
        work((own_ref, rn_ref, rf_ref))

    @pl.when(part == 2)
    def _():
        sums_ref[3:4, :] = work((own_ref, rn_ref, rf_ref))
        dh = dh_ref[...].T
        unit, inverse = normalise(x_ref[...].astype(F32))
        gain = full_row(at, mine_ref, theirs_ref, GAIN_ATTN)
        out_ref[...] = dx_ref[...] + normalise_back(dh, unit, inverse, gain)
        sums_ref[0:1, :] = jnp.sum(dh * unit, axis=0, keepdims=True)
        sums_ref[1:2, :] = jnp.sum(dh, axis=0, keepdims=True)


def back(place, dp, x, dx, mine, theirs, own, query_w, rest_w):
    rows, width = x.shape
    heads, parts, head, _ = dp.shape
    vectors = (x, dx, mine, theirs)
    return pl.pallas_call(
        back_body,
        grid_spec=pltpu.PrefetchScalarGridSpec(
            num_scalar_prefetch=1,
            grid=(parts,),
            in_specs=[pl.BlockSpec((heads, 1, head, rows), lambda t, _: (0, t, 0, 0))]
            + [whole(member.shape) for member in vectors]
            + [pl.BlockSpec((own.shape[0], width), lambda t, _: (0, t))]
            + [whole(member.shape) for member in query_w]
            + [pl.BlockSpec((member.shape[0], width), lambda t, _: (0, jnp.maximum(t - 1, 0))) for member in rest_w],
            out_specs=[whole((rows, width)), whole((8, width))],
            scratch_shapes=[pltpu.VMEM((width, rows), F32)],
        ),
        out_shape=[
            jax.ShapeDtypeStruct((rows, width), F32),
            jax.ShapeDtypeStruct((8, width), F32),
        ],
        compiler_params=params(),
        cost_estimate=about(8),
        name="back",
    )(place, dp, *vectors, own, *query_w, *rest_w)


def after(value, *others):
    return lax.optimization_barrier((value,) + others)[0]


def per_device(
    nctx, tokens_in, gain_attn, shift_attn, w_heads, bias_query, bias_value, w_merge, bias_merge, gain_mlp, shift_mlp,
    w_expand, bias_expand, w_contract, bias_contract, cotangent,
):
    seqs, tokens, width = tokens_in.shape
    rows = seqs * tokens
    half = width // 2
    heads = width // HEAD
    hidden = w_expand.shape[1]
    pairs = seqs * heads
    same = max(1, nctx // pairs)
    per = max(1, pairs // nctx)
    groups = seqs // per
    ctx = lax.axis_index("ctx")
    at = lax.axis_index("fsdp")
    core = ctx % 2
    place = jnp.stack([at, core]).astype(jnp.int32)

    def over_x(value):
        return lax.ppermute(value, "fsdp", [(0, 1), (1, 0)])

    def over_core(value):
        return lax.ppermute(value, "ctx", [(i, i ^ 1) for i in range(nctx)])

    def exchange(value):
        return lax.all_to_all(value, "ctx", 0, 0)

    def to_send(value):
        lead = value.shape[1:-1]
        value = value.reshape((heads,) + lead + (groups, per * tokens))
        value = jnp.moveaxis(value, -2, 1).reshape((nctx // same,) + lead + (per * tokens,))
        return value if same == 1 else jnp.repeat(value, same, axis=0)

    def received(value):
        value = value[::same]
        lead = value.shape[1:-1]
        value = value.reshape((heads, groups) + lead + (per * tokens,))
        return jnp.moveaxis(value, 1, -2).reshape((heads,) + lead + (rows,))

    def quarter_of(weight, first, count):
        size = weight.shape[0] // 2
        return lax.dynamic_slice(weight, (core * size, first), (size, count))

    def halves(value):
        mine = lax.dynamic_index_in_dim(value, at, 0, keepdims=False)
        return mine + over_x(lax.dynamic_index_in_dim(value, 1 - at, 0, keepdims=False))

    mine = jnp.concatenate(
        [
            member.reshape(-1, half)
            for member in (
                gain_attn, shift_attn, bias_query, bias_value, bias_merge, gain_mlp, shift_mlp, bias_contract,
                bias_expand, jnp.zeros(((-8 - bias_expand.shape[0] // half) % 16 * half,), BF16),
            )
        ]
    )
    theirs = over_x(mine)
    query_near = over_x(quarter_of(w_heads, 0, width))
    query_w = (query_near, over_core(query_near))
    shard = w_contract.shape[0] // nctx
    contract_shard = over_x(
        after(lax.dynamic_slice_in_dim(w_contract, ctx * shard, shard, 0), query_near)
    )
    contract_rest = lax.all_gather(contract_shard, "ctx", axis=0, tiled=False)
    rest_near = over_x(after(quarter_of(w_heads, width, 2 * width), query_near))
    rest_w = (rest_near, over_core(rest_near))
    expand_near = over_x(after(quarter_of(w_expand, 0, hidden), rest_near))
    merge_near = over_x(after(quarter_of(w_merge, 0, width), rest_near))

    x = tokens_in.reshape(rows, width)
    dy = cotangent.reshape(rows, width)
    dy_x = over_x(after(dy, expand_near))

    query_rows, normed = front_query(place, x, mine, theirs, w_heads, *query_w)
    query = exchange(to_send(query_rows))
    kv = exchange(to_send(front_rest(place, normed, mine, theirs, w_heads, *rest_w)))
    normed_all = lax.all_gather(after(normed, kv), "ctx", axis=0, tiled=False)
    mixed_b, mixed_f, lse = attend(query, kv, per)
    expand_w = (w_expand, expand_near, over_core(after(expand_near, lse)))
    merge_w = (w_merge, merge_near, over_core(after(merge_near, lse)))
    mixed = received(exchange(mixed_b)).reshape(width, rows)
    x1, normed_two, mixed_rows = merge(place, x, mixed, mine, theirs, merge_w)

    def of_four(value, there):
        return value, there, over_core(value), over_core(there)

    normed_four = of_four(normed_two, over_x(normed_two))
    dy_four = of_four(after(dy, lse), dy_x)
    mixed_x = over_x(mixed_rows)
    block_out, dx1, da, grad_mixed, sums_mlp, sums_expand = mlp(
        place, x1, normed_two, dy, mine, theirs, merge_w, expand_w, w_contract, contract_rest
    )
    grad_out = exchange(to_send(grad_mixed.reshape(heads, HEAD, rows)))

    grad_mlp = mlp_weights(
        place, nctx // 2, normed_four, dy_four, mine, theirs, expand_w, w_contract, contract_rest
    )
    chips = [[2 * chip + one for chip in range(nctx // 2)] for one in range(2)]
    grad_mlp = lax.psum_scatter(grad_mlp, "ctx", scatter_dimension=0, axis_index_groups=chips)
    grad_mlp = lax.all_gather(grad_mlp, "ctx", axis=0, tiled=False)
    contract_sum, expand_sum = spread_mlp(grad_mlp, w_contract.shape, w_expand.shape)

    grad_merge = merge_weights(place, (mixed_rows, mixed_x), (da, over_x(da)))
    vectors = halves(
        jnp.concatenate(
            [sums_mlp[:4].reshape(4, 2, half).swapaxes(0, 1), sums_expand.reshape(2, -1, half)], axis=1
        )
    )
    vectors = vectors.reshape(-1, width).astype(BF16)
    vectors = jnp.pad(vectors, ((0, -vectors.shape[0] % 16), (0, 0)))
    parcel = jnp.concatenate(
        [grad_merge.reshape(nctx, -1, width), jnp.broadcast_to(vectors, (nctx,) + vectors.shape)], axis=1
    )
    parcel = jnp.sum(exchange(parcel).astype(F32), axis=0)
    merge_part = parcel[: half // nctx].astype(BF16)
    vectors = parcel[half // nctx :].reshape(-1, half)

    dqkv = attend_back(query, kv, grad_out, mixed_f, lse, per)
    dp = received(exchange(dqkv))

    if groups > 1:
        normed_all = lax.dynamic_slice_in_dim(normed_all, (ctx // same % groups) * tokens * per, tokens * per, 1)
    grad_heads = heads_gradient(dqkv, normed_all)
    if groups > 1:
        members = [
            [first + one + same * group for group in range(groups)]
            for first in range(0, nctx, groups * same)
            for one in range(same)
        ]
        grad_heads = lax.psum(grad_heads, "ctx", axis_index_groups=members)
    kept = lax.dynamic_slice_in_dim(grad_heads, at * half, half, 1)
    sent = lax.dynamic_slice_in_dim(grad_heads, (1 - at) * half, half, 1)
    kept = (kept + over_x(sent.astype(BF16)).astype(F32)).astype(BF16)
    if groups * same > 1:
        share = kept.shape[0] // (groups * same)
        kept = lax.dynamic_slice_in_dim(kept, ctx % (groups * same) * share, share, 0)
    kept = jnp.concatenate([kept, merge_part[:, :half], merge_part[:, half:]])
    spread = lax.all_gather(kept, "ctx", axis=0, tiled=False)
    if groups * same > 1:
        share = 3 * HEAD // (groups * same)
        first = spread[:, :share].reshape(heads, 3 * HEAD, half)
        rest = spread[:, share:].reshape(heads, groups * same, 2, -1, half)
        rest = jnp.moveaxis(rest, 1, 2).reshape(heads, -1, half)
        spread = jnp.concatenate([first, rest], axis=1)
    heads_sum, merge_sum = spread_heads(spread, w_heads.shape, w_merge.shape)

    grad_tokens, sums_attn = back(place, dp, x, dx1, mine, theirs, w_heads, query_w, rest_w)
    last = halves(sums_attn[:4].reshape(4, 2, half).swapaxes(0, 1))
    last = jnp.sum(exchange(jnp.broadcast_to(last, (nctx,) + last.shape)), axis=0)
    return (
        block_out.reshape(tokens_in.shape),
        grad_tokens.reshape(tokens_in.shape),
        last[0],
        last[1],
        heads_sum,
        last[2],
        last[3],
        merge_sum,
        vectors[3],
        vectors[1],
        vectors[2],
        expand_sum,
        vectors[4 : 4 + hidden // width].reshape(-1),
        contract_sum,
        vectors[0],
    )


def solution(mesh):
    rows, vec, mat = P("fsdp", "ctx", None), P("fsdp"), P("fsdp", None)
    return jax.shard_map(
        functools.partial(per_device, mesh.shape["ctx"]),
        mesh=mesh,
        in_specs=(rows, vec, vec, mat, vec, vec, mat, vec, vec, vec, mat, vec, mat, vec, rows),
        out_specs=(rows, rows, vec, vec, mat, vec, vec, mat, vec, vec, vec, mat, vec, mat, vec),
        check_vma=False,
    )
```

```python
import functools
import math

import jax
import jax.numpy as jnp
from jax import lax
from jax.experimental import pallas as pl
from jax.experimental.pallas import tpu as pltpu
from jax.sharding import PartitionSpec as P

HEAD = 64
EPS = 1e-05
LOWEST = -1e30
GELU_A = math.sqrt(2.0 / math.pi)
GELU_B = 0.044715
F32 = jnp.float32
BF16 = jnp.bfloat16
VMEM_BYTES = 62 * 1024 * 1024
GAIN_ATTN, SHIFT_ATTN, BIAS_QUERY, BIAS_VALUE = 0, 1, 2, 3
BIAS_MERGE, GAIN_MLP, SHIFT_MLP, BIAS_CONTRACT = 4, 5, 6, 7
BIAS_EXPAND = 8
SUM_EXPAND = 4


def mm(left, right):
    return jnp.dot(left, right, preferred_element_type=F32)


def mm_nt(left, right):
    return lax.dot_general(left, right, (((1,), (1,)), ((), ())), preferred_element_type=F32)


def mm_tn(left, right):
    return lax.dot_general(left, right, (((0,), (0,)), ((), ())), preferred_element_type=F32)


def params(**extra):
    return pltpu.CompilerParams(vmem_limit_bytes=VMEM_BYTES, **extra)


def about(us):
    return pl.CostEstimate(flops=int(us * 1.15e9), bytes_accessed=0, transcendentals=0)


def whole(shape):
    return pl.BlockSpec(shape, lambda *_: (0,) * len(shape))


def full_row(at, mine_ref, theirs_ref, row):
    half = mine_ref.shape[1] // 2
    line, lanes = row // 2, slice(row % 2 * half, (row % 2 + 1) * half)
    mine = mine_ref[line : line + 1, lanes].astype(F32)
    theirs = theirs_ref[line : line + 1, lanes].astype(F32)
    low = jnp.where(at == 0, mine, theirs)
    high = jnp.where(at == 0, theirs, mine)
    return jnp.concatenate([low, high], axis=1)


def normalise(rows):
    mean = jnp.mean(rows, axis=-1, keepdims=True)
    centered = rows - mean
    variance = jnp.mean(centered * centered, axis=-1, keepdims=True)
    inverse = lax.rsqrt(variance + EPS)
    return centered * inverse, inverse


def normalise_back(grad, unit, inverse, gain):
    scaled = grad * gain
    mean = jnp.mean(scaled, axis=-1, keepdims=True)
    along = jnp.mean(scaled * unit, axis=-1, keepdims=True)
    return inverse * (scaled - mean - unit * along)


def piece_starts(at, core, half):
    other = (1 - at) * half
    quarter = half // 2
    return (
        (pl.multiple_of(at * half, quarter), half),
        (pl.multiple_of(other + core * quarter, quarter), quarter),
        (pl.multiple_of(other + (1 - core) * quarter, quarter), quarter),
    )


def parcel_body(place, heads_ref, contract_ref, *refs):
    vectors, first_ref, mine_ref = refs[:9], refs[9], refs[10]
    quarter, shard = heads_ref.shape[0], contract_ref.shape[0]
    first_ref[:quarter, :] = heads_ref[...]
    first_ref[quarter : quarter + shard, :] = contract_ref[...]
    mine_ref[...] = jnp.zeros_like(mine_ref)
    at = 0
    width = mine_ref.shape[1]
    for vector in vectors:
        value = vector[...].astype(F32)
        size = min(value.shape[0], width)
        for begin in range(0, value.shape[0], size):
            line, lane = at // width, at % width
            piece = value[begin : begin + size].reshape(1, size)
            mine_ref[line : line + 1, lane : lane + size] = piece.astype(BF16)
            at += size
    first_ref[quarter + shard :, :] = mine_ref[...]


def parcel(place, w_heads, w_contract, vectors, shard):
    quarter, width = w_heads.shape[0] // 2, w_contract.shape[1]
    lines = -(-sum(vector.size for vector in vectors) // (16 * width)) * 16
    shapes = [(quarter + shard + lines, width), (lines, width)]
    return pl.pallas_call(
        parcel_body,
        grid_spec=pltpu.PrefetchScalarGridSpec(
            num_scalar_prefetch=1,
            grid=(1,),
            in_specs=[
                pl.BlockSpec((quarter, width), lambda i, s: (s[1], 0)),
                pl.BlockSpec((shard, width), lambda i, s: (s[4], 0)),
            ]
            + [whole(vector.shape) for vector in vectors],
            out_specs=[whole(shape) for shape in shapes],
        ),
        out_shape=[jax.ShapeDtypeStruct(shape, BF16) for shape in shapes],
        compiler_params=params(),
        cost_estimate=about(1),
        name="parcel",
    )(place, w_heads, w_contract, *vectors)


def project(at, core, normed, bias, own, near, far, out_ref, part):
    total = bias
    for (begin, size), weight in zip(piece_starts(at, core, own.shape[0]), (own, near, far)):
        total = total + mm(normed[:, pl.ds(begin, size)], weight[...])
    turned = total.T.astype(BF16)
    for head in range(turned.shape[0] // HEAD):
        piece = turned[head * HEAD : (head + 1) * HEAD, :]
        if part is None:
            out_ref[head] = piece
        else:
            out_ref[head, part] = piece


def front_query_body(place, x_ref, mine_ref, theirs_ref, own, near, far, out_ref, h_ref, bias_ref):
    at, core = place[0], place[1]
    step = pl.program_id(0)
    wide = own.shape[1]

    @pl.when(step == 0)
    def _():
        unit, _ = normalise(x_ref[...].astype(F32))
        gain = full_row(at, mine_ref, theirs_ref, GAIN_ATTN)
        shift = full_row(at, mine_ref, theirs_ref, SHIFT_ATTN)
        h_ref[...] = (unit * gain + shift).astype(BF16)
        bias_ref[0:1, :] = full_row(at, mine_ref, theirs_ref, BIAS_QUERY)

    columns = pl.ds(pl.multiple_of(step * wide, wide), wide)
    project(at, core, h_ref, bias_ref[0:1, columns], own, near, far, out_ref, None)


def front_query(place, x, mine, theirs, own, near, far):
    rows, width = x.shape
    heads = width // HEAD
    wide = 256
    return pl.pallas_call(
        front_query_body,
        grid_spec=pltpu.PrefetchScalarGridSpec(
            num_scalar_prefetch=1,
            grid=(width // wide,),
            in_specs=[whole(x.shape), whole(mine.shape), whole(theirs.shape)]
            + [pl.BlockSpec((member.shape[0], wide), lambda i, _: (0, i)) for member in (own, near, far)],
            out_specs=[
                pl.BlockSpec((wide // HEAD, HEAD, rows), lambda i, _: (i, 0, 0)),
                whole((rows, width)),
            ],
            scratch_shapes=[pltpu.VMEM((8, width), F32)],
        ),
        out_shape=[
            jax.ShapeDtypeStruct((heads, HEAD, rows), BF16),
            jax.ShapeDtypeStruct((rows, width), BF16),
        ],
        compiler_params=params(),
        cost_estimate=about(1),
        name="front_query",
    )(place, x, mine, theirs, own, near, far)


def front_rest_body(place, h_ref, mine_ref, theirs_ref, *rest):
    weights, (out_ref, bias_ref) = rest[:6], rest[6:]
    at, core = place[0], place[1]
    step = pl.program_id(0)
    wide = weights[0].shape[1]

    @pl.when(step == 0)
    def _():
        bias_ref[0:1, :] = jnp.zeros_like(bias_ref[0:1, :])
        bias_ref[1:2, :] = full_row(at, mine_ref, theirs_ref, BIAS_VALUE)

    columns = pl.ds(pl.multiple_of(step * wide, wide), wide)
    for part in range(2):
        bias = bias_ref[part : part + 1, columns]
        project(at, core, h_ref, bias, *weights[3 * part : 3 * part + 3], out_ref, part)


def front_rest(place, normed, mine, theirs, own, near, far):
    rows, width = normed.shape
    heads = width // HEAD
    wide = 256
    steps = width // wide
    specs = []
    for part in range(2):
        for member, skip in ((own, 1), (near, 0), (far, 0)):
            first = (part + skip) * steps
            specs.append(pl.BlockSpec((member.shape[0], wide), lambda i, _, first=first: (0, first + i)))
    return pl.pallas_call(
        front_rest_body,
        grid_spec=pltpu.PrefetchScalarGridSpec(
            num_scalar_prefetch=1,
            grid=(steps,),
            in_specs=[whole(normed.shape), whole(mine.shape), whole(theirs.shape)] + specs,
            out_specs=pl.BlockSpec((wide // HEAD, 2, HEAD, rows), lambda i, _: (i, 0, 0, 0)),
            scratch_shapes=[pltpu.VMEM((8, width), F32)],
        ),
        out_shape=jax.ShapeDtypeStruct((heads, 2, HEAD, rows), BF16),
        compiler_params=params(),
        cost_estimate=about(1),
        name="front_rest",
    )(place, normed, mine, theirs, *([own, near, far] * 2))


def lay_out(source, target, per, tokens, block, turned=False, scale=None):
    for src in range(source.shape[0]):
        for pair in range(per):
            piece = source[src, :, pair * tokens : (pair + 1) * tokens]
            if scale is not None:
                piece = piece * jnp.asarray(scale, BF16)
            begin = src * tokens
            if turned:
                target[pair, begin : begin + tokens, :] = piece.astype(F32).T.astype(BF16)
            else:
                inner = begin % block
                target[pair, begin // block, :, inner : inner + tokens] = piece


def allowed_at(first_key, first_query, keys, queries):
    key_at = first_key + lax.broadcasted_iota(jnp.int32, (keys, queries), 0)
    query_at = first_query + lax.broadcasted_iota(jnp.int32, (keys, queries), 1)
    return key_at <= query_at


def attend_body(per, tokens, block, chunk, query_ref, kv_ref, out_ref, outf_ref, lse_ref, q_ref, k_ref, v_ref):
    step = pl.program_id(0)

    @pl.when(step == 0)
    def _():
        lay_out(query_ref, q_ref, per, tokens, block, scale=HEAD**-0.5)
        lay_out(kv_ref.at[:, 0], k_ref, per, tokens, chunk, turned=True)
        lay_out(kv_ref.at[:, 1], v_ref, per, tokens, chunk)

    queries = [q_ref[pair, step] for pair in range(per)]

    def scores(pair, index):
        keys = k_ref[pair, pl.ds(pl.multiple_of(index * chunk, chunk), chunk), :]
        return mm(keys, queries[pair])

    last = (step * block) // chunk
    allowed = allowed_at(last * chunk, step * block, chunk, block)
    carried = []
    for pair in range(per):
        masked = jnp.where(allowed, scores(pair, last), LOWEST)
        top = jnp.max(masked, axis=0, keepdims=True)
        weights = jnp.exp(masked - top)
        total = jnp.sum(weights, axis=0, keepdims=True)
        mixed = mm(v_ref[pair, last], weights.astype(BF16))
        carried += [top, total, mixed]

    def one(index, state):
        fresh = []
        for pair in range(per):
            top, total, mixed = state[3 * pair : 3 * pair + 3]
            here = scores(pair, index)
            new_top = jnp.maximum(top, jnp.max(here, axis=0, keepdims=True))
            weights = jnp.exp(here - new_top)
            factor = jnp.exp(top - new_top)
            total = total * factor + jnp.sum(weights, axis=0, keepdims=True)
            mixed = mixed * factor + mm(v_ref[pair, index], weights.astype(BF16))
            fresh += [new_top, total, mixed]
        return tuple(fresh)

    final = lax.fori_loop(0, last, one, tuple(carried))
    for pair in range(per):
        top, total, mixed = final[3 * pair : 3 * pair + 3]
        mixed = mixed / total
        lse_ref[0, pair : pair + 1, :] = top + jnp.log(total)
        for dst in range(block // tokens):
            piece = mixed[:, dst * tokens : (dst + 1) * tokens]
            lanes = slice(pair * tokens, (pair + 1) * tokens)
            outf_ref[dst, :, lanes] = piece
            out_ref[dst, :, lanes] = piece.astype(BF16)


def attend(query, kv, per, block=512, chunk=512):
    sources, _, lanes = query.shape
    tokens = lanes // per
    length = sources * tokens
    steps = length // block
    here = pl.BlockSpec((block // tokens, HEAD, lanes), lambda i: (i, 0, 0))
    return pl.pallas_call(
        functools.partial(attend_body, per, tokens, block, chunk),
        grid=(steps,),
        in_specs=[whole(query.shape), whole(kv.shape)],
        out_specs=[here, here, pl.BlockSpec((1, 8, block), lambda i: (i, 0, 0))],
        out_shape=[
            jax.ShapeDtypeStruct((sources, HEAD, lanes), BF16),
            jax.ShapeDtypeStruct((sources, HEAD, lanes), F32),
            jax.ShapeDtypeStruct((steps, 8, block), F32),
        ],
        scratch_shapes=[
            pltpu.VMEM((per, steps, HEAD, block), BF16),
            pltpu.VMEM((per, length, HEAD), BF16),
            pltpu.VMEM((per, length // chunk, HEAD, chunk), BF16),
        ],
        compiler_params=params(),
        cost_estimate=about(2),
        name="attend",
    )(query, kv)


def attend_back_body(
    per, tokens, block, chunk, query_ref, kv_ref, go_ref, of_ref, lse_ref, out_ref, qt_ref, q_ref, kt_ref, k_ref, v_ref,
    dk_ref, dv_ref,
):
    sources = query_ref.shape[0]
    step = pl.program_id(0)

    @pl.when(step == 0)
    def _():
        lay_out(query_ref, qt_ref, per, tokens, block, scale=HEAD**-0.5)
        lay_out(query_ref, q_ref, per, tokens, block, turned=True, scale=HEAD**-0.5)
        lay_out(kv_ref.at[:, 0], kt_ref, per, tokens, chunk, scale=HEAD**-0.5)
        lay_out(kv_ref.at[:, 0], k_ref, per, tokens, chunk, turned=True)
        lay_out(kv_ref.at[:, 1], v_ref, per, tokens, chunk, turned=True)
        dk_ref[...] = jnp.zeros_like(dk_ref)
        dv_ref[...] = jnp.zeros_like(dv_ref)

    inner = block // tokens
    grads, deltas, lses, turned_grads, turned_queries, queries = [], [], [], [], [], []
    for pair in range(per):
        lanes = slice(pair * tokens, (pair + 1) * tokens)
        grad = jnp.concatenate([go_ref[dst, :, lanes] for dst in range(inner)], axis=1)
        mixed = jnp.concatenate([of_ref[dst, :, lanes] for dst in range(inner)], axis=1)
        wide = grad.astype(F32)
        grads.append(grad)
        deltas.append(jnp.sum(wide * mixed, axis=0, keepdims=True))
        turned_grads.append(wide.T.astype(BF16))
        lses.append(lse_ref[0, pair : pair + 1, :])
        queries.append(qt_ref[pair, step])
        turned_queries.append(q_ref[pair, pl.ds(pl.multiple_of(step * block, block), block), :])

    def one(index, state, allowed):
        rows = pl.ds(pl.multiple_of(index * chunk, chunk), chunk)
        fresh = []
        for pair in range(per):
            weights = jnp.exp(mm(k_ref[pair, rows, :], queries[pair]) - lses[pair])
            if allowed is not None:
                weights = jnp.where(allowed, weights, 0.0)
            back = mm(v_ref[pair, rows, :], grads[pair])
            dscore = (weights * (back - deltas[pair])).astype(BF16)
            dv_ref[pair, rows, :] += mm(weights.astype(BF16), turned_grads[pair])
            dk_ref[pair, rows, :] += mm(dscore, turned_queries[pair])
            fresh.append(state[pair] + mm(kt_ref[pair, index], dscore))
        return tuple(fresh)

    last = (step * block) // chunk
    start = tuple(jnp.zeros((HEAD, block), F32) for _ in range(per))
    state = lax.fori_loop(0, last, lambda i, s: one(i, s, None), start)
    state = one(last, state, allowed_at(last * chunk, step * block, chunk, block))
    for pair in range(per):
        lanes = slice(pair * tokens, (pair + 1) * tokens)
        for dst in range(inner):
            out_ref[step * inner + dst, 0, :, lanes] = state[pair][
                :, dst * tokens : (dst + 1) * tokens
            ].astype(BF16)

    @pl.when(step == pl.num_programs(0) - 1)
    def _():
        for pair in range(per):
            lanes = slice(pair * tokens, (pair + 1) * tokens)
            for src in range(sources):
                rows = slice(src * tokens, (src + 1) * tokens)
                out_ref[src, 1, :, lanes] = dk_ref[pair, rows, :].T.astype(BF16)
                out_ref[src, 2, :, lanes] = dv_ref[pair, rows, :].T.astype(BF16)


def attend_back(query, kv, grad, mixed, lse, per, chunk=512):
    sources, _, lanes = query.shape
    tokens = lanes // per
    length = sources * tokens
    steps, _, block = lse.shape
    here = pl.BlockSpec((block // tokens, HEAD, lanes), lambda i: (i, 0, 0))
    shape = (sources, 3, HEAD, lanes)
    return pl.pallas_call(
        functools.partial(attend_back_body, per, tokens, block, chunk),
        grid=(steps,),
        in_specs=[
            whole(query.shape), whole(kv.shape), here, here, pl.BlockSpec((1, 8, block), lambda i: (i, 0, 0)),
        ],
        out_specs=whole(shape),
        out_shape=jax.ShapeDtypeStruct(shape, BF16),
        scratch_shapes=[
            pltpu.VMEM((per, steps, HEAD, block), BF16),
            pltpu.VMEM((per, length, HEAD), BF16),
            pltpu.VMEM((per, length // chunk, HEAD, chunk), BF16),
            pltpu.VMEM((per, length, HEAD), BF16),
            pltpu.VMEM((per, length, HEAD), BF16),
            pltpu.VMEM((per, length, HEAD), F32),
            pltpu.VMEM((per, length, HEAD), F32),
        ],
        compiler_params=params(),
        cost_estimate=about(40),
        name="attend_back",
    )(query, kv, grad, mixed, lse)


def merge_body(place, x_ref, ot_ref, mine_ref, theirs_ref, mo_ref, mn_ref, mf_ref, x1_ref, h_ref, o_ref):
    at, core = place[0], place[1]
    starts = piece_starts(at, core, mo_ref.shape[0])
    o_ref[...] = ot_ref[...].astype(F32).T.astype(BF16)
    merged = full_row(at, mine_ref, theirs_ref, BIAS_MERGE)
    for (begin, size), weight in zip(starts, (mo_ref, mn_ref, mf_ref)):
        merged = merged + mm(o_ref[:, pl.ds(begin, size)], weight[...])
    x1 = x_ref[...].astype(F32) + merged
    x1_ref[...] = x1
    unit, _ = normalise(x1)
    gain = full_row(at, mine_ref, theirs_ref, GAIN_MLP)
    shift = full_row(at, mine_ref, theirs_ref, SHIFT_MLP)
    h_ref[...] = (unit * gain + shift).astype(BF16)


def merge(place, x, ot, mine, theirs, weights):
    shape = x.shape
    operands = (x, ot, mine, theirs, *weights)
    return pl.pallas_call(
        merge_body,
        grid_spec=pltpu.PrefetchScalarGridSpec(
            num_scalar_prefetch=1,
            grid=(1,),
            in_specs=[whole(member.shape) for member in operands],
            out_specs=[whole(shape)] * 3,
        ),
        out_shape=[
            jax.ShapeDtypeStruct(shape, F32),
            jax.ShapeDtypeStruct(shape, BF16),
            jax.ShapeDtypeStruct(shape, BF16),
        ],
        compiler_params=params(),
        cost_estimate=about(1),
        name="merge",
    )(place, *operands)


def gelu_pair(inner):
    square = inner * inner
    bend = jnp.tanh(GELU_A * (inner + GELU_B * (inner * square)))
    active = 0.5 * inner * (1.0 + bend)
    slope = 0.5 * (1.0 + bend) + 0.5 * inner * (1.0 - bend * bend) * (GELU_A * (1.0 + 3.0 * GELU_B * square))
    return active, slope


def read_expand_bias(at, mine_ref, theirs_ref, bias_ref):
    count, wide = bias_ref.shape
    count = count // 2
    beside = mine_ref.shape[1] // wide
    for row in range(count):
        line = BIAS_EXPAND // 2 + row // beside
        lanes = slice(row % beside * wide, (row % beside + 1) * wide)
        mine = mine_ref[line : line + 1, lanes].astype(F32)
        theirs = theirs_ref[line : line + 1, lanes].astype(F32)
        bias_ref[row : row + 1, :] = jnp.where(at == 0, mine, theirs)
        bias_ref[count + row : count + row + 1, :] = jnp.where(at == 0, theirs, mine)


def mlp_body(
    place, x1_ref, h_ref, dy_ref, mine_ref, theirs_ref, mo_ref, mn_ref, mf_ref, eo_ref, en0_ref, en1_ref, ef0_ref,
    ef1_ref, own_ref, rest_ref, out_ref, dx_ref, da_ref, dot_ref, total_ref, dh_ref, bias_ref, sums_ref,
):
    at, core = place[0], place[1]
    step = pl.program_id(0)
    starts = piece_starts(at, core, mo_ref.shape[0])
    wide = eo_ref.shape[1]
    width = sums_ref.shape[1]
    beside = width // wide

    @pl.when(step == 0)
    def _():
        total_ref[...] = jnp.zeros_like(total_ref)
        dh_ref[...] = jnp.zeros_like(dh_ref)
        sums_ref[...] = jnp.zeros_like(sums_ref)
        read_expand_bias(at, mine_ref, theirs_ref, bias_ref)

    contract = contract_block(step, pl.num_programs(0), at, own_ref, rest_ref)
    expand = expand_pieces(step, pl.num_programs(0), eo_ref, en0_ref, en1_ref, ef0_ref, ef1_ref)
    inner = bias_ref[pl.ds(step, 1), :]
    for (begin, size), weight in zip(starts, expand):
        inner = inner + mm(h_ref[:, pl.ds(begin, size)], weight)
    active, slope = gelu_pair(inner)
    total_ref[...] += mm(active.astype(BF16), contract)
    grad = (mm_nt(dy_ref[...], contract) * slope).astype(BF16)
    sums_ref[
        pl.ds(SUM_EXPAND + step // beside, 1), pl.ds(pl.multiple_of(step % beside * wide, wide), wide)
    ] = jnp.sum(grad.astype(F32), axis=0, keepdims=True)
    for (begin, size), weight in zip(starts, expand):
        dh_ref[:, pl.ds(begin, size)] += mm_nt(grad, weight)

    @pl.when(step == pl.num_programs(0) - 1)
    def _():
        x1 = x1_ref[...]
        bias = full_row(at, mine_ref, theirs_ref, BIAS_CONTRACT)
        out_ref[...] = (x1 + total_ref[...] + bias).astype(BF16)
        gain = full_row(at, mine_ref, theirs_ref, GAIN_MLP)
        unit, inverse = normalise(x1)
        grad = dh_ref[...]
        dy = dy_ref[...].astype(F32)
        dx = dy + normalise_back(grad, unit, inverse, gain)
        dx_ref[...] = dx
        da = dx.astype(BF16)
        rows = da.shape[0]
        da_ref[:rows, :] = da
        sums_ref[0:1, :] = jnp.sum(dy, axis=0, keepdims=True)
        sums_ref[1:2, :] = jnp.sum(grad * unit, axis=0, keepdims=True)
        sums_ref[2:3, :] = jnp.sum(grad, axis=0, keepdims=True)
        sums_ref[3:4, :] = jnp.sum(da.astype(F32), axis=0, keepdims=True)
        da_ref[rows:, :] = sums_ref[...].astype(BF16)
        for (begin, size), weight in zip(starts, (mo_ref, mn_ref, mf_ref)):
            dot_ref[pl.ds(begin, size), :] = mm_nt(weight[...], da).astype(BF16)


def expand_pieces(block, blocks, own, near_low, near_high, far_low, far_high):
    low = block < blocks // 2
    return (
        own[...],
        jnp.where(low, near_low[...], near_high[...]),
        jnp.where(low, far_low[...], far_high[...]),
    )


def hidden_specs(expand, contract, wide, block_of):
    own = expand[0].shape[1] // wide
    each = expand[1].shape[1] // wide
    own_contract, rest = contract
    _, shard, width = rest.shape
    held = wide // shard
    specs = [pl.BlockSpec((expand[0].shape[0], wide), lambda i, s: (0, block_of(i, s)))]
    for index in range(1, 5):
        first = (index - 1) % 2 * each
        specs.append(
            pl.BlockSpec(
                (expand[index].shape[0], wide),
                lambda i, s, first=first: (0, jnp.clip(block_of(i, s) - first, 0, each - 1)),
            )
        )
    blocks = own // 2
    specs.append(
        pl.BlockSpec((wide, width), lambda i, s: (jnp.clip(block_of(i, s) - s[0] * blocks, 0, blocks - 1), 0))
    )
    specs.append(
        pl.BlockSpec(
            (held, shard, width), lambda i, s: (jnp.clip(block_of(i, s) - (1 - s[0]) * blocks, 0, blocks - 1), 0, 0)
        )
    )
    return specs


def contract_block(block, blocks, at, own_ref, rest_ref):
    wide, width = own_ref.shape
    return jnp.where(block // (blocks // 2) == at, own_ref[...], rest_ref[...].reshape(wide, width))


def mlp(place, x1, normed, dy, mine, theirs, merge_w, expand, contract):
    rows, width = x1.shape
    wide = 512
    steps = expand[0].shape[1] // wide
    sums = -(-(SUM_EXPAND + steps * wide // width) // 16) * 16
    operands = (x1, normed, dy, mine, theirs, *merge_w)
    in_specs = [whole(member.shape) for member in operands]
    in_specs += hidden_specs(expand, contract, wide, lambda i, _: i)
    shapes = [
        ((rows, width), BF16),
        ((rows, width), F32),
        ((rows + sums, width), BF16),
        ((width, rows), BF16),
    ]
    return pl.pallas_call(
        mlp_body,
        grid_spec=pltpu.PrefetchScalarGridSpec(
            num_scalar_prefetch=1,
            grid=(steps,),
            in_specs=in_specs,
            out_specs=[whole(shape) for shape, _ in shapes],
            scratch_shapes=[
                pltpu.VMEM((rows, width), F32),
                pltpu.VMEM((rows, width), F32),
                pltpu.VMEM((steps, wide), F32),
                pltpu.VMEM((sums, width), F32),
            ],
        ),
        out_shape=[jax.ShapeDtypeStruct(shape, dtype) for shape, dtype in shapes],
        compiler_params=params(),
        cost_estimate=about(60),
        name="mlp",
    )(place, *operands, *expand, *contract)


def hidden_part(step, at, core, own_steps):
    part = own_steps // 2
    return jnp.where(
        step < part, at * own_steps + core * part + step, (1 - at) * own_steps + core * part + step - part
    )


def tail_rows(merge_rows):
    return -(-(merge_rows + 2) // 16) * 16


def weights_body(own_steps, place, *refs):
    h_refs, dy_refs = refs[:4], refs[4:8]
    mine_ref, theirs_ref, eo_ref, en0_ref, en1_ref, ef0_ref, ef1_ref, own_ref, rest_ref = refs[8:17]
    contract_ref, out_ref, bias_ref, h_ref, turned_ref, dy_ref, act_ref, du_ref = refs[17:]
    at, core = place[0], place[1]
    step = pl.program_id(0)
    part = own_steps // 2
    half = eo_ref.shape[0]
    starts = piece_starts(at, core, half)
    block = hidden_part(step, at, core, own_steps)
    wide = eo_ref.shape[1]
    chips, _, width = out_ref.shape
    expand_rows = half // chips
    first = tail_rows(half // 2 // chips)
    rows = h_refs[0].shape[0]
    some = 2 * rows

    @pl.when(step == 0)
    def _():
        read_expand_bias(at, mine_ref, theirs_ref, bias_ref)
        for index in range(4):
            here = slice(index * rows, (index + 1) * rows)
            h_ref[here, :] = h_refs[index][...]
            dy_ref[here, :] = dy_refs[index][...]
            mine = h_refs[index][:, pl.ds(pl.multiple_of(at * half, half), half)]
            turned_ref[:, here] = mine.astype(F32).T.astype(BF16)

    def work(forward):
        contract = contract_block(block, 2 * own_steps, at, own_ref, rest_ref)
        expand = expand_pieces(block, 2 * own_steps, eo_ref, en0_ref, en1_ref, ef0_ref, ef1_ref)
        for index in range(4 * rows // some):
            here = slice(index * some, (index + 1) * some)
            inner = bias_ref[pl.ds(block, 1), :]
            for (begin, size), weight in zip(starts, expand):
                inner = inner + mm(h_ref[here, pl.ds(begin, size)], weight)
            active, slope = gelu_pair(inner)
            if forward:
                act_ref[here, :] = active.astype(BF16)
            du_ref[here, :] = (mm_nt(dy_ref[here, :], contract) * slope).astype(BF16)
        return mm(turned_ref[...], du_ref[...]).astype(BF16)

    def store_expand(value, turn, column):
        begin = first + turn * expand_rows
        own = pl.ds(pl.multiple_of(begin, 16), expand_rows)
        for chip in range(chips):
            out_ref[chip, own, column * wide : (column + 1) * wide] = value[
                chip * expand_rows : (chip + 1) * expand_rows, :
            ]

    for now in range(part):

        @pl.when(step == now)
        def _():
            store_expand(work(True), at, now)
            contract_ref[now * wide : (now + 1) * wide, :] = mm_tn(act_ref[...], dy_ref[...]).astype(BF16)

        @pl.when(step == part + now)
        def _():
            store_expand(work(False), 1 - at, now)


def mlp_weights(place, chips, normed, dy, mine, theirs, expand, contract):
    rows, width = dy[0].shape
    wide = 512
    half = expand[0].shape[0]
    own_steps = expand[0].shape[1] // wide // 2
    part = own_steps // 2
    operands = (*normed, *dy, mine, theirs)
    in_specs = [whole(member.shape) for member in operands]
    in_specs += hidden_specs(expand, contract, wide, lambda i, s: hidden_part(i, s[0], s[1], own_steps))
    chunk = tail_rows(half // 2 // chips) + 2 * (half // chips)
    shapes = [(part * wide, width), (chips, chunk, width)]
    return pl.pallas_call(
        functools.partial(weights_body, own_steps),
        grid_spec=pltpu.PrefetchScalarGridSpec(
            num_scalar_prefetch=1,
            grid=(own_steps,),
            in_specs=in_specs,
            out_specs=[whole(shape) for shape in shapes],
            scratch_shapes=[
                pltpu.VMEM((2 * own_steps, wide), F32),
                pltpu.VMEM((4 * rows, width), BF16),
                pltpu.VMEM((half, 4 * rows), BF16),
                pltpu.VMEM((4 * rows, width), BF16),
                pltpu.VMEM((4 * rows, wide), BF16),
                pltpu.VMEM((4 * rows, wide), BF16),
            ],
        ),
        out_shape=[jax.ShapeDtypeStruct(shape, BF16) for shape in shapes],
        compiler_params=params(),
        cost_estimate=about(60),
        name="mlp_weights",
    )(place, *operands, *expand, *contract)


def merge_weights_body(hidden, place, *refs):
    o_refs, da_refs, out_ref = refs[:4], refs[4:8], refs[9]
    at, core = place[0], place[1]
    chips, tail, width = out_ref.shape
    half = width // 2
    tokens = o_refs[0].shape[0]
    total, sums = 0.0, 0.0
    for o_ref, da_ref in zip(o_refs, da_refs):
        total = total + mm_tn(o_ref[...], da_ref[:tokens, :])
        sums = sums + da_ref[tokens:, :].astype(F32)
    rows = total.shape[0] // chips
    for chip in range(chips):
        out_ref[chip, :rows, :] = total[chip * rows : (chip + 1) * rows, :].astype(BF16)
    out_ref[:, rows:, :] = jnp.zeros((chips, tail - rows, width), BF16)
    own = jnp.where(at == 0, sums[:, :half], sums[:, half:])
    own_hidden = jnp.where(at == 0, sums[SUM_EXPAND : SUM_EXPAND + hidden], sums[SUM_EXPAND + hidden : SUM_EXPAND + 2 * hidden])
    for row in range(2):
        vector = jnp.concatenate([own[2 * row : 2 * row + 1], own[2 * row + 1 : 2 * row + 2]], axis=1)
        vector = jnp.where(core == 0, vector, own_hidden[row : row + 1])
        out_ref[0, rows + row : rows + row + 1, :] = vector.astype(BF16)


def merge_weights(place, mixed, grad, hidden, chunks):
    rows, width = mixed[0].shape
    quarter = mixed[1].shape[1]
    chips = chunks.shape[0]
    tail = pl.BlockSpec((chips, tail_rows(quarter // chips), width), lambda i, _: (0, 0, 0))
    return pl.pallas_call(
        functools.partial(merge_weights_body, hidden // width // 2),
        grid_spec=pltpu.PrefetchScalarGridSpec(
            num_scalar_prefetch=1,
            grid=(1,),
            in_specs=[pl.BlockSpec((rows, quarter), lambda i, s: (0, 2 * s[0] + s[1]))]
            + [whole((rows, quarter))] * 3
            + [whole(grad[0].shape)] * 4
            + [pl.BlockSpec(memory_space=pl.ANY)],
            out_specs=tail,
        ),
        out_shape=jax.ShapeDtypeStruct(chunks.shape, BF16),
        input_output_aliases={9: 0},
        compiler_params=params(),
        cost_estimate=about(5),
        name="merge_weights",
    )(place, *mixed, *grad, chunks)


def spread_rest_body(begin, in_ref, expand_ref, merge_ref):
    expand_rows = expand_ref.shape[0]
    _, _, merge_rows, width = merge_ref.shape
    first = begin + tail_rows(merge_rows)
    for core in range(2):
        merge_ref[core, 0] = in_ref[core, begin : begin + merge_rows, :].astype(F32)
        for part in range(2):
            row = first + part * expand_rows
            column = (2 * part + core) * width
            expand_ref[:, column : column + width] = in_ref[core, row : row + expand_rows, :].astype(F32)


def spread_rest(gathered, begin, expand_shape, merge_shape):
    devices, rows, width = gathered.shape
    chips = devices // 2
    expand_rows = expand_shape[0] // chips
    chunked = (2, chips, merge_shape[0] // devices, width)
    expand, merged = pl.pallas_call(
        functools.partial(spread_rest_body, begin),
        grid=(chips,),
        in_specs=[pl.BlockSpec((2, rows, width), lambda i: (i, 0, 0))],
        out_specs=[
            pl.BlockSpec((expand_rows, expand_shape[1]), lambda i: (i, 0)),
            pl.BlockSpec((2, 1) + chunked[2:], lambda i: (0, i, 0, 0)),
        ],
        out_shape=[jax.ShapeDtypeStruct(expand_shape, F32), jax.ShapeDtypeStruct(chunked, F32)],
        compiler_params=params(),
        cost_estimate=about(7),
        name="spread_rest",
    )(gathered)
    return expand, merged.reshape(merge_shape)


def spread_contract_body(place, *refs):
    out_ref = refs[4]
    phase = 2 * pl.program_id(0) + pl.program_id(1)
    for index in range(4):

        @pl.when(phase == index)
        def _():
            out_ref[...] = refs[index][...].reshape(out_ref.shape).astype(F32)


def spread_contract(place, stacks, shape):
    ring, rows, width = stacks[0].shape

    def source(index):
        def block(i, j, k, s):
            phase = 2 * i + j
            slot = jnp.where(phase < index, 0, jnp.where(phase > index, ring - 1, k))
            return ((s[3] - slot + ring) % ring, 0, 0)

        return pl.BlockSpec((1, rows, width), block)

    def target(i, j, k, s):
        return (((i + s[1]) % 2 * 2 + (j + s[2]) % 2) * ring + k, 0)

    return pl.pallas_call(
        spread_contract_body,
        grid_spec=pltpu.PrefetchScalarGridSpec(
            num_scalar_prefetch=1,
            grid=(2, 2, ring),
            in_specs=[source(index) for index in range(4)],
            out_specs=pl.BlockSpec((rows, width), target),
        ),
        out_shape=jax.ShapeDtypeStruct(shape, F32),
        compiler_params=params(),
        cost_estimate=about(5),
        name="spread_contract",
    )(place, *stacks)


def heads_body(dp_ref, h_ref, out_ref):
    @pl.when(pl.program_id(0) == 0)
    def _():
        out_ref[...] = jnp.zeros_like(out_ref)

    _, parts, head, lanes = dp_ref.shape
    out_ref[...] += mm(dp_ref[0].reshape(parts * head, lanes), h_ref[0])


def heads_gradient(dp, normed):
    sources, parts, head, lanes = dp.shape
    width = normed.shape[2]
    return pl.pallas_call(
        heads_body,
        grid=(sources,),
        in_specs=[
            pl.BlockSpec((1, parts, head, lanes), lambda i: (i, 0, 0, 0)),
            pl.BlockSpec((1, lanes, width), lambda i: (i, 0, 0)),
        ],
        out_specs=whole((parts * head, width)),
        out_shape=jax.ShapeDtypeStruct((parts * head, width), F32),
        compiler_params=params(),
        cost_estimate=about(11),
        name="heads_gradient",
    )(dp, normed)


def spread_body(in_ref, out_ref):
    heads, rows, width = in_ref.shape
    half = width // 2
    some = 4
    parts = 2 * rows // HEAD
    for part in range(parts):
        for first in range(0, heads, some):
            turned = []
            for head in range(first, first + some):
                for row in range(part * HEAD, (part + 1) * HEAD, 32):
                    side = row // rows
                    here = row - side * rows
                    turned.append(in_ref[head, here : here + 32, side * half : (side + 1) * half])
            piece = jnp.concatenate([member.astype(F32) for member in turned], axis=0)
            column = (part * heads + first) * HEAD
            out_ref[:, column : column + some * HEAD] = piece.T


def spread_heads(gathered, rows, shape):
    heads, _, width = gathered.shape
    return pl.pallas_call(
        spread_body,
        grid=(1,),
        in_specs=[pl.BlockSpec((heads, rows, width), lambda i: (0, 0, 0))],
        out_specs=whole(shape),
        out_shape=jax.ShapeDtypeStruct(shape, F32),
        compiler_params=params(),
        cost_estimate=about(6),
        name="spread_heads",
    )(gathered)


def back_body(
    place, dp_ref, x_ref, dx_ref, mine_ref, theirs_ref, own_ref, qn_ref, qf_ref, rn_ref, rf_ref, out_ref, sums_ref, dh_ref
):
    at, core = place[0], place[1]
    part = pl.program_id(0)
    starts = piece_starts(at, core, own_ref.shape[0])
    heads, _, head, rows = dp_ref.shape

    @pl.when(part == 0)
    def _():
        dh_ref[...] = jnp.zeros_like(dh_ref)
        sums_ref[...] = jnp.zeros_like(sums_ref)

    def work(weights):
        grad = dp_ref[...].reshape(heads * head, rows)
        for (begin, size), weight in zip(starts, weights):
            dh_ref[pl.ds(begin, size), :] += mm(weight[...], grad)
        return mm_nt(jnp.ones((8, rows), BF16), grad)[0:1, :]

    @pl.when(part == 0)
    def _():
        sums_ref[2:3, :] = work((own_ref, qn_ref, qf_ref))

    @pl.when(part == 1)
    def _():
        work((own_ref, rn_ref, rf_ref))

    @pl.when(part == 2)
    def _():
        sums_ref[3:4, :] = work((own_ref, rn_ref, rf_ref))
        dh = dh_ref[...].T
        unit, inverse = normalise(x_ref[...].astype(F32))
        gain = full_row(at, mine_ref, theirs_ref, GAIN_ATTN)
        out_ref[...] = dx_ref[...] + normalise_back(dh, unit, inverse, gain)
        sums_ref[0:1, :] = jnp.sum(dh * unit, axis=0, keepdims=True)
        sums_ref[1:2, :] = jnp.sum(dh, axis=0, keepdims=True)


def back(place, dp, x, dx, mine, theirs, own, query_w, rest_w):
    rows, width = x.shape
    heads, parts, head, _ = dp.shape
    vectors = (x, dx, mine, theirs)
    return pl.pallas_call(
        back_body,
        grid_spec=pltpu.PrefetchScalarGridSpec(
            num_scalar_prefetch=1,
            grid=(parts,),
            in_specs=[pl.BlockSpec((heads, 1, head, rows), lambda t, _: (0, t, 0, 0))]
            + [whole(member.shape) for member in vectors]
            + [pl.BlockSpec((own.shape[0], width), lambda t, _: (0, t))]
            + [whole(member.shape) for member in query_w]
            + [pl.BlockSpec((member.shape[0], width), lambda t, _: (0, jnp.maximum(t - 1, 0))) for member in rest_w],
            out_specs=[whole((rows, width)), whole((8, width))],
            scratch_shapes=[pltpu.VMEM((width, rows), F32)],
        ),
        out_shape=[
            jax.ShapeDtypeStruct((rows, width), F32),
            jax.ShapeDtypeStruct((8, width), F32),
        ],
        compiler_params=params(),
        cost_estimate=about(8),
        name="back",
    )(place, dp, *vectors, own, *query_w, *rest_w)


def after(value, *others):
    return lax.optimization_barrier((value,) + others)[0]


def per_device(
    mesh_sizes, tokens_in, gain_attn, shift_attn, w_heads, bias_query, bias_value, w_merge, bias_merge, gain_mlp, shift_mlp,
    w_expand, bias_expand, w_contract, bias_contract, cotangent,
):
    nctx = mesh_sizes[0]
    seqs, tokens, width = tokens_in.shape
    rows = seqs * tokens
    half = width // 2
    heads = width // HEAD
    hidden = w_expand.shape[1]
    pairs = seqs * heads
    same = max(1, nctx // pairs)
    per = max(1, pairs // nctx)
    groups = seqs // per
    ctx = lax.axis_index("ctx")
    at = lax.axis_index("fsdp")
    core = ctx % 2
    line, ring_at, ring = ctx // 2 % 2, ctx // 4, nctx // 4
    place = jnp.stack([at, core, line, ring_at, ctx]).astype(jnp.int32)

    def over_x(value):
        return lax.ppermute(value, "fsdp", [(0, 1), (1, 0)])

    def over_core(value):
        return lax.ppermute(value, "ctx", [(i, i ^ 1) for i in range(nctx)])

    def over_line(value):
        return lax.ppermute(value, "ctx", [(i, i ^ 2) for i in range(nctx)])

    def on_ring(value, by):
        return lax.ppermute(value, "ctx", [(i, (i + 4 * by) % nctx) for i in range(nctx)])

    def over_both(value):
        size = mesh_sizes[1]
        swap = [(i * size + j, (i ^ 1) * size + 1 - j) for i in range(nctx) for j in range(size)]
        return lax.ppermute(value, ("ctx", "fsdp"), swap)

    def exchange(value):
        return lax.all_to_all(value, "ctx", 0, 0)

    def to_send(value):
        lead = value.shape[1:-1]
        value = value.reshape((heads,) + lead + (groups, per * tokens))
        value = jnp.moveaxis(value, -2, 1).reshape((nctx // same,) + lead + (per * tokens,))
        return value if same == 1 else jnp.repeat(value, same, axis=0)

    def received(value):
        value = value[::same]
        lead = value.shape[1:-1]
        value = value.reshape((heads, groups) + lead + (per * tokens,))
        return jnp.moveaxis(value, 1, -2).reshape((heads,) + lead + (rows,))

    def quarter_of(weight, first, count):
        size = weight.shape[0] // 2
        return lax.dynamic_slice(weight, (core * size, first), (size, count))

    def halves(value):
        mine = lax.dynamic_index_in_dim(value, at, 0, keepdims=False)
        return mine + over_x(lax.dynamic_index_in_dim(value, 1 - at, 0, keepdims=False))

    vectors = (gain_attn, shift_attn, bias_query, bias_value, bias_merge, gain_mlp, shift_mlp, bias_contract, bias_expand)
    shard = w_contract.shape[0] // nctx
    first, mine = parcel(place, w_heads, w_contract, vectors, shard)
    first_near = over_x(first)
    rest_piece, first_near = lax.optimization_barrier((quarter_of(w_heads, width, 2 * width), first_near))
    query_near = first_near[: half // 2]
    theirs = first_near[half // 2 + shard :]
    contract = (w_contract, lax.all_gather(first_near[half // 2 : half // 2 + shard], "ctx", axis=0))
    query_w = (query_near, over_core(query_near))
    rest_near = over_x(rest_piece)
    merge_near = over_x(after(quarter_of(w_merge, 0, width), rest_near))
    expand_low = over_x(after(quarter_of(w_expand, 0, hidden // 2), rest_near))
    expand_high = over_x(after(quarter_of(w_expand, hidden // 2, hidden // 2), expand_low))

    x = tokens_in.reshape(rows, width)
    dy = cotangent.reshape(rows, width)
    dy_x = over_x(after(dy, expand_high))

    query_rows, normed = front_query(place, x, mine, theirs, w_heads, *query_w)
    query = exchange(to_send(query_rows))
    rest_w = (rest_near, over_core(after(rest_near, query)))
    kv = exchange(to_send(front_rest(place, after(normed, query), mine, theirs, w_heads, *rest_w)))
    normed_all = lax.all_gather(after(normed, kv), "ctx", axis=0, tiled=False)
    mixed_b, mixed_f, lse = attend(query, kv, per)
    merge_w = (w_merge, merge_near, over_core(after(merge_near, kv)))
    expand_w = (
        w_expand, expand_low, expand_high, over_core(after(expand_low, kv)), over_core(after(expand_high, lse)),
    )
    mixed = received(exchange(mixed_b)).reshape(width, rows)
    x1, normed_two, mixed_rows = merge(place, x, mixed, mine, theirs, merge_w)

    def of_four(value, there):
        return value, there, over_core(value), over_core(there)

    def all_four(value):
        return value, over_x(value), over_core(value), over_both(value)

    def quarter_at(value, at, core):
        return lax.dynamic_slice_in_dim(value, (2 * at + core) * (width // 4), width // 4, 1)

    dy_four = of_four(after(dy, mixed), after(dy_x, mixed))
    normed_four = all_four(normed_two)
    block_out, dx1, da, grad_mixed = mlp(
        place, x1, normed_two, dy, mine, theirs, merge_w, expand_w, contract
    )
    grad_out = exchange(to_send(grad_mixed.reshape(heads, HEAD, rows)))

    late = after(mixed_rows, da)
    mixed_four = (
        mixed_rows,
        over_x(quarter_at(late, 1 - at, core)),
        over_core(quarter_at(late, at, 1 - core)),
        over_both(quarter_at(late, 1 - at, 1 - core)),
    )
    grads_four = all_four(da)
    grad_contract, chunks = mlp_weights(
        after(place, da), nctx // 2, normed_four, dy_four, mine, theirs, expand_w, contract
    )
    grad_contract = grad_contract.reshape(2, ring, -1, width)
    contract_line = over_line(lax.dynamic_index_in_dim(grad_contract, 1 - line, 0, keepdims=False))
    mixed_four, grads_four, _, chunks = lax.optimization_barrier((mixed_four, grads_four, grad_out, chunks))
    chunks = merge_weights(place, mixed_four, grads_four, hidden, chunks)
    chips = [[2 * chip + one for chip in range(nctx // 2)] for one in range(2)]
    reduced = lax.psum_scatter(chunks, "ctx", scatter_dimension=0, axis_index_groups=chips)

    dqkv = attend_back(query, kv, after(grad_out, chunks), mixed_f, lse, per)
    dp = received(exchange(dqkv))

    contract_half = lax.dynamic_index_in_dim(grad_contract, line, 0, keepdims=False).astype(F32)
    contract_half = (contract_half + after(contract_line, dqkv).astype(F32)).astype(BF16)

    def chunk_of(by):
        return lax.dynamic_index_in_dim(contract_half, (ring_at + by) % ring, 0, keepdims=False)

    contract_parts = [on_ring(chunk_of(by), by) for by in range(1, ring)]

    if groups > 1:
        normed_all = lax.dynamic_slice_in_dim(normed_all, (ctx // same % groups) * tokens * per, tokens * per, 1)
    grad_heads = heads_gradient(after(dqkv, contract_half), normed_all)

    contract_sum = chunk_of(0).astype(F32)
    for part in lax.optimization_barrier((contract_parts, grad_heads))[0]:
        contract_sum = contract_sum + part.astype(F32)
    contract_sum = contract_sum.astype(BF16)
    own_line = jnp.stack([contract_sum] + [on_ring(contract_sum, by) for by in range(1, ring)])
    other_line = over_line(own_line)
    stacks = (own_line, other_line, over_core(own_line), over_core(other_line))
    contract_sum = spread_contract(place, stacks, w_contract.shape)
    if groups > 1:
        members = [
            [first + one + same * group for group in range(groups)]
            for first in range(0, nctx, groups * same)
            for one in range(same)
        ]
        grad_heads = lax.psum(grad_heads, "ctx", axis_index_groups=members)
    kept = lax.dynamic_slice_in_dim(grad_heads, at * half, half, 1)
    sent = lax.dynamic_slice_in_dim(grad_heads, (1 - at) * half, half, 1)
    kept = (kept + over_x(sent.astype(BF16)).astype(F32)).astype(BF16)
    if groups * same > 1:
        share = kept.shape[0] // (groups * same)
        kept = lax.dynamic_slice_in_dim(kept, ctx % (groups * same) * share, share, 0)
    rows_here = kept.shape[0] // 2
    kept = jnp.concatenate([kept[:rows_here], kept[rows_here:]], axis=1)
    kept = jnp.pad(kept, ((0, -rows_here % 16), (0, 0)))
    spread = lax.all_gather(jnp.concatenate([kept, after(reduced, own_line)]), "ctx", axis=0, tiled=False)
    begin = kept.shape[0]
    expand_sum, merge_sum = spread_rest(spread, begin, w_expand.shape, w_merge.shape)
    by_head = spread
    if groups * same > 1:
        by_head = spread[:, :rows_here].reshape(nctx, rows_here, 2, half)
        by_head = jnp.swapaxes(by_head, 1, 2).reshape(heads, 2, -1, half)
        by_head = jnp.swapaxes(by_head, 1, 2).reshape(heads, -1, width)
    heads_sum = spread_heads(by_head, 3 * HEAD // 2, w_heads.shape)
    first = begin + half // nctx
    vectors = spread[:2, first : first + 2].astype(F32)

    grad_tokens, sums_attn = back(place, after(dp, own_line), x, dx1, mine, theirs, w_heads, query_w, rest_w)
    last = halves(sums_attn[:4].reshape(4, 2, half).swapaxes(0, 1))
    last = jnp.sum(exchange(jnp.broadcast_to(last, (nctx,) + last.shape)), axis=0)
    return (
        block_out.reshape(tokens_in.shape),
        grad_tokens.reshape(tokens_in.shape),
        last[0],
        last[1],
        heads_sum,
        last[2],
        last[3],
        merge_sum,
        vectors[0, 1, half:],
        vectors[0, 0, half:],
        vectors[0, 1, :half],
        expand_sum,
        vectors[1].reshape(-1),
        contract_sum,
        vectors[0, 0, :half],
    )


def solution(mesh):
    rows, vec, mat = P("fsdp", "ctx", None), P("fsdp"), P("fsdp", None)
    return jax.shard_map(
        functools.partial(per_device, (mesh.shape["ctx"], mesh.shape["fsdp"])),
        mesh=mesh,
        in_specs=(rows, vec, vec, mat, vec, vec, mat, vec, vec, vec, mat, vec, mat, vec, rows),
        out_specs=(rows, rows, vec, vec, mat, vec, vec, mat, vec, vec, vec, mat, vec, mat, vec),
        check_vma=False,
    )
```

```python
import functools
import math

import jax
import jax.numpy as jnp
from jax import lax
from jax.experimental import pallas as pl
from jax.experimental.pallas import tpu as pltpu
from jax.sharding import PartitionSpec as P

HEAD = 64
EPS = 1e-05
LOWEST = -1e30
GELU_A = math.sqrt(2.0 / math.pi)
GELU_B = 0.044715
F32 = jnp.float32
BF16 = jnp.bfloat16
VMEM_BYTES = 62 * 1024 * 1024
GAIN_ATTN, SHIFT_ATTN, BIAS_QUERY, BIAS_VALUE = 0, 1, 2, 3
BIAS_MERGE, GAIN_MLP, SHIFT_MLP, BIAS_CONTRACT = 4, 5, 6, 7
BIAS_EXPAND = 8
SUM_EXPAND = 4


def mm(left, right):
    return jnp.dot(left, right, preferred_element_type=F32)


def mm_nt(left, right):
    return lax.dot_general(left, right, (((1,), (1,)), ((), ())), preferred_element_type=F32)


def mm_tn(left, right):
    return lax.dot_general(left, right, (((0,), (0,)), ((), ())), preferred_element_type=F32)


def params(**extra):
    return pltpu.CompilerParams(vmem_limit_bytes=VMEM_BYTES, **extra)


def about(us):
    return pl.CostEstimate(flops=int(us * 1.15e9), bytes_accessed=0, transcendentals=0)


def whole(shape):
    return pl.BlockSpec(shape, lambda *_: (0,) * len(shape))


def full_row(at, mine_ref, theirs_ref, row):
    half = mine_ref.shape[1] // 2
    line, lanes = row // 2, slice(row % 2 * half, (row % 2 + 1) * half)
    mine = mine_ref[line : line + 1, lanes].astype(F32)
    theirs = theirs_ref[line : line + 1, lanes].astype(F32)
    low = jnp.where(at == 0, mine, theirs)
    high = jnp.where(at == 0, theirs, mine)
    return jnp.concatenate([low, high], axis=1)


def normalise(rows):
    mean = jnp.mean(rows, axis=-1, keepdims=True)
    centered = rows - mean
    variance = jnp.mean(centered * centered, axis=-1, keepdims=True)
    inverse = lax.rsqrt(variance + EPS)
    return centered * inverse, inverse


def normalise_back(grad, unit, inverse, gain):
    scaled = grad * gain
    mean = jnp.mean(scaled, axis=-1, keepdims=True)
    along = jnp.mean(scaled * unit, axis=-1, keepdims=True)
    return inverse * (scaled - mean - unit * along)


def piece_starts(at, core, half):
    other = (1 - at) * half
    quarter = half // 2
    return (
        (pl.multiple_of(at * half, quarter), half),
        (pl.multiple_of(other + core * quarter, quarter), quarter),
        (pl.multiple_of(other + (1 - core) * quarter, quarter), quarter),
    )


def parcel_body(place, heads_ref, contract_ref, *refs):
    vectors, first_ref, mine_ref = refs[:9], refs[9], refs[10]
    quarter, shard = heads_ref.shape[0], contract_ref.shape[0]
    first_ref[:quarter, :] = heads_ref[...]
    first_ref[quarter : quarter + shard, :] = contract_ref[...]
    mine_ref[...] = jnp.zeros_like(mine_ref)
    at = 0
    width = mine_ref.shape[1]
    for vector in vectors:
        value = vector[...].astype(F32)
        size = min(value.shape[0], width)
        for begin in range(0, value.shape[0], size):
            line, lane = at // width, at % width
            piece = value[begin : begin + size].reshape(1, size)
            mine_ref[line : line + 1, lane : lane + size] = piece.astype(BF16)
            at += size
    first_ref[quarter + shard :, :] = mine_ref[...]


def parcel(place, w_heads, w_contract, vectors, shard):
    quarter, width = w_heads.shape[0] // 2, w_contract.shape[1]
    lines = -(-sum(vector.size for vector in vectors) // (16 * width)) * 16
    shapes = [(quarter + shard + lines, width), (lines, width)]
    return pl.pallas_call(
        parcel_body,
        grid_spec=pltpu.PrefetchScalarGridSpec(
            num_scalar_prefetch=1,
            grid=(1,),
            in_specs=[
                pl.BlockSpec((quarter, width), lambda i, s: (s[1], 0)),
                pl.BlockSpec((shard, width), lambda i, s: (s[4], 0)),
            ]
            + [whole(vector.shape) for vector in vectors],
            out_specs=[whole(shape) for shape in shapes],
        ),
        out_shape=[jax.ShapeDtypeStruct(shape, BF16) for shape in shapes],
        compiler_params=params(),
        cost_estimate=about(1),
        name="parcel",
    )(place, w_heads, w_contract, *vectors)


def project(at, core, normed, bias, own, near, far, out_ref, part):
    total = bias
    for (begin, size), weight in zip(piece_starts(at, core, own.shape[0]), (own, near, far)):
        total = total + mm(normed[:, pl.ds(begin, size)], weight[...])
    turned = total.T.astype(BF16)
    for head in range(turned.shape[0] // HEAD):
        piece = turned[head * HEAD : (head + 1) * HEAD, :]
        if part is None:
            out_ref[head] = piece
        else:
            out_ref[head, part] = piece


def front_query_body(place, x_ref, mine_ref, theirs_ref, own, near, far, out_ref, h_ref, bias_ref):
    at, core = place[0], place[1]
    step = pl.program_id(0)
    wide = own.shape[1]

    @pl.when(step == 0)
    def _():
        unit, _ = normalise(x_ref[...].astype(F32))
        gain = full_row(at, mine_ref, theirs_ref, GAIN_ATTN)
        shift = full_row(at, mine_ref, theirs_ref, SHIFT_ATTN)
        h_ref[...] = (unit * gain + shift).astype(BF16)
        bias_ref[0:1, :] = full_row(at, mine_ref, theirs_ref, BIAS_QUERY)

    columns = pl.ds(pl.multiple_of(step * wide, wide), wide)
    project(at, core, h_ref, bias_ref[0:1, columns], own, near, far, out_ref, None)


def front_query(place, x, mine, theirs, own, near, far):
    rows, width = x.shape
    heads = width // HEAD
    wide = 256
    return pl.pallas_call(
        front_query_body,
        grid_spec=pltpu.PrefetchScalarGridSpec(
            num_scalar_prefetch=1,
            grid=(width // wide,),
            in_specs=[whole(x.shape), whole(mine.shape), whole(theirs.shape)]
            + [pl.BlockSpec((member.shape[0], wide), lambda i, _: (0, i)) for member in (own, near, far)],
            out_specs=[
                pl.BlockSpec((wide // HEAD, HEAD, rows), lambda i, _: (i, 0, 0)),
                whole((rows, width)),
            ],
            scratch_shapes=[pltpu.VMEM((8, width), F32)],
        ),
        out_shape=[
            jax.ShapeDtypeStruct((heads, HEAD, rows), BF16),
            jax.ShapeDtypeStruct((rows, width), BF16),
        ],
        compiler_params=params(),
        cost_estimate=about(1),
        name="front_query",
    )(place, x, mine, theirs, own, near, far)


def front_rest_body(place, h_ref, mine_ref, theirs_ref, *rest):
    weights, (out_ref, bias_ref) = rest[:6], rest[6:]
    at, core = place[0], place[1]
    step = pl.program_id(0)
    wide = weights[0].shape[1]

    @pl.when(step == 0)
    def _():
        bias_ref[0:1, :] = jnp.zeros_like(bias_ref[0:1, :])
        bias_ref[1:2, :] = full_row(at, mine_ref, theirs_ref, BIAS_VALUE)

    columns = pl.ds(pl.multiple_of(step * wide, wide), wide)
    for part in range(2):
        bias = bias_ref[part : part + 1, columns]
        project(at, core, h_ref, bias, *weights[3 * part : 3 * part + 3], out_ref, part)


def front_rest(place, normed, mine, theirs, own, near, far):
    rows, width = normed.shape
    heads = width // HEAD
    wide = 256
    steps = width // wide
    specs = []
    for part in range(2):
        for member, skip in ((own, 1), (near, 0), (far, 0)):
            first = (part + skip) * steps
            specs.append(pl.BlockSpec((member.shape[0], wide), lambda i, _, first=first: (0, first + i)))
    return pl.pallas_call(
        front_rest_body,
        grid_spec=pltpu.PrefetchScalarGridSpec(
            num_scalar_prefetch=1,
            grid=(steps,),
            in_specs=[whole(normed.shape), whole(mine.shape), whole(theirs.shape)] + specs,
            out_specs=pl.BlockSpec((wide // HEAD, 2, HEAD, rows), lambda i, _: (i, 0, 0, 0)),
            scratch_shapes=[pltpu.VMEM((8, width), F32)],
        ),
        out_shape=jax.ShapeDtypeStruct((heads, 2, HEAD, rows), BF16),
        compiler_params=params(),
        cost_estimate=about(1),
        name="front_rest",
    )(place, normed, mine, theirs, *([own, near, far] * 2))


def lay_out(source, target, per, tokens, block, turned=False, scale=None):
    for src in range(source.shape[0]):
        for pair in range(per):
            piece = source[src, :, pair * tokens : (pair + 1) * tokens]
            if scale is not None:
                piece = piece * jnp.asarray(scale, BF16)
            begin = src * tokens
            if turned:
                target[pair, begin : begin + tokens, :] = piece.astype(F32).T.astype(BF16)
            else:
                inner = begin % block
                target[pair, begin // block, :, inner : inner + tokens] = piece


def allowed_at(first_key, first_query, keys, queries):
    key_at = first_key + lax.broadcasted_iota(jnp.int32, (keys, queries), 0)
    query_at = first_query + lax.broadcasted_iota(jnp.int32, (keys, queries), 1)
    return key_at <= query_at


def attend_body(per, tokens, block, chunk, query_ref, kv_ref, out_ref, outf_ref, lse_ref, q_ref, k_ref, v_ref):
    step = pl.program_id(0)

    @pl.when(step == 0)
    def _():
        lay_out(query_ref, q_ref, per, tokens, block, scale=HEAD**-0.5)
        lay_out(kv_ref.at[:, 0], k_ref, per, tokens, chunk, turned=True)
        lay_out(kv_ref.at[:, 1], v_ref, per, tokens, chunk)

    queries = [q_ref[pair, step] for pair in range(per)]

    def scores(pair, index):
        keys = k_ref[pair, pl.ds(pl.multiple_of(index * chunk, chunk), chunk), :]
        return mm(keys, queries[pair])

    last = (step * block) // chunk
    allowed = allowed_at(last * chunk, step * block, chunk, block)
    carried = []
    for pair in range(per):
        masked = jnp.where(allowed, scores(pair, last), LOWEST)
        top = jnp.max(masked, axis=0, keepdims=True)
        weights = jnp.exp(masked - top)
        total = jnp.sum(weights, axis=0, keepdims=True)
        mixed = mm(v_ref[pair, last], weights.astype(BF16))
        carried += [top, total, mixed]

    def one(index, state):
        fresh = []
        for pair in range(per):
            top, total, mixed = state[3 * pair : 3 * pair + 3]
            here = scores(pair, index)
            new_top = jnp.maximum(top, jnp.max(here, axis=0, keepdims=True))
            weights = jnp.exp(here - new_top)
            factor = jnp.exp(top - new_top)
            total = total * factor + jnp.sum(weights, axis=0, keepdims=True)
            mixed = mixed * factor + mm(v_ref[pair, index], weights.astype(BF16))
            fresh += [new_top, total, mixed]
        return tuple(fresh)

    final = lax.fori_loop(0, last, one, tuple(carried))
    for pair in range(per):
        top, total, mixed = final[3 * pair : 3 * pair + 3]
        mixed = mixed / total
        lse_ref[0, pair : pair + 1, :] = top + jnp.log(total)
        for dst in range(block // tokens):
            piece = mixed[:, dst * tokens : (dst + 1) * tokens]
            lanes = slice(pair * tokens, (pair + 1) * tokens)
            outf_ref[dst, :, lanes] = piece
            out_ref[dst, :, lanes] = piece.astype(BF16)


def attend(query, kv, per, block=512, chunk=512):
    sources, _, lanes = query.shape
    tokens = lanes // per
    length = sources * tokens
    steps = length // block
    here = pl.BlockSpec((block // tokens, HEAD, lanes), lambda i: (i, 0, 0))
    return pl.pallas_call(
        functools.partial(attend_body, per, tokens, block, chunk),
        grid=(steps,),
        in_specs=[whole(query.shape), whole(kv.shape)],
        out_specs=[here, here, pl.BlockSpec((1, 8, block), lambda i: (i, 0, 0))],
        out_shape=[
            jax.ShapeDtypeStruct((sources, HEAD, lanes), BF16),
            jax.ShapeDtypeStruct((sources, HEAD, lanes), F32),
            jax.ShapeDtypeStruct((steps, 8, block), F32),
        ],
        scratch_shapes=[
            pltpu.VMEM((per, steps, HEAD, block), BF16),
            pltpu.VMEM((per, length, HEAD), BF16),
            pltpu.VMEM((per, length // chunk, HEAD, chunk), BF16),
        ],
        compiler_params=params(),
        cost_estimate=about(1),
        name="attend",
    )(query, kv)


def attend_back_body(
    per, tokens, block, chunk, query_ref, kv_ref, go_ref, of_ref, lse_ref, out_ref, qt_ref, q_ref, kt_ref, k_ref, v_ref,
    dk_ref, dv_ref,
):
    sources = query_ref.shape[0]
    step = pl.program_id(0)

    @pl.when(step == 0)
    def _():
        lay_out(query_ref, qt_ref, per, tokens, block, scale=HEAD**-0.5)
        lay_out(query_ref, q_ref, per, tokens, block, turned=True, scale=HEAD**-0.5)
        lay_out(kv_ref.at[:, 0], kt_ref, per, tokens, chunk, scale=HEAD**-0.5)
        lay_out(kv_ref.at[:, 0], k_ref, per, tokens, chunk, turned=True)
        lay_out(kv_ref.at[:, 1], v_ref, per, tokens, chunk, turned=True)
        dk_ref[...] = jnp.zeros_like(dk_ref)
        dv_ref[...] = jnp.zeros_like(dv_ref)

    inner = block // tokens
    grads, deltas, lses, turned_grads, turned_queries, queries = [], [], [], [], [], []
    for pair in range(per):
        lanes = slice(pair * tokens, (pair + 1) * tokens)
        grad = jnp.concatenate([go_ref[dst, :, lanes] for dst in range(inner)], axis=1)
        mixed = jnp.concatenate([of_ref[dst, :, lanes] for dst in range(inner)], axis=1)
        wide = grad.astype(F32)
        grads.append(grad)
        deltas.append(jnp.sum(wide * mixed, axis=0, keepdims=True))
        turned_grads.append(wide.T.astype(BF16))
        lses.append(lse_ref[0, pair : pair + 1, :])
        queries.append(qt_ref[pair, step])
        turned_queries.append(q_ref[pair, pl.ds(pl.multiple_of(step * block, block), block), :])

    def one(index, state, allowed):
        rows = pl.ds(pl.multiple_of(index * chunk, chunk), chunk)
        fresh = []
        for pair in range(per):
            weights = jnp.exp(mm(k_ref[pair, rows, :], queries[pair]) - lses[pair])
            if allowed is not None:
                weights = jnp.where(allowed, weights, 0.0)
            back = mm(v_ref[pair, rows, :], grads[pair])
            dscore = (weights * (back - deltas[pair])).astype(BF16)
            dv_ref[pair, rows, :] += mm(weights.astype(BF16), turned_grads[pair])
            dk_ref[pair, rows, :] += mm(dscore, turned_queries[pair])
            fresh.append(state[pair] + mm(kt_ref[pair, index], dscore))
        return tuple(fresh)

    last = (step * block) // chunk
    start = tuple(jnp.zeros((HEAD, block), F32) for _ in range(per))
    state = lax.fori_loop(0, last, lambda i, s: one(i, s, None), start)
    state = one(last, state, allowed_at(last * chunk, step * block, chunk, block))
    for pair in range(per):
        lanes = slice(pair * tokens, (pair + 1) * tokens)
        for dst in range(inner):
            out_ref[step * inner + dst, 0, :, lanes] = state[pair][
                :, dst * tokens : (dst + 1) * tokens
            ].astype(BF16)

    @pl.when(step == pl.num_programs(0) - 1)
    def _():
        for pair in range(per):
            lanes = slice(pair * tokens, (pair + 1) * tokens)
            for src in range(sources):
                rows = slice(src * tokens, (src + 1) * tokens)
                out_ref[src, 1, :, lanes] = dk_ref[pair, rows, :].T.astype(BF16)
                out_ref[src, 2, :, lanes] = dv_ref[pair, rows, :].T.astype(BF16)


def attend_back(query, kv, grad, mixed, lse, per, chunk=512):
    sources, _, lanes = query.shape
    tokens = lanes // per
    length = sources * tokens
    steps, _, block = lse.shape
    here = pl.BlockSpec((block // tokens, HEAD, lanes), lambda i: (i, 0, 0))
    shape = (sources, 3, HEAD, lanes)
    return pl.pallas_call(
        functools.partial(attend_back_body, per, tokens, block, chunk),
        grid=(steps,),
        in_specs=[
            whole(query.shape), whole(kv.shape), here, here, pl.BlockSpec((1, 8, block), lambda i: (i, 0, 0)),
        ],
        out_specs=whole(shape),
        out_shape=jax.ShapeDtypeStruct(shape, BF16),
        scratch_shapes=[
            pltpu.VMEM((per, steps, HEAD, block), BF16),
            pltpu.VMEM((per, length, HEAD), BF16),
            pltpu.VMEM((per, length // chunk, HEAD, chunk), BF16),
            pltpu.VMEM((per, length, HEAD), BF16),
            pltpu.VMEM((per, length, HEAD), BF16),
            pltpu.VMEM((per, length, HEAD), F32),
            pltpu.VMEM((per, length, HEAD), F32),
        ],
        compiler_params=params(),
        cost_estimate=about(1),
        name="attend_back",
    )(query, kv, grad, mixed, lse)


def merge_body(place, x_ref, ot_ref, mine_ref, theirs_ref, mo_ref, mn_ref, mf_ref, x1_ref, h_ref, o_ref):
    at, core = place[0], place[1]
    starts = piece_starts(at, core, mo_ref.shape[0])
    o_ref[...] = ot_ref[...].astype(F32).T.astype(BF16)
    merged = full_row(at, mine_ref, theirs_ref, BIAS_MERGE)
    for (begin, size), weight in zip(starts, (mo_ref, mn_ref, mf_ref)):
        merged = merged + mm(o_ref[:, pl.ds(begin, size)], weight[...])
    x1 = x_ref[...].astype(F32) + merged
    x1_ref[...] = x1
    unit, _ = normalise(x1)
    gain = full_row(at, mine_ref, theirs_ref, GAIN_MLP)
    shift = full_row(at, mine_ref, theirs_ref, SHIFT_MLP)
    h_ref[...] = (unit * gain + shift).astype(BF16)


def merge(place, x, ot, mine, theirs, weights):
    shape = x.shape
    operands = (x, ot, mine, theirs, *weights)
    return pl.pallas_call(
        merge_body,
        grid_spec=pltpu.PrefetchScalarGridSpec(
            num_scalar_prefetch=1,
            grid=(1,),
            in_specs=[whole(member.shape) for member in operands],
            out_specs=[whole(shape)] * 3,
        ),
        out_shape=[
            jax.ShapeDtypeStruct(shape, F32),
            jax.ShapeDtypeStruct(shape, BF16),
            jax.ShapeDtypeStruct(shape, BF16),
        ],
        compiler_params=params(),
        cost_estimate=about(1),
        name="merge",
    )(place, *operands)


def gelu_pair(inner):
    square = inner * inner
    bend = jnp.tanh(GELU_A * (inner + GELU_B * (inner * square)))
    active = 0.5 * inner * (1.0 + bend)
    slope = 0.5 * (1.0 + bend) + 0.5 * inner * (1.0 - bend * bend) * (GELU_A * (1.0 + 3.0 * GELU_B * square))
    return active, slope


def read_expand_bias(at, mine_ref, theirs_ref, bias_ref):
    count, wide = bias_ref.shape
    count = count // 2
    beside = mine_ref.shape[1] // wide
    for row in range(count):
        line = BIAS_EXPAND // 2 + row // beside
        lanes = slice(row % beside * wide, (row % beside + 1) * wide)
        mine = mine_ref[line : line + 1, lanes].astype(F32)
        theirs = theirs_ref[line : line + 1, lanes].astype(F32)
        bias_ref[row : row + 1, :] = jnp.where(at == 0, mine, theirs)
        bias_ref[count + row : count + row + 1, :] = jnp.where(at == 0, theirs, mine)


def mlp_body(
    place, x1_ref, h_ref, dy_ref, mine_ref, theirs_ref, mo_ref, mn_ref, mf_ref, eo_ref, en0_ref, en1_ref, ef0_ref,
    ef1_ref, own_ref, rest_ref, out_ref, dx_ref, da_ref, dot_ref, total_ref, dh_ref, bias_ref, sums_ref,
):
    at, core = place[0], place[1]
    step = pl.program_id(0)
    starts = piece_starts(at, core, mo_ref.shape[0])
    wide = eo_ref.shape[1]
    width = sums_ref.shape[1]
    beside = width // wide

    @pl.when(step == 0)
    def _():
        total_ref[...] = jnp.zeros_like(total_ref)
        dh_ref[...] = jnp.zeros_like(dh_ref)
        sums_ref[...] = jnp.zeros_like(sums_ref)
        read_expand_bias(at, mine_ref, theirs_ref, bias_ref)

    contract = contract_block(step, pl.num_programs(0), at, own_ref, rest_ref)
    expand = expand_pieces(step, pl.num_programs(0), eo_ref, en0_ref, en1_ref, ef0_ref, ef1_ref)
    inner = bias_ref[pl.ds(step, 1), :]
    for (begin, size), weight in zip(starts, expand):
        inner = inner + mm(h_ref[:, pl.ds(begin, size)], weight)
    active, slope = gelu_pair(inner)
    total_ref[...] += mm(active.astype(BF16), contract)
    grad = (mm_nt(dy_ref[...], contract) * slope).astype(BF16)
    sums_ref[
        pl.ds(SUM_EXPAND + step // beside, 1), pl.ds(pl.multiple_of(step % beside * wide, wide), wide)
    ] = jnp.sum(grad.astype(F32), axis=0, keepdims=True)
    for (begin, size), weight in zip(starts, expand):
        dh_ref[:, pl.ds(begin, size)] += mm_nt(grad, weight)

    @pl.when(step == pl.num_programs(0) - 1)
    def _():
        x1 = x1_ref[...]
        bias = full_row(at, mine_ref, theirs_ref, BIAS_CONTRACT)
        out_ref[...] = (x1 + total_ref[...] + bias).astype(BF16)
        gain = full_row(at, mine_ref, theirs_ref, GAIN_MLP)
        unit, inverse = normalise(x1)
        grad = dh_ref[...]
        dy = dy_ref[...].astype(F32)
        dx = dy + normalise_back(grad, unit, inverse, gain)
        dx_ref[...] = dx
        da = dx.astype(BF16)
        rows = da.shape[0]
        da_ref[:rows, :] = da
        sums_ref[0:1, :] = jnp.sum(dy, axis=0, keepdims=True)
        sums_ref[1:2, :] = jnp.sum(grad * unit, axis=0, keepdims=True)
        sums_ref[2:3, :] = jnp.sum(grad, axis=0, keepdims=True)
        sums_ref[3:4, :] = jnp.sum(da.astype(F32), axis=0, keepdims=True)
        da_ref[rows:, :] = sums_ref[...].astype(BF16)
        for (begin, size), weight in zip(starts, (mo_ref, mn_ref, mf_ref)):
            dot_ref[pl.ds(begin, size), :] = mm_nt(weight[...], da).astype(BF16)


def expand_pieces(block, blocks, own, near_low, near_high, far_low, far_high):
    low = block < blocks // 2
    return (
        own[...],
        jnp.where(low, near_low[...], near_high[...]),
        jnp.where(low, far_low[...], far_high[...]),
    )


def hidden_specs(expand, contract, wide, block_of):
    own = expand[0].shape[1] // wide
    each = expand[1].shape[1] // wide
    own_contract, rest = contract
    _, shard, width = rest.shape
    held = wide // shard
    specs = [pl.BlockSpec((expand[0].shape[0], wide), lambda i, s: (0, block_of(i, s)))]
    for index in range(1, 5):
        first = (index - 1) % 2 * each
        specs.append(
            pl.BlockSpec(
                (expand[index].shape[0], wide),
                lambda i, s, first=first: (0, jnp.clip(block_of(i, s) - first, 0, each - 1)),
            )
        )
    blocks = own // 2
    specs.append(
        pl.BlockSpec((wide, width), lambda i, s: (jnp.clip(block_of(i, s) - s[0] * blocks, 0, blocks - 1), 0))
    )
    specs.append(
        pl.BlockSpec(
            (held, shard, width), lambda i, s: (jnp.clip(block_of(i, s) - (1 - s[0]) * blocks, 0, blocks - 1), 0, 0)
        )
    )
    return specs


def contract_block(block, blocks, at, own_ref, rest_ref):
    wide, width = own_ref.shape
    return jnp.where(block // (blocks // 2) == at, own_ref[...], rest_ref[...].reshape(wide, width))


def mlp(place, x1, normed, dy, mine, theirs, merge_w, expand, contract):
    rows, width = x1.shape
    wide = 512
    steps = expand[0].shape[1] // wide
    sums = -(-(SUM_EXPAND + steps * wide // width) // 16) * 16
    operands = (x1, normed, dy, mine, theirs, *merge_w)
    in_specs = [whole(member.shape) for member in operands]
    in_specs += hidden_specs(expand, contract, wide, lambda i, _: i)
    shapes = [
        ((rows, width), BF16),
        ((rows, width), F32),
        ((rows + sums, width), BF16),
        ((width, rows), BF16),
    ]
    return pl.pallas_call(
        mlp_body,
        grid_spec=pltpu.PrefetchScalarGridSpec(
            num_scalar_prefetch=1,
            grid=(steps,),
            in_specs=in_specs,
            out_specs=[whole(shape) for shape, _ in shapes],
            scratch_shapes=[
                pltpu.VMEM((rows, width), F32),
                pltpu.VMEM((rows, width), F32),
                pltpu.VMEM((steps, wide), F32),
                pltpu.VMEM((sums, width), F32),
            ],
        ),
        out_shape=[jax.ShapeDtypeStruct(shape, dtype) for shape, dtype in shapes],
        compiler_params=params(),
        cost_estimate=about(1),
        name="mlp",
    )(place, *operands, *expand, *contract)


def hidden_part(step, at, core, own_steps):
    part = own_steps // 2
    return jnp.where(
        step < part, at * own_steps + core * part + step, (1 - at) * own_steps + core * part + step - part
    )


def tail_rows(merge_rows):
    return -(-(merge_rows + 2) // 16) * 16


def weights_body(own_steps, place, *refs):
    h_refs, dy_refs = refs[:4], refs[4:8]
    mine_ref, theirs_ref, eo_ref, en0_ref, en1_ref, ef0_ref, ef1_ref, own_ref, rest_ref = refs[8:17]
    contract_ref, out_ref, bias_ref, h_ref, turned_ref, dy_ref, act_ref, du_ref = refs[17:]
    at, core = place[0], place[1]
    step = pl.program_id(0)
    part = own_steps // 2
    half = eo_ref.shape[0]
    starts = piece_starts(at, core, half)
    block = hidden_part(step, at, core, own_steps)
    wide = eo_ref.shape[1]
    chips, _, width = out_ref.shape
    expand_rows = half // chips
    rows = h_refs[0].shape[0]
    some = 2 * rows

    @pl.when(step == 0)
    def _():
        read_expand_bias(at, mine_ref, theirs_ref, bias_ref)
        for index in range(4):
            here = slice(index * rows, (index + 1) * rows)
            h_ref[here, :] = h_refs[index][...]
            dy_ref[here, :] = dy_refs[index][...]
            mine = h_refs[index][:, pl.ds(pl.multiple_of(at * half, half), half)]
            turned_ref[:, here] = mine.astype(F32).T.astype(BF16)

    def work(forward):
        contract = contract_block(block, 2 * own_steps, at, own_ref, rest_ref)
        expand = expand_pieces(block, 2 * own_steps, eo_ref, en0_ref, en1_ref, ef0_ref, ef1_ref)
        for index in range(4 * rows // some):
            here = slice(index * some, (index + 1) * some)
            inner = bias_ref[pl.ds(block, 1), :]
            for (begin, size), weight in zip(starts, expand):
                inner = inner + mm(h_ref[here, pl.ds(begin, size)], weight)
            active, slope = gelu_pair(inner)
            if forward:
                act_ref[here, :] = active.astype(BF16)
            du_ref[here, :] = (mm_nt(dy_ref[here, :], contract) * slope).astype(BF16)
        return mm(turned_ref[...], du_ref[...]).astype(BF16)

    def store_expand(value, turn, column):
        own = pl.ds(pl.multiple_of(turn * expand_rows, expand_rows), expand_rows)
        for chip in range(chips):
            out_ref[chip, own, column * wide : (column + 1) * wide] = value[
                chip * expand_rows : (chip + 1) * expand_rows, :
            ]

    for now in range(part):

        @pl.when(step == now)
        def _():
            store_expand(work(True), at, now)
            contract_ref[now * wide : (now + 1) * wide, :] = mm_tn(act_ref[...], dy_ref[...]).astype(BF16)

        @pl.when(step == part + now)
        def _():
            store_expand(work(False), 1 - at, now)


def mlp_weights(place, chips, normed, dy, mine, theirs, expand, contract):
    rows, width = dy[0].shape
    wide = 512
    half = expand[0].shape[0]
    own_steps = expand[0].shape[1] // wide // 2
    part = own_steps // 2
    operands = (*normed, *dy, mine, theirs)
    in_specs = [whole(member.shape) for member in operands]
    in_specs += hidden_specs(expand, contract, wide, lambda i, s: hidden_part(i, s[0], s[1], own_steps))
    shapes = [(part * wide, width), (chips, 2 * (half // chips), width)]
    return pl.pallas_call(
        functools.partial(weights_body, own_steps),
        grid_spec=pltpu.PrefetchScalarGridSpec(
            num_scalar_prefetch=1,
            grid=(own_steps,),
            in_specs=in_specs,
            out_specs=[whole(shape) for shape in shapes],
            scratch_shapes=[
                pltpu.VMEM((2 * own_steps, wide), F32),
                pltpu.VMEM((4 * rows, width), BF16),
                pltpu.VMEM((half, 4 * rows), BF16),
                pltpu.VMEM((4 * rows, width), BF16),
                pltpu.VMEM((4 * rows, wide), BF16),
                pltpu.VMEM((4 * rows, wide), BF16),
            ],
        ),
        out_shape=[jax.ShapeDtypeStruct(shape, BF16) for shape in shapes],
        compiler_params=params(),
        cost_estimate=about(1),
        name="mlp_weights",
    )(place, *operands, *expand, *contract)


def merge_weights_body(hidden, place, *refs):
    o_refs, da_refs, out_ref = refs[:4], refs[4:8], refs[8]
    at, core = place[0], place[1]
    chips, tail, width = out_ref.shape
    half = width // 2
    tokens = o_refs[0].shape[0]
    total, sums = 0.0, 0.0
    for o_ref, da_ref in zip(o_refs, da_refs):
        total = total + mm_tn(o_ref[...], da_ref[:tokens, :])
        sums = sums + da_ref[tokens:, :].astype(F32)
    rows = total.shape[0] // chips
    for chip in range(chips):
        out_ref[chip, :rows, :] = total[chip * rows : (chip + 1) * rows, :].astype(BF16)
    out_ref[:, rows:, :] = jnp.zeros((chips, tail - rows, width), BF16)
    own = jnp.where(at == 0, sums[:, :half], sums[:, half:])
    own_hidden = jnp.where(at == 0, sums[SUM_EXPAND : SUM_EXPAND + hidden], sums[SUM_EXPAND + hidden : SUM_EXPAND + 2 * hidden])
    for row in range(2):
        vector = jnp.concatenate([own[2 * row : 2 * row + 1], own[2 * row + 1 : 2 * row + 2]], axis=1)
        vector = jnp.where(core == 0, vector, own_hidden[row : row + 1])
        out_ref[0, rows + row : rows + row + 1, :] = vector.astype(BF16)


def merge_weights(place, chips, mixed, grad, hidden):
    rows, width = mixed[0].shape
    quarter = mixed[1].shape[1]
    shape = (chips, tail_rows(quarter // chips), width)
    return pl.pallas_call(
        functools.partial(merge_weights_body, hidden // width // 2),
        grid_spec=pltpu.PrefetchScalarGridSpec(
            num_scalar_prefetch=1,
            grid=(1,),
            in_specs=[pl.BlockSpec((rows, quarter), lambda i, s: (0, 2 * s[0] + s[1]))]
            + [whole((rows, quarter))] * 3
            + [whole(grad[0].shape)] * 4,
            out_specs=whole(shape),
        ),
        out_shape=jax.ShapeDtypeStruct(shape, BF16),
        compiler_params=params(),
        cost_estimate=about(1),
        name="merge_weights",
    )(place, *mixed, *grad)


def spread_expand_body(in_ref, out_ref):
    rows, columns = out_ref.shape
    width = columns // 4
    for core in range(2):
        for part in range(2):
            column = (2 * part + core) * width
            out_ref[:, column : column + width] = in_ref[core, part * rows : (part + 1) * rows, :].astype(F32)


def spread_expand(gathered, shape):
    devices, rows, width = gathered.shape
    chips = devices // 2
    return pl.pallas_call(
        spread_expand_body,
        grid=(chips,),
        in_specs=[pl.BlockSpec((2, rows, width), lambda i: (i, 0, 0))],
        out_specs=pl.BlockSpec((shape[0] // chips, shape[1]), lambda i: (i, 0)),
        out_shape=jax.ShapeDtypeStruct(shape, F32),
        compiler_params=params(),
        cost_estimate=about(1),
        name="spread_expand",
    )(gathered)


def spread_contract_body(place, *refs):
    out_ref = refs[4]
    phase = 2 * pl.program_id(0) + pl.program_id(1)
    for index in range(4):

        @pl.when(phase == index)
        def _():
            out_ref[...] = refs[index][...].reshape(out_ref.shape).astype(F32)


def spread_contract(place, stacks, shape):
    ring, rows, width = stacks[0].shape

    def source(index):
        def block(i, j, k, s):
            phase = 2 * i + j
            slot = jnp.where(phase < index, 0, jnp.where(phase > index, ring - 1, k))
            return ((s[3] - slot + ring) % ring, 0, 0)

        return pl.BlockSpec((1, rows, width), block)

    def target(i, j, k, s):
        return (((i + s[1]) % 2 * 2 + (j + s[2]) % 2) * ring + k, 0)

    return pl.pallas_call(
        spread_contract_body,
        grid_spec=pltpu.PrefetchScalarGridSpec(
            num_scalar_prefetch=1,
            grid=(2, 2, ring),
            in_specs=[source(index) for index in range(4)],
            out_specs=pl.BlockSpec((rows, width), target),
        ),
        out_shape=jax.ShapeDtypeStruct(shape, F32),
        compiler_params=params(),
        cost_estimate=about(1),
        name="spread_contract",
    )(place, *stacks)


def heads_body(dp_ref, h_ref, out_ref):
    @pl.when(pl.program_id(0) == 0)
    def _():
        out_ref[...] = jnp.zeros_like(out_ref)

    _, parts, head, lanes = dp_ref.shape
    out_ref[...] += mm(dp_ref[0].reshape(parts * head, lanes), h_ref[0])


def heads_gradient(dp, normed):
    sources, parts, head, lanes = dp.shape
    width = normed.shape[2]
    return pl.pallas_call(
        heads_body,
        grid=(sources,),
        in_specs=[
            pl.BlockSpec((1, parts, head, lanes), lambda i: (i, 0, 0, 0)),
            pl.BlockSpec((1, lanes, width), lambda i: (i, 0, 0)),
        ],
        out_specs=whole((parts * head, width)),
        out_shape=jax.ShapeDtypeStruct((parts * head, width), F32),
        compiler_params=params(),
        cost_estimate=about(1),
        name="heads_gradient",
    )(dp, normed)


def spread_heads_body(begin, in_ref, heads_ref, merge_ref):
    heads, _, width = in_ref.shape
    half = width // 2
    rows = 3 * HEAD // 2
    some = 4
    for part in range(3):
        for first in range(0, heads, some):
            turned = []
            for head in range(first, first + some):
                for row in range(part * HEAD, (part + 1) * HEAD, 32):
                    side = row // rows
                    here = row - side * rows
                    turned.append(in_ref[head, here : here + 32, side * half : (side + 1) * half])
            piece = jnp.concatenate([member.astype(F32) for member in turned], axis=0)
            column = (part * heads + first) * HEAD
            heads_ref[:, column : column + some * HEAD] = piece.T
    if merge_ref is not None:
        spread_merge_body(begin, in_ref, merge_ref)


def spread_merge_body(begin, in_ref, merge_ref):
    _, chips, rows, _ = merge_ref.shape
    for chip in range(chips):
        for core in range(2):
            merge_ref[core, chip] = in_ref[2 * chip + core, begin : begin + rows, :].astype(F32)


def spread_heads(gathered, begin, shape, merge_shape):
    devices, _, width = gathered.shape
    chunked = (2, devices // 2, merge_shape[0] // devices, width)
    heads, merged = pl.pallas_call(
        functools.partial(spread_heads_body, begin),
        grid=(1,),
        in_specs=[whole(gathered.shape)],
        out_specs=[whole(shape), whole(chunked)],
        out_shape=[jax.ShapeDtypeStruct(shape, F32), jax.ShapeDtypeStruct(chunked, F32)],
        compiler_params=params(),
        cost_estimate=about(1),
        name="spread_heads",
    )(gathered)
    return heads, merged.reshape(merge_shape)


def back_body(
    place, dp_ref, x_ref, dx_ref, mine_ref, theirs_ref, own_ref, qn_ref, qf_ref, rn_ref, rf_ref, out_ref, sums_ref, dh_ref
):
    at, core = place[0], place[1]
    part = pl.program_id(0)
    starts = piece_starts(at, core, own_ref.shape[0])
    heads, _, head, rows = dp_ref.shape

    @pl.when(part == 0)
    def _():
        dh_ref[...] = jnp.zeros_like(dh_ref)
        sums_ref[...] = jnp.zeros_like(sums_ref)

    def work(weights):
        grad = dp_ref[...].reshape(heads * head, rows)
        for (begin, size), weight in zip(starts, weights):
            dh_ref[pl.ds(begin, size), :] += mm(weight[...], grad)
        return mm_nt(jnp.ones((8, rows), BF16), grad)[0:1, :]

    @pl.when(part == 0)
    def _():
        sums_ref[2:3, :] = work((own_ref, qn_ref, qf_ref))

    @pl.when(part == 1)
    def _():
        work((own_ref, rn_ref, rf_ref))

    @pl.when(part == 2)
    def _():
        sums_ref[3:4, :] = work((own_ref, rn_ref, rf_ref))
        dh = dh_ref[...].T
        unit, inverse = normalise(x_ref[...].astype(F32))
        gain = full_row(at, mine_ref, theirs_ref, GAIN_ATTN)
        out_ref[...] = dx_ref[...] + normalise_back(dh, unit, inverse, gain)
        sums_ref[0:1, :] = jnp.sum(dh * unit, axis=0, keepdims=True)
        sums_ref[1:2, :] = jnp.sum(dh, axis=0, keepdims=True)


def back(place, dp, x, dx, mine, theirs, own, query_w, rest_w):
    rows, width = x.shape
    heads, parts, head, _ = dp.shape
    vectors = (x, dx, mine, theirs)
    return pl.pallas_call(
        back_body,
        grid_spec=pltpu.PrefetchScalarGridSpec(
            num_scalar_prefetch=1,
            grid=(parts,),
            in_specs=[pl.BlockSpec((heads, 1, head, rows), lambda t, _: (0, t, 0, 0))]
            + [whole(member.shape) for member in vectors]
            + [pl.BlockSpec((own.shape[0], width), lambda t, _: (0, t))]
            + [whole(member.shape) for member in query_w]
            + [pl.BlockSpec((member.shape[0], width), lambda t, _: (0, jnp.maximum(t - 1, 0))) for member in rest_w],
            out_specs=[whole((rows, width)), whole((8, width))],
            scratch_shapes=[pltpu.VMEM((width, rows), F32)],
        ),
        out_shape=[
            jax.ShapeDtypeStruct((rows, width), F32),
            jax.ShapeDtypeStruct((8, width), F32),
        ],
        compiler_params=params(),
        cost_estimate=about(1),
        name="back",
    )(place, dp, *vectors, own, *query_w, *rest_w)


def after(value, *others):
    return lax.optimization_barrier((value,) + others)[0]


def per_device(
    mesh_sizes, tokens_in, gain_attn, shift_attn, w_heads, bias_query, bias_value, w_merge, bias_merge, gain_mlp, shift_mlp,
    w_expand, bias_expand, w_contract, bias_contract, cotangent,
):
    nctx = mesh_sizes[0]
    seqs, tokens, width = tokens_in.shape
    rows = seqs * tokens
    half = width // 2
    heads = width // HEAD
    hidden = w_expand.shape[1]
    pairs = seqs * heads
    same = max(1, nctx // pairs)
    per = max(1, pairs // nctx)
    groups = seqs // per
    ctx = lax.axis_index("ctx")
    at = lax.axis_index("fsdp")
    core = ctx % 2
    line, ring_at, ring = ctx // 2 % 2, ctx // 4, nctx // 4
    place = jnp.stack([at, core, line, ring_at, ctx]).astype(jnp.int32)

    def over_x(value):
        return lax.ppermute(value, "fsdp", [(0, 1), (1, 0)])

    def over_core(value):
        return lax.ppermute(value, "ctx", [(i, i ^ 1) for i in range(nctx)])

    def over_line(value):
        return lax.ppermute(value, "ctx", [(i, i ^ 2) for i in range(nctx)])

    def on_ring(value, by):
        return lax.ppermute(value, "ctx", [(i, (i + 4 * by) % nctx) for i in range(nctx)])

    def over_both(value):
        size = mesh_sizes[1]
        swap = [(i * size + j, (i ^ 1) * size + 1 - j) for i in range(nctx) for j in range(size)]
        return lax.ppermute(value, ("ctx", "fsdp"), swap)

    def exchange(value):
        return lax.all_to_all(value, "ctx", 0, 0)

    def to_send(value):
        lead = value.shape[1:-1]
        value = value.reshape((heads,) + lead + (groups, per * tokens))
        value = jnp.moveaxis(value, -2, 1).reshape((nctx // same,) + lead + (per * tokens,))
        return value if same == 1 else jnp.repeat(value, same, axis=0)

    def received(value):
        value = value[::same]
        lead = value.shape[1:-1]
        value = value.reshape((heads, groups) + lead + (per * tokens,))
        return jnp.moveaxis(value, 1, -2).reshape((heads,) + lead + (rows,))

    def quarter_of(weight, first, count):
        size = weight.shape[0] // 2
        return lax.dynamic_slice(weight, (core * size, first), (size, count))

    def halves(value):
        mine = lax.dynamic_index_in_dim(value, at, 0, keepdims=False)
        return mine + over_x(lax.dynamic_index_in_dim(value, 1 - at, 0, keepdims=False))

    vectors = (gain_attn, shift_attn, bias_query, bias_value, bias_merge, gain_mlp, shift_mlp, bias_contract, bias_expand)
    shard = w_contract.shape[0] // nctx
    first, mine = parcel(place, w_heads, w_contract, vectors, shard)
    first_near = over_x(first)
    rest_piece, first_near = lax.optimization_barrier((quarter_of(w_heads, width, 2 * width), first_near))
    query_near = first_near[: half // 2]
    theirs = first_near[half // 2 + shard :]
    contract = (w_contract, lax.all_gather(first_near[half // 2 : half // 2 + shard], "ctx", axis=0))
    query_w = (query_near, over_core(query_near))
    rest_near = over_x(rest_piece)
    merge_near = over_x(after(quarter_of(w_merge, 0, width), rest_near))
    expand_low = over_x(after(quarter_of(w_expand, 0, hidden // 2), rest_near))
    expand_high = over_x(after(quarter_of(w_expand, hidden // 2, hidden // 2), expand_low))

    x = tokens_in.reshape(rows, width)
    dy = cotangent.reshape(rows, width)
    dy_x = over_x(after(dy, expand_high))

    query_rows, normed = front_query(place, x, mine, theirs, w_heads, *query_w)
    query = exchange(to_send(query_rows))
    rest_w = (rest_near, over_core(after(rest_near, query)))
    kv = exchange(to_send(front_rest(place, after(normed, query), mine, theirs, w_heads, *rest_w)))
    normed_all = lax.all_gather(normed, "ctx", axis=0, tiled=False)
    mixed_b, mixed_f, lse = attend(query, kv, per)
    merge_w = (w_merge, merge_near, over_core(after(merge_near, kv)))
    expand_w = (
        w_expand, expand_low, expand_high, over_core(after(expand_low, kv)), over_core(after(expand_high, lse)),
    )
    mixed = received(exchange(mixed_b)).reshape(width, rows)
    x1, normed_two, mixed_rows = merge(place, x, mixed, mine, theirs, merge_w)

    def of_four(value, there):
        return value, there, over_core(value), over_core(there)

    def all_four(value):
        return value, over_x(value), over_core(value), over_both(value)

    def quarter_at(value, at, core):
        return lax.dynamic_slice_in_dim(value, (2 * at + core) * (width // 4), width // 4, 1)

    dy_four = of_four(after(dy, mixed), after(dy_x, mixed))
    normed_four = of_four(normed_two, over_x(normed_two))
    grad_contract, grad_expand = mlp_weights(
        place, nctx // 2, normed_four, dy_four, mine, theirs, expand_w, contract
    )
    chips = [[2 * chip + one for chip in range(nctx // 2)] for one in range(2)]
    grad_contract = grad_contract.reshape(2, ring, -1, width)
    to_line = lax.dynamic_index_in_dim(grad_contract, 1 - line, 0, keepdims=False)
    x1, to_line, grad_expand, normed_all = lax.optimization_barrier((x1, to_line, grad_expand, normed_all))
    reduced = lax.psum_scatter(grad_expand, "ctx", scatter_dimension=0, axis_index_groups=chips)
    contract_line = over_line(to_line)
    block_out, dx1, da, grad_mixed = mlp(
        place, x1, normed_two, dy, mine, theirs, merge_w, expand_w, contract
    )
    grad_out = exchange(to_send(grad_mixed.reshape(heads, HEAD, rows)))

    contract_half = lax.dynamic_index_in_dim(grad_contract, line, 0, keepdims=False).astype(F32)
    contract_half = (contract_half + after(contract_line, da).astype(F32)).astype(BF16)

    def chunk_of(by):
        return lax.dynamic_index_in_dim(contract_half, (ring_at + by) % ring, 0, keepdims=False)

    contract_parts = [on_ring(chunk_of(by), by) for by in range(1, ring)]

    mixed_four = (
        mixed_rows,
        over_x(quarter_at(mixed_rows, 1 - at, core)),
        over_core(quarter_at(mixed_rows, at, 1 - core)),
        over_both(quarter_at(mixed_rows, 1 - at, 1 - core)),
    )
    mixed_four = lax.optimization_barrier((mixed_four, da))[0]
    grads_four = of_four(da, over_x(da))
    grads_four, contract_half = lax.optimization_barrier((grads_four, contract_half))
    grad_merge = merge_weights(place, nctx // 2, mixed_four, grads_four, hidden)
    contract_sum = chunk_of(0).astype(F32)
    contract_parts, grad_merge = lax.optimization_barrier((contract_parts, grad_merge))
    for part in contract_parts:
        contract_sum = contract_sum + part.astype(F32)
    contract_sum = contract_sum.astype(BF16)
    grad_merge, grad_out, contract_sum = lax.optimization_barrier((grad_merge, grad_out, contract_sum))
    grad_merge = grad_merge.reshape((ring, 2) + grad_merge.shape[1:])
    merge_line = over_line(lax.dynamic_index_in_dim(grad_merge, 1 - line, 1, keepdims=False))

    dqkv = attend_back(query, kv, grad_out, mixed_f, lse, per)
    dp = received(exchange(dqkv))

    own_line = [on_ring(contract_sum, by) for by in range(1, ring)]
    own_line, dqkv = lax.optimization_barrier((own_line, dqkv))
    grad_expand = lax.all_gather(after(reduced, dqkv), "ctx", axis=0)
    own_line = jnp.stack([contract_sum] + own_line)
    other_line = over_line(own_line)
    merge_half = lax.dynamic_index_in_dim(grad_merge, line, 1, keepdims=False).astype(F32)
    merge_half = (merge_half + after(merge_line, dqkv).astype(F32)).astype(BF16)
    merge_parts = [
        on_ring(lax.dynamic_index_in_dim(merge_half, (ring_at + by) % ring, 0, keepdims=False), by)
        for by in range(1, ring)
    ]

    if groups > 1:
        normed_all = lax.dynamic_slice_in_dim(normed_all, (ctx // same % groups) * tokens * per, tokens * per, 1)
    grad_heads = heads_gradient(dqkv, normed_all)
    merge_parts = lax.optimization_barrier((merge_parts, grad_heads))[0]
    if groups > 1:
        members = [
            [first + one + same * group for group in range(groups)]
            for first in range(0, nctx, groups * same)
            for one in range(same)
        ]
        grad_heads = lax.psum(grad_heads, "ctx", axis_index_groups=members)
    kept = lax.dynamic_slice_in_dim(grad_heads, at * half, half, 1)
    sent = lax.dynamic_slice_in_dim(grad_heads, (1 - at) * half, half, 1)
    kept = (kept + over_x(sent.astype(BF16)).astype(F32)).astype(BF16)
    if groups * same > 1:
        share = kept.shape[0] // (groups * same)
        kept = lax.dynamic_slice_in_dim(kept, ctx % (groups * same) * share, share, 0)
    rows_here = kept.shape[0] // 2
    kept = jnp.concatenate([kept[:rows_here], kept[rows_here:]], axis=1)
    kept = jnp.pad(kept, ((0, -rows_here % 16), (0, 0)))
    own_merge = lax.dynamic_index_in_dim(merge_half, ring_at, 0, keepdims=False).astype(F32)
    for part in merge_parts:
        own_merge = own_merge + part.astype(F32)
    own_merge = own_merge.astype(BF16)
    spread = jnp.concatenate([kept, own_merge])
    spread, other_line, dp, grad_expand = lax.optimization_barrier((spread, other_line, dp, grad_expand))
    expand_sum = spread_expand(grad_expand, w_expand.shape)
    spread = lax.all_gather(spread, "ctx", axis=0, tiled=False)
    stacks = (own_line, other_line, over_core(own_line), over_core(other_line))
    contract_sum = spread_contract(place, stacks, w_contract.shape)
    begin = kept.shape[0]
    merge_rows = half // nctx
    first = begin + merge_rows
    vectors = spread[:2, first : first + 2].astype(F32)
    if groups * same == 1:
        heads_sum, merge_sum = spread_heads(spread, begin, w_heads.shape, w_merge.shape)
    else:
        by_head = spread[:, :rows_here].reshape(nctx, rows_here, 2, half)
        by_head = jnp.swapaxes(by_head, 1, 2).reshape(heads, 2, -1, half)
        by_head = jnp.swapaxes(by_head, 1, 2).reshape(heads, -1, width)
        merge_sum = spread[:, begin:first].reshape(nctx // 2, 2, merge_rows, width)
        merge_sum = jnp.swapaxes(merge_sum, 0, 1).reshape(heads, -1, width)
        heads_sum, merge_sum = spread_heads(
            jnp.concatenate([by_head, merge_sum], axis=1), by_head.shape[1], w_heads.shape, w_merge.shape
        )

    grad_tokens, sums_attn = back(place, dp, x, dx1, mine, theirs, w_heads, query_w, rest_w)
    last = halves(sums_attn[:4].reshape(4, 2, half).swapaxes(0, 1))
    last = jnp.sum(exchange(jnp.broadcast_to(last, (nctx,) + last.shape)), axis=0)
    return (
        block_out.reshape(tokens_in.shape),
        grad_tokens.reshape(tokens_in.shape),
        last[0],
        last[1],
        heads_sum,
        last[2],
        last[3],
        merge_sum,
        vectors[0, 1, half:],
        vectors[0, 0, half:],
        vectors[0, 1, :half],
        expand_sum,
        vectors[1].reshape(-1),
        contract_sum,
        vectors[0, 0, :half],
    )


def solution(mesh):
    rows, vec, mat = P("fsdp", "ctx", None), P("fsdp"), P("fsdp", None)
    return jax.shard_map(
        functools.partial(per_device, (mesh.shape["ctx"], mesh.shape["fsdp"])),
        mesh=mesh,
        in_specs=(rows, vec, vec, mat, vec, vec, mat, vec, vec, vec, mat, vec, mat, vec, rows),
        out_specs=(rows, rows, vec, vec, mat, vec, vec, mat, vec, vec, vec, mat, vec, mat, vec),
        check_vma=False,
    )
```

```python
import functools
import math

import jax
import jax.numpy as jnp
from jax import lax
from jax.experimental import pallas as pl
from jax.experimental.pallas import tpu as pltpu
from jax.sharding import PartitionSpec as P

HEAD = 64
EPS = 1e-05
LOWEST = -1e30
GELU_A = math.sqrt(2.0 / math.pi)
GELU_B = 0.044715
F32 = jnp.float32
BF16 = jnp.bfloat16
VMEM_BYTES = 62 * 1024 * 1024
GAIN_ATTN, SHIFT_ATTN, BIAS_QUERY, BIAS_VALUE = 0, 1, 2, 3
BIAS_MERGE, GAIN_MLP, SHIFT_MLP, BIAS_CONTRACT = 4, 5, 6, 7
BIAS_EXPAND = 8
SUM_EXPAND = 4


def mm(left, right):
    return jnp.dot(left, right, preferred_element_type=F32)


def mm_nt(left, right):
    return lax.dot_general(left, right, (((1,), (1,)), ((), ())), preferred_element_type=F32)


def mm_tn(left, right):
    return lax.dot_general(left, right, (((0,), (0,)), ((), ())), preferred_element_type=F32)


def params(**extra):
    return pltpu.CompilerParams(vmem_limit_bytes=VMEM_BYTES, **extra)


def about(us):
    return pl.CostEstimate(flops=int(us * 1.15e9), bytes_accessed=0, transcendentals=0)


def whole(shape):
    return pl.BlockSpec(shape, lambda *_: (0,) * len(shape))


def full_row(at, mine_ref, theirs_ref, row):
    half = mine_ref.shape[1] // 2
    line, lanes = row // 2, slice(row % 2 * half, (row % 2 + 1) * half)
    mine = mine_ref[line : line + 1, lanes].astype(F32)
    theirs = theirs_ref[line : line + 1, lanes].astype(F32)
    low = jnp.where(at == 0, mine, theirs)
    high = jnp.where(at == 0, theirs, mine)
    return jnp.concatenate([low, high], axis=1)


def normalise(rows):
    mean = jnp.mean(rows, axis=-1, keepdims=True)
    centered = rows - mean
    variance = jnp.mean(centered * centered, axis=-1, keepdims=True)
    inverse = lax.rsqrt(variance + EPS)
    return centered * inverse, inverse


def normalise_back(grad, unit, inverse, gain):
    scaled = grad * gain
    mean = jnp.mean(scaled, axis=-1, keepdims=True)
    along = jnp.mean(scaled * unit, axis=-1, keepdims=True)
    return inverse * (scaled - mean - unit * along)


def piece_starts(at, core, half):
    other = (1 - at) * half
    quarter = half // 2
    return (
        (pl.multiple_of(at * half, quarter), half),
        (pl.multiple_of(other + core * quarter, quarter), quarter),
        (pl.multiple_of(other + (1 - core) * quarter, quarter), quarter),
    )


def parcel_body(place, heads_ref, contract_ref, *refs):
    vectors, first_ref, mine_ref = refs[:9], refs[9], refs[10]
    quarter, shard = heads_ref.shape[0], contract_ref.shape[0]
    first_ref[:quarter, :] = heads_ref[...]
    first_ref[quarter : quarter + shard, :] = contract_ref[...]
    mine_ref[...] = jnp.zeros_like(mine_ref)
    at = 0
    width = mine_ref.shape[1]
    for vector in vectors:
        value = vector[...].astype(F32)
        size = min(value.shape[0], width)
        for begin in range(0, value.shape[0], size):
            line, lane = at // width, at % width
            piece = value[begin : begin + size].reshape(1, size)
            mine_ref[line : line + 1, lane : lane + size] = piece.astype(BF16)
            at += size
    first_ref[quarter + shard :, :] = mine_ref[...]


def parcel(place, w_heads, w_contract, vectors, shard):
    quarter, width = w_heads.shape[0] // 2, w_contract.shape[1]
    lines = -(-sum(vector.size for vector in vectors) // (16 * width)) * 16
    shapes = [(quarter + shard + lines, width), (lines, width)]
    return pl.pallas_call(
        parcel_body,
        grid_spec=pltpu.PrefetchScalarGridSpec(
            num_scalar_prefetch=1,
            grid=(1,),
            in_specs=[
                pl.BlockSpec((quarter, width), lambda i, s: (s[1], 0)),
                pl.BlockSpec((shard, width), lambda i, s: (s[4], 0)),
            ]
            + [whole(vector.shape) for vector in vectors],
            out_specs=[whole(shape) for shape in shapes],
        ),
        out_shape=[jax.ShapeDtypeStruct(shape, BF16) for shape in shapes],
        compiler_params=params(),
        cost_estimate=about(1),
        name="parcel",
    )(place, w_heads, w_contract, *vectors)


def project(at, core, normed, bias, own, near, far, out_ref, part):
    total = bias
    for (begin, size), weight in zip(piece_starts(at, core, own.shape[0]), (own, near, far)):
        total = total + mm(normed[:, pl.ds(begin, size)], weight[...])
    turned = total.T.astype(BF16)
    for head in range(turned.shape[0] // HEAD):
        piece = turned[head * HEAD : (head + 1) * HEAD, :]
        if part is None:
            out_ref[head] = piece
        else:
            out_ref[head, part] = piece


def front_query_body(place, x_ref, mine_ref, theirs_ref, own, near, far, out_ref, h_ref, bias_ref):
    at, core = place[0], place[1]
    step = pl.program_id(0)
    wide = own.shape[1]

    @pl.when(step == 0)
    def _():
        unit, _ = normalise(x_ref[...].astype(F32))
        gain = full_row(at, mine_ref, theirs_ref, GAIN_ATTN)
        shift = full_row(at, mine_ref, theirs_ref, SHIFT_ATTN)
        h_ref[...] = (unit * gain + shift).astype(BF16)
        bias_ref[0:1, :] = full_row(at, mine_ref, theirs_ref, BIAS_QUERY)

    columns = pl.ds(pl.multiple_of(step * wide, wide), wide)
    project(at, core, h_ref, bias_ref[0:1, columns], own, near, far, out_ref, None)


def front_query(place, x, mine, theirs, own, near, far):
    rows, width = x.shape
    heads = width // HEAD
    wide = 256
    return pl.pallas_call(
        front_query_body,
        grid_spec=pltpu.PrefetchScalarGridSpec(
            num_scalar_prefetch=1,
            grid=(width // wide,),
            in_specs=[whole(x.shape), whole(mine.shape), whole(theirs.shape)]
            + [pl.BlockSpec((member.shape[0], wide), lambda i, _: (0, i)) for member in (own, near, far)],
            out_specs=[
                pl.BlockSpec((wide // HEAD, HEAD, rows), lambda i, _: (i, 0, 0)),
                whole((rows, width)),
            ],
            scratch_shapes=[pltpu.VMEM((8, width), F32)],
        ),
        out_shape=[
            jax.ShapeDtypeStruct((heads, HEAD, rows), BF16),
            jax.ShapeDtypeStruct((rows, width), BF16),
        ],
        compiler_params=params(),
        cost_estimate=about(1),
        name="front_query",
    )(place, x, mine, theirs, own, near, far)


def front_rest_body(place, h_ref, mine_ref, theirs_ref, *rest):
    weights, (out_ref, bias_ref) = rest[:6], rest[6:]
    at, core = place[0], place[1]
    step = pl.program_id(0)
    wide = weights[0].shape[1]

    @pl.when(step == 0)
    def _():
        bias_ref[0:1, :] = jnp.zeros_like(bias_ref[0:1, :])
        bias_ref[1:2, :] = full_row(at, mine_ref, theirs_ref, BIAS_VALUE)

    columns = pl.ds(pl.multiple_of(step * wide, wide), wide)
    for part in range(2):
        bias = bias_ref[part : part + 1, columns]
        project(at, core, h_ref, bias, *weights[3 * part : 3 * part + 3], out_ref, part)


def front_rest(place, normed, mine, theirs, own, near, far):
    rows, width = normed.shape
    heads = width // HEAD
    wide = 256
    steps = width // wide
    specs = []
    for part in range(2):
        for member, skip in ((own, 1), (near, 0), (far, 0)):
            first = (part + skip) * steps
            specs.append(pl.BlockSpec((member.shape[0], wide), lambda i, _, first=first: (0, first + i)))
    return pl.pallas_call(
        front_rest_body,
        grid_spec=pltpu.PrefetchScalarGridSpec(
            num_scalar_prefetch=1,
            grid=(steps,),
            in_specs=[whole(normed.shape), whole(mine.shape), whole(theirs.shape)] + specs,
            out_specs=pl.BlockSpec((wide // HEAD, 2, HEAD, rows), lambda i, _: (i, 0, 0, 0)),
            scratch_shapes=[pltpu.VMEM((8, width), F32)],
        ),
        out_shape=jax.ShapeDtypeStruct((heads, 2, HEAD, rows), BF16),
        compiler_params=params(),
        cost_estimate=about(1),
        name="front_rest",
    )(place, normed, mine, theirs, *([own, near, far] * 2))


def lay_out(source, target, per, tokens, block, turned=False, scale=None):
    for src in range(source.shape[0]):
        for pair in range(per):
            piece = source[src, :, pair * tokens : (pair + 1) * tokens]
            if scale is not None:
                piece = piece * jnp.asarray(scale, BF16)
            begin = src * tokens
            if turned:
                target[pair, begin : begin + tokens, :] = piece.astype(F32).T.astype(BF16)
            else:
                inner = begin % block
                target[pair, begin // block, :, inner : inner + tokens] = piece


def allowed_at(first_key, first_query, keys, queries):
    key_at = first_key + lax.broadcasted_iota(jnp.int32, (keys, queries), 0)
    query_at = first_query + lax.broadcasted_iota(jnp.int32, (keys, queries), 1)
    return key_at <= query_at


def attend_body(per, tokens, block, chunk, query_ref, kv_ref, out_ref, outf_ref, lse_ref, q_ref, k_ref, v_ref):
    step = pl.program_id(0)

    @pl.when(step == 0)
    def _():
        lay_out(query_ref, q_ref, per, tokens, block, scale=HEAD**-0.5)
        lay_out(kv_ref.at[:, 0], k_ref, per, tokens, chunk, turned=True)
        lay_out(kv_ref.at[:, 1], v_ref, per, tokens, chunk)

    queries = [q_ref[pair, step] for pair in range(per)]

    def scores(pair, index):
        keys = k_ref[pair, pl.ds(pl.multiple_of(index * chunk, chunk), chunk), :]
        return mm(keys, queries[pair])

    last = (step * block) // chunk
    allowed = allowed_at(last * chunk, step * block, chunk, block)
    carried = []
    for pair in range(per):
        masked = jnp.where(allowed, scores(pair, last), LOWEST)
        top = jnp.max(masked, axis=0, keepdims=True)
        weights = jnp.exp(masked - top)
        total = jnp.sum(weights, axis=0, keepdims=True)
        mixed = mm(v_ref[pair, last], weights.astype(BF16))
        carried += [top, total, mixed]

    def one(index, state):
        fresh = []
        for pair in range(per):
            top, total, mixed = state[3 * pair : 3 * pair + 3]
            here = scores(pair, index)
            new_top = jnp.maximum(top, jnp.max(here, axis=0, keepdims=True))
            weights = jnp.exp(here - new_top)
            factor = jnp.exp(top - new_top)
            total = total * factor + jnp.sum(weights, axis=0, keepdims=True)
            mixed = mixed * factor + mm(v_ref[pair, index], weights.astype(BF16))
            fresh += [new_top, total, mixed]
        return tuple(fresh)

    final = lax.fori_loop(0, last, one, tuple(carried))
    for pair in range(per):
        top, total, mixed = final[3 * pair : 3 * pair + 3]
        mixed = mixed / total
        lse_ref[0, pair : pair + 1, :] = top + jnp.log(total)
        for dst in range(block // tokens):
            piece = mixed[:, dst * tokens : (dst + 1) * tokens]
            lanes = slice(pair * tokens, (pair + 1) * tokens)
            outf_ref[dst, :, lanes] = piece
            out_ref[dst, :, lanes] = piece.astype(BF16)


def attend(query, kv, per, block=512, chunk=512):
    sources, _, lanes = query.shape
    tokens = lanes // per
    length = sources * tokens
    steps = length // block
    here = pl.BlockSpec((block // tokens, HEAD, lanes), lambda i: (i, 0, 0))
    return pl.pallas_call(
        functools.partial(attend_body, per, tokens, block, chunk),
        grid=(steps,),
        in_specs=[whole(query.shape), whole(kv.shape)],
        out_specs=[here, here, pl.BlockSpec((1, 8, block), lambda i: (i, 0, 0))],
        out_shape=[
            jax.ShapeDtypeStruct((sources, HEAD, lanes), BF16),
            jax.ShapeDtypeStruct((sources, HEAD, lanes), F32),
            jax.ShapeDtypeStruct((steps, 8, block), F32),
        ],
        scratch_shapes=[
            pltpu.VMEM((per, steps, HEAD, block), BF16),
            pltpu.VMEM((per, length, HEAD), BF16),
            pltpu.VMEM((per, length // chunk, HEAD, chunk), BF16),
        ],
        compiler_params=params(),
        cost_estimate=about(1),
        name="attend",
    )(query, kv)


def attend_back_body(
    per, tokens, block, chunk, query_ref, kv_ref, go_ref, of_ref, lse_ref, out_ref, qt_ref, q_ref, kt_ref, k_ref, v_ref,
    dk_ref, dv_ref,
):
    sources = query_ref.shape[0]
    step = pl.program_id(0)

    @pl.when(step == 0)
    def _():
        lay_out(query_ref, qt_ref, per, tokens, block, scale=HEAD**-0.5)
        lay_out(query_ref, q_ref, per, tokens, block, turned=True, scale=HEAD**-0.5)
        lay_out(kv_ref.at[:, 0], kt_ref, per, tokens, chunk, scale=HEAD**-0.5)
        lay_out(kv_ref.at[:, 0], k_ref, per, tokens, chunk, turned=True)
        lay_out(kv_ref.at[:, 1], v_ref, per, tokens, chunk, turned=True)
        dk_ref[...] = jnp.zeros_like(dk_ref)
        dv_ref[...] = jnp.zeros_like(dv_ref)

    inner = block // tokens
    grads, deltas, lses, turned_grads, turned_queries, queries = [], [], [], [], [], []
    for pair in range(per):
        lanes = slice(pair * tokens, (pair + 1) * tokens)
        grad = jnp.concatenate([go_ref[dst, :, lanes] for dst in range(inner)], axis=1)
        mixed = jnp.concatenate([of_ref[dst, :, lanes] for dst in range(inner)], axis=1)
        wide = grad.astype(F32)
        grads.append(grad)
        deltas.append(jnp.sum(wide * mixed, axis=0, keepdims=True))
        turned_grads.append(wide.T.astype(BF16))
        lses.append(lse_ref[0, pair : pair + 1, :])
        queries.append(qt_ref[pair, step])
        turned_queries.append(q_ref[pair, pl.ds(pl.multiple_of(step * block, block), block), :])

    def one(index, state, allowed):
        rows = pl.ds(pl.multiple_of(index * chunk, chunk), chunk)
        fresh = []
        for pair in range(per):
            weights = jnp.exp(mm(k_ref[pair, rows, :], queries[pair]) - lses[pair])
            if allowed is not None:
                weights = jnp.where(allowed, weights, 0.0)
            back = mm(v_ref[pair, rows, :], grads[pair])
            dscore = (weights * (back - deltas[pair])).astype(BF16)
            dv_ref[pair, rows, :] += mm(weights.astype(BF16), turned_grads[pair])
            dk_ref[pair, rows, :] += mm(dscore, turned_queries[pair])
            fresh.append(state[pair] + mm(kt_ref[pair, index], dscore))
        return tuple(fresh)

    last = (step * block) // chunk
    start = tuple(jnp.zeros((HEAD, block), F32) for _ in range(per))
    state = lax.fori_loop(0, last, lambda i, s: one(i, s, None), start)
    state = one(last, state, allowed_at(last * chunk, step * block, chunk, block))
    for pair in range(per):
        lanes = slice(pair * tokens, (pair + 1) * tokens)
        for dst in range(inner):
            out_ref[step * inner + dst, 0, :, lanes] = state[pair][
                :, dst * tokens : (dst + 1) * tokens
            ].astype(BF16)

    @pl.when(step == pl.num_programs(0) - 1)
    def _():
        for pair in range(per):
            lanes = slice(pair * tokens, (pair + 1) * tokens)
            for src in range(sources):
                rows = slice(src * tokens, (src + 1) * tokens)
                out_ref[src, 1, :, lanes] = dk_ref[pair, rows, :].T.astype(BF16)
                out_ref[src, 2, :, lanes] = dv_ref[pair, rows, :].T.astype(BF16)


def attend_back(query, kv, grad, mixed, lse, per, chunk=512):
    sources, _, lanes = query.shape
    tokens = lanes // per
    length = sources * tokens
    steps, _, block = lse.shape
    here = pl.BlockSpec((block // tokens, HEAD, lanes), lambda i: (i, 0, 0))
    shape = (sources, 3, HEAD, lanes)
    return pl.pallas_call(
        functools.partial(attend_back_body, per, tokens, block, chunk),
        grid=(steps,),
        in_specs=[
            whole(query.shape), whole(kv.shape), here, here, pl.BlockSpec((1, 8, block), lambda i: (i, 0, 0)),
        ],
        out_specs=whole(shape),
        out_shape=jax.ShapeDtypeStruct(shape, BF16),
        scratch_shapes=[
            pltpu.VMEM((per, steps, HEAD, block), BF16),
            pltpu.VMEM((per, length, HEAD), BF16),
            pltpu.VMEM((per, length // chunk, HEAD, chunk), BF16),
            pltpu.VMEM((per, length, HEAD), BF16),
            pltpu.VMEM((per, length, HEAD), BF16),
            pltpu.VMEM((per, length, HEAD), F32),
            pltpu.VMEM((per, length, HEAD), F32),
        ],
        compiler_params=params(),
        cost_estimate=about(1),
        name="attend_back",
    )(query, kv, grad, mixed, lse)


def merge_body(place, x_ref, ot_ref, mine_ref, theirs_ref, mo_ref, mn_ref, mf_ref, x1_ref, h_ref, o_ref):
    at, core = place[0], place[1]
    starts = piece_starts(at, core, mo_ref.shape[0])
    o_ref[...] = ot_ref[...].astype(F32).T.astype(BF16)
    merged = full_row(at, mine_ref, theirs_ref, BIAS_MERGE)
    for (begin, size), weight in zip(starts, (mo_ref, mn_ref, mf_ref)):
        merged = merged + mm(o_ref[:, pl.ds(begin, size)], weight[...])
    x1 = x_ref[...].astype(F32) + merged
    x1_ref[...] = x1
    unit, _ = normalise(x1)
    gain = full_row(at, mine_ref, theirs_ref, GAIN_MLP)
    shift = full_row(at, mine_ref, theirs_ref, SHIFT_MLP)
    h_ref[...] = (unit * gain + shift).astype(BF16)


def merge(place, x, ot, mine, theirs, weights):
    shape = x.shape
    operands = (x, ot, mine, theirs, *weights)
    return pl.pallas_call(
        merge_body,
        grid_spec=pltpu.PrefetchScalarGridSpec(
            num_scalar_prefetch=1,
            grid=(1,),
            in_specs=[whole(member.shape) for member in operands],
            out_specs=[whole(shape)] * 3,
        ),
        out_shape=[
            jax.ShapeDtypeStruct(shape, F32),
            jax.ShapeDtypeStruct(shape, BF16),
            jax.ShapeDtypeStruct(shape, BF16),
        ],
        compiler_params=params(),
        cost_estimate=about(1),
        name="merge",
    )(place, *operands)


def gelu_pair(inner):
    square = inner * inner
    bend = jnp.tanh(GELU_A * (inner + GELU_B * (inner * square)))
    active = 0.5 * inner * (1.0 + bend)
    slope = 0.5 * (1.0 + bend) + 0.5 * inner * (1.0 - bend * bend) * (GELU_A * (1.0 + 3.0 * GELU_B * square))
    return active, slope


def read_expand_bias(at, mine_ref, theirs_ref, bias_ref):
    count, wide = bias_ref.shape
    count = count // 2
    beside = mine_ref.shape[1] // wide
    for row in range(count):
        line = BIAS_EXPAND // 2 + row // beside
        lanes = slice(row % beside * wide, (row % beside + 1) * wide)
        mine = mine_ref[line : line + 1, lanes].astype(F32)
        theirs = theirs_ref[line : line + 1, lanes].astype(F32)
        bias_ref[row : row + 1, :] = jnp.where(at == 0, mine, theirs)
        bias_ref[count + row : count + row + 1, :] = jnp.where(at == 0, theirs, mine)


def mlp_body(
    place, x1_ref, h_ref, dy_ref, mine_ref, theirs_ref, mo_ref, mn_ref, mf_ref, eo_ref, en0_ref, en1_ref, ef0_ref,
    ef1_ref, own_ref, rest_ref, out_ref, dx_ref, da_ref, dot_ref, total_ref, dh_ref, bias_ref, sums_ref,
):
    at, core = place[0], place[1]
    step = pl.program_id(0)
    starts = piece_starts(at, core, mo_ref.shape[0])
    wide = eo_ref.shape[1]
    width = sums_ref.shape[1]
    beside = width // wide

    @pl.when(step == 0)
    def _():
        total_ref[...] = jnp.zeros_like(total_ref)
        dh_ref[...] = jnp.zeros_like(dh_ref)
        sums_ref[...] = jnp.zeros_like(sums_ref)
        read_expand_bias(at, mine_ref, theirs_ref, bias_ref)

    contract = contract_block(step, pl.num_programs(0), at, own_ref, rest_ref)
    expand = expand_pieces(step, pl.num_programs(0), eo_ref, en0_ref, en1_ref, ef0_ref, ef1_ref)
    inner = bias_ref[pl.ds(step, 1), :]
    for (begin, size), weight in zip(starts, expand):
        inner = inner + mm(h_ref[:, pl.ds(begin, size)], weight)
    active, slope = gelu_pair(inner)
    total_ref[...] += mm(active.astype(BF16), contract)
    grad = (mm_nt(dy_ref[...], contract) * slope).astype(BF16)
    sums_ref[
        pl.ds(SUM_EXPAND + step // beside, 1), pl.ds(pl.multiple_of(step % beside * wide, wide), wide)
    ] = jnp.sum(grad.astype(F32), axis=0, keepdims=True)
    for (begin, size), weight in zip(starts, expand):
        dh_ref[:, pl.ds(begin, size)] += mm_nt(grad, weight)

    @pl.when(step == pl.num_programs(0) - 1)
    def _():
        x1 = x1_ref[...]
        bias = full_row(at, mine_ref, theirs_ref, BIAS_CONTRACT)
        out_ref[...] = (x1 + total_ref[...] + bias).astype(BF16)
        gain = full_row(at, mine_ref, theirs_ref, GAIN_MLP)
        unit, inverse = normalise(x1)
        grad = dh_ref[...]
        dy = dy_ref[...].astype(F32)
        dx = dy + normalise_back(grad, unit, inverse, gain)
        dx_ref[...] = dx
        da = dx.astype(BF16)
        rows = da.shape[0]
        da_ref[:rows, :] = da
        sums_ref[0:1, :] = jnp.sum(dy, axis=0, keepdims=True)
        sums_ref[1:2, :] = jnp.sum(grad * unit, axis=0, keepdims=True)
        sums_ref[2:3, :] = jnp.sum(grad, axis=0, keepdims=True)
        sums_ref[3:4, :] = jnp.sum(da.astype(F32), axis=0, keepdims=True)
        da_ref[rows:, :] = sums_ref[...].astype(BF16)
        for (begin, size), weight in zip(starts, (mo_ref, mn_ref, mf_ref)):
            dot_ref[pl.ds(begin, size), :] = mm_nt(weight[...], da).astype(BF16)


def expand_pieces(block, blocks, own, near_low, near_high, far_low, far_high):
    low = block < blocks // 2
    return (
        own[...],
        jnp.where(low, near_low[...], near_high[...]),
        jnp.where(low, far_low[...], far_high[...]),
    )


def hidden_specs(expand, contract, wide, block_of):
    own = expand[0].shape[1] // wide
    each = expand[1].shape[1] // wide
    own_contract, rest = contract
    _, shard, width = rest.shape
    held = wide // shard
    specs = [pl.BlockSpec((expand[0].shape[0], wide), lambda i, s: (0, block_of(i, s)))]
    for index in range(1, 5):
        first = (index - 1) % 2 * each
        specs.append(
            pl.BlockSpec(
                (expand[index].shape[0], wide),
                lambda i, s, first=first: (0, jnp.clip(block_of(i, s) - first, 0, each - 1)),
            )
        )
    blocks = own // 2
    specs.append(
        pl.BlockSpec((wide, width), lambda i, s: (jnp.clip(block_of(i, s) - s[0] * blocks, 0, blocks - 1), 0))
    )
    specs.append(
        pl.BlockSpec(
            (held, shard, width), lambda i, s: (jnp.clip(block_of(i, s) - (1 - s[0]) * blocks, 0, blocks - 1), 0, 0)
        )
    )
    return specs


def contract_block(block, blocks, at, own_ref, rest_ref):
    wide, width = own_ref.shape
    return jnp.where(block // (blocks // 2) == at, own_ref[...], rest_ref[...].reshape(wide, width))


def mlp(place, x1, normed, dy, mine, theirs, merge_w, expand, contract):
    rows, width = x1.shape
    wide = 512
    steps = expand[0].shape[1] // wide
    sums = -(-(SUM_EXPAND + steps * wide // width) // 16) * 16
    operands = (x1, normed, dy, mine, theirs, *merge_w)
    in_specs = [whole(member.shape) for member in operands]
    in_specs += hidden_specs(expand, contract, wide, lambda i, _: i)
    shapes = [
        ((rows, width), BF16),
        ((rows, width), F32),
        ((rows + sums, width), BF16),
        ((width, rows), BF16),
    ]
    return pl.pallas_call(
        mlp_body,
        grid_spec=pltpu.PrefetchScalarGridSpec(
            num_scalar_prefetch=1,
            grid=(steps,),
            in_specs=in_specs,
            out_specs=[whole(shape) for shape, _ in shapes],
            scratch_shapes=[
                pltpu.VMEM((rows, width), F32),
                pltpu.VMEM((rows, width), F32),
                pltpu.VMEM((steps, wide), F32),
                pltpu.VMEM((sums, width), F32),
            ],
        ),
        out_shape=[jax.ShapeDtypeStruct(shape, dtype) for shape, dtype in shapes],
        compiler_params=params(),
        cost_estimate=about(1),
        name="mlp",
    )(place, *operands, *expand, *contract)


def hidden_part(step, at, core, own_steps):
    part = own_steps // 2
    return jnp.where(
        step < part, at * own_steps + core * part + step, (1 - at) * own_steps + core * part + step - part
    )


def tail_rows(merge_rows):
    return -(-(merge_rows + 2) // 16) * 16


def weights_body(own_steps, place, *refs):
    h_refs, dy_refs = refs[:4], refs[4:8]
    mine_ref, theirs_ref, eo_ref, en0_ref, en1_ref, ef0_ref, ef1_ref, own_ref, rest_ref = refs[8:17]
    contract_ref, out_ref, bias_ref, h_ref, turned_ref, dy_ref, act_ref, du_ref = refs[17:]
    at, core = place[0], place[1]
    step = pl.program_id(0)
    part = own_steps // 2
    half = eo_ref.shape[0]
    starts = piece_starts(at, core, half)
    block = hidden_part(step, at, core, own_steps)
    wide = eo_ref.shape[1]
    chips, _, width = out_ref.shape
    expand_rows = half // chips
    rows = h_refs[0].shape[0]
    some = 2 * rows

    @pl.when(step == 0)
    def _():
        read_expand_bias(at, mine_ref, theirs_ref, bias_ref)
        for index in range(4):
            here = slice(index * rows, (index + 1) * rows)
            h_ref[here, :] = h_refs[index][...]
            dy_ref[here, :] = dy_refs[index][...]
            mine = h_refs[index][:, pl.ds(pl.multiple_of(at * half, half), half)]
            turned_ref[:, here] = mine.astype(F32).T.astype(BF16)

    def work(forward):
        contract = contract_block(block, 2 * own_steps, at, own_ref, rest_ref)
        expand = expand_pieces(block, 2 * own_steps, eo_ref, en0_ref, en1_ref, ef0_ref, ef1_ref)
        for index in range(4 * rows // some):
            here = slice(index * some, (index + 1) * some)
            inner = bias_ref[pl.ds(block, 1), :]
            for (begin, size), weight in zip(starts, expand):
                inner = inner + mm(h_ref[here, pl.ds(begin, size)], weight)
            active, slope = gelu_pair(inner)
            if forward:
                act_ref[here, :] = active.astype(BF16)
            du_ref[here, :] = (mm_nt(dy_ref[here, :], contract) * slope).astype(BF16)
        return mm(turned_ref[...], du_ref[...]).astype(BF16)

    def store_expand(value, turn, column):
        own = pl.ds(pl.multiple_of(turn * expand_rows, expand_rows), expand_rows)
        for chip in range(chips):
            out_ref[chip, own, column * wide : (column + 1) * wide] = value[
                chip * expand_rows : (chip + 1) * expand_rows, :
            ]

    for now in range(part):

        @pl.when(step == now)
        def _():
            store_expand(work(True), at, now)
            contract_ref[now * wide : (now + 1) * wide, :] = mm_tn(act_ref[...], dy_ref[...]).astype(BF16)

        @pl.when(step == part + now)
        def _():
            store_expand(work(False), 1 - at, now)


def mlp_weights(place, chips, normed, dy, mine, theirs, expand, contract):
    rows, width = dy[0].shape
    wide = 512
    half = expand[0].shape[0]
    own_steps = expand[0].shape[1] // wide // 2
    part = own_steps // 2
    operands = (*normed, *dy, mine, theirs)
    in_specs = [whole(member.shape) for member in operands]
    in_specs += hidden_specs(expand, contract, wide, lambda i, s: hidden_part(i, s[0], s[1], own_steps))
    shapes = [(part * wide, width), (chips, 2 * (half // chips), width)]
    return pl.pallas_call(
        functools.partial(weights_body, own_steps),
        grid_spec=pltpu.PrefetchScalarGridSpec(
            num_scalar_prefetch=1,
            grid=(own_steps,),
            in_specs=in_specs,
            out_specs=[whole(shape) for shape in shapes],
            scratch_shapes=[
                pltpu.VMEM((2 * own_steps, wide), F32),
                pltpu.VMEM((4 * rows, width), BF16),
                pltpu.VMEM((half, 4 * rows), BF16),
                pltpu.VMEM((4 * rows, width), BF16),
                pltpu.VMEM((4 * rows, wide), BF16),
                pltpu.VMEM((4 * rows, wide), BF16),
            ],
        ),
        out_shape=[jax.ShapeDtypeStruct(shape, BF16) for shape in shapes],
        compiler_params=params(),
        cost_estimate=about(1),
        name="mlp_weights",
    )(place, *operands, *expand, *contract)


def merge_weights_body(hidden, place, *refs):
    o_refs, da_refs, out_ref = refs[:4], refs[4:8], refs[8]
    at, core = place[0], place[1]
    chips, tail, width = out_ref.shape
    half = width // 2
    tokens = o_refs[0].shape[0]
    total, sums = 0.0, 0.0
    for o_ref, da_ref in zip(o_refs, da_refs):
        total = total + mm_tn(o_ref[...], da_ref[:tokens, :])
        sums = sums + da_ref[tokens:, :].astype(F32)
    rows = total.shape[0] // chips
    for chip in range(chips):
        out_ref[chip, :rows, :] = total[chip * rows : (chip + 1) * rows, :].astype(BF16)
    out_ref[:, rows:, :] = jnp.zeros((chips, tail - rows, width), BF16)
    own = jnp.where(at == 0, sums[:, :half], sums[:, half:])
    own_hidden = jnp.where(at == 0, sums[SUM_EXPAND : SUM_EXPAND + hidden], sums[SUM_EXPAND + hidden : SUM_EXPAND + 2 * hidden])
    for row in range(2):
        vector = jnp.concatenate([own[2 * row : 2 * row + 1], own[2 * row + 1 : 2 * row + 2]], axis=1)
        vector = jnp.where(core == 0, vector, own_hidden[row : row + 1])
        out_ref[0, rows + row : rows + row + 1, :] = vector.astype(BF16)


def merge_weights(place, chips, mixed, grad, hidden):
    rows, width = mixed[0].shape
    quarter = mixed[1].shape[1]
    shape = (chips, tail_rows(quarter // chips), width)
    return pl.pallas_call(
        functools.partial(merge_weights_body, hidden // width // 2),
        grid_spec=pltpu.PrefetchScalarGridSpec(
            num_scalar_prefetch=1,
            grid=(1,),
            in_specs=[pl.BlockSpec((rows, quarter), lambda i, s: (0, 2 * s[0] + s[1]))]
            + [whole((rows, quarter))] * 3
            + [whole(grad[0].shape)] * 4,
            out_specs=whole(shape),
        ),
        out_shape=jax.ShapeDtypeStruct(shape, BF16),
        compiler_params=params(),
        cost_estimate=about(1),
        name="merge_weights",
    )(place, *mixed, *grad)


def spread_expand_body(in_ref, out_ref):
    rows, columns = out_ref.shape
    width = columns // 4
    for core in range(2):
        for part in range(2):
            column = (2 * part + core) * width
            out_ref[:, column : column + width] = in_ref[core, part * rows : (part + 1) * rows, :].astype(F32)


def spread_expand(gathered, shape):
    devices, rows, width = gathered.shape
    chips = devices // 2
    return pl.pallas_call(
        spread_expand_body,
        grid=(chips,),
        in_specs=[pl.BlockSpec((2, rows, width), lambda i: (i, 0, 0))],
        out_specs=pl.BlockSpec((shape[0] // chips, shape[1]), lambda i: (i, 0)),
        out_shape=jax.ShapeDtypeStruct(shape, F32),
        compiler_params=params(),
        cost_estimate=about(1),
        name="spread_expand",
    )(gathered)


def spread_contract_body(place, *refs):
    out_ref = refs[4]
    phase = 2 * pl.program_id(0) + pl.program_id(1)
    for index in range(4):

        @pl.when(phase == index)
        def _():
            out_ref[...] = refs[index][...].reshape(out_ref.shape).astype(F32)


def spread_contract(place, stacks, shape):
    ring, rows, width = stacks[0].shape

    def source(index):
        def block(i, j, k, s):
            phase = 2 * i + j
            slot = jnp.where(phase < index, 0, jnp.where(phase > index, ring - 1, k))
            return ((s[3] - slot + ring) % ring, 0, 0)

        return pl.BlockSpec((1, rows, width), block)

    def target(i, j, k, s):
        return (((i + s[1]) % 2 * 2 + (j + s[2]) % 2) * ring + k, 0)

    return pl.pallas_call(
        spread_contract_body,
        grid_spec=pltpu.PrefetchScalarGridSpec(
            num_scalar_prefetch=1,
            grid=(2, 2, ring),
            in_specs=[source(index) for index in range(4)],
            out_specs=pl.BlockSpec((rows, width), target),
        ),
        out_shape=jax.ShapeDtypeStruct(shape, F32),
        compiler_params=params(),
        cost_estimate=about(1),
        name="spread_contract",
    )(place, *stacks)


def heads_body(dp_ref, h_ref, out_ref):
    @pl.when(pl.program_id(0) == 0)
    def _():
        out_ref[...] = jnp.zeros_like(out_ref)

    _, parts, head, lanes = dp_ref.shape
    out_ref[...] += mm(dp_ref[0].reshape(parts * head, lanes), h_ref[0])


def heads_gradient(dp, normed):
    sources, parts, head, lanes = dp.shape
    width = normed.shape[2]
    return pl.pallas_call(
        heads_body,
        grid=(sources,),
        in_specs=[
            pl.BlockSpec((1, parts, head, lanes), lambda i: (i, 0, 0, 0)),
            pl.BlockSpec((1, lanes, width), lambda i: (i, 0, 0)),
        ],
        out_specs=whole((parts * head, width)),
        out_shape=jax.ShapeDtypeStruct((parts * head, width), F32),
        compiler_params=params(),
        cost_estimate=about(1),
        name="heads_gradient",
    )(dp, normed)


def spread_heads_body(begin, in_ref, heads_ref, merge_ref):
    some, _, width = in_ref.shape
    half = width // 2
    rows = 3 * HEAD // 2
    now = pl.program_id(1)

    def turn(part):
        pieces = []
        for head in range(some):
            for row in range(part * HEAD, (part + 1) * HEAD, 32):
                side = row // rows
                here = row - side * rows
                pieces.append(in_ref[head, here : here + 32, side * half : (side + 1) * half].astype(F32))
        heads_ref[...] = jnp.concatenate(pieces, axis=0).T

    for part in range(3):

        @pl.when(now == part)
        def _():
            turn(part)

    @pl.when(now == 0)
    def _():
        _, chips, rows, _ = merge_ref.shape
        for chip in range(chips):
            for core in range(2):
                merge_ref[core, chip] = in_ref[2 * chip + core, begin : begin + rows, :].astype(F32)


def spread_heads(gathered, begin, shape, merge_shape):
    devices, rows, width = gathered.shape
    some = 4
    steps = devices // some
    chunked = (2, devices // 2, merge_shape[0] // devices, width)
    heads, merged = pl.pallas_call(
        functools.partial(spread_heads_body, begin),
        grid=(steps, 3),
        in_specs=[pl.BlockSpec((some, rows, width), lambda i, j: (i, 0, 0))],
        out_specs=[
            pl.BlockSpec((shape[0], some * HEAD), lambda i, j: (0, j * steps + i)),
            pl.BlockSpec((2, some // 2) + chunked[2:], lambda i, j: (0, i, 0, 0)),
        ],
        out_shape=[jax.ShapeDtypeStruct(shape, F32), jax.ShapeDtypeStruct(chunked, F32)],
        compiler_params=params(),
        cost_estimate=about(1),
        name="spread_heads",
    )(gathered)
    return heads, merged.reshape(merge_shape)


def back_body(
    place, dp_ref, x_ref, dx_ref, mine_ref, theirs_ref, own_ref, qn_ref, qf_ref, rn_ref, rf_ref, out_ref, sums_ref, dh_ref
):
    at, core = place[0], place[1]
    part = pl.program_id(0)
    starts = piece_starts(at, core, own_ref.shape[0])
    heads, _, head, rows = dp_ref.shape

    @pl.when(part == 0)
    def _():
        dh_ref[...] = jnp.zeros_like(dh_ref)
        sums_ref[...] = jnp.zeros_like(sums_ref)

    def work(weights):
        grad = dp_ref[...].reshape(heads * head, rows)
        for (begin, size), weight in zip(starts, weights):
            dh_ref[pl.ds(begin, size), :] += mm(weight[...], grad)
        return mm_nt(jnp.ones((8, rows), BF16), grad)[0:1, :]

    @pl.when(part == 0)
    def _():
        sums_ref[2:3, :] = work((own_ref, qn_ref, qf_ref))

    @pl.when(part == 1)
    def _():
        work((own_ref, rn_ref, rf_ref))

    @pl.when(part == 2)
    def _():
        sums_ref[3:4, :] = work((own_ref, rn_ref, rf_ref))
        dh = dh_ref[...].T
        unit, inverse = normalise(x_ref[...].astype(F32))
        gain = full_row(at, mine_ref, theirs_ref, GAIN_ATTN)
        out_ref[...] = dx_ref[...] + normalise_back(dh, unit, inverse, gain)
        sums_ref[0:1, :] = jnp.sum(dh * unit, axis=0, keepdims=True)
        sums_ref[1:2, :] = jnp.sum(dh, axis=0, keepdims=True)


def back(place, dp, x, dx, mine, theirs, own, query_w, rest_w):
    rows, width = x.shape
    heads, parts, head, _ = dp.shape
    vectors = (x, dx, mine, theirs)
    return pl.pallas_call(
        back_body,
        grid_spec=pltpu.PrefetchScalarGridSpec(
            num_scalar_prefetch=1,
            grid=(parts,),
            in_specs=[pl.BlockSpec((heads, 1, head, rows), lambda t, _: (0, t, 0, 0))]
            + [whole(member.shape) for member in vectors]
            + [pl.BlockSpec((own.shape[0], width), lambda t, _: (0, t))]
            + [whole(member.shape) for member in query_w]
            + [pl.BlockSpec((member.shape[0], width), lambda t, _: (0, jnp.maximum(t - 1, 0))) for member in rest_w],
            out_specs=[whole((rows, width)), whole((8, width))],
            scratch_shapes=[pltpu.VMEM((width, rows), F32)],
        ),
        out_shape=[
            jax.ShapeDtypeStruct((rows, width), F32),
            jax.ShapeDtypeStruct((8, width), F32),
        ],
        compiler_params=params(),
        cost_estimate=about(1),
        name="back",
    )(place, dp, *vectors, own, *query_w, *rest_w)


def after(value, *others):
    return lax.optimization_barrier((value,) + others)[0]


def per_device(
    mesh_sizes, tokens_in, gain_attn, shift_attn, w_heads, bias_query, bias_value, w_merge, bias_merge, gain_mlp, shift_mlp,
    w_expand, bias_expand, w_contract, bias_contract, cotangent,
):
    nctx = mesh_sizes[0]
    seqs, tokens, width = tokens_in.shape
    rows = seqs * tokens
    half = width // 2
    heads = width // HEAD
    hidden = w_expand.shape[1]
    pairs = seqs * heads
    same = max(1, nctx // pairs)
    per = max(1, pairs // nctx)
    groups = seqs // per
    ctx = lax.axis_index("ctx")
    at = lax.axis_index("fsdp")
    core = ctx % 2
    line, ring_at, ring = ctx // 2 % 2, ctx // 4, nctx // 4
    place = jnp.stack([at, core, line, ring_at, ctx]).astype(jnp.int32)

    def over_x(value):
        return lax.ppermute(value, "fsdp", [(0, 1), (1, 0)])

    def over_core(value):
        return lax.ppermute(value, "ctx", [(i, i ^ 1) for i in range(nctx)])

    def over_line(value):
        return lax.ppermute(value, "ctx", [(i, i ^ 2) for i in range(nctx)])

    def on_ring(value, by):
        return lax.ppermute(value, "ctx", [(i, (i + 4 * by) % nctx) for i in range(nctx)])

    def over_both(value):
        size = mesh_sizes[1]
        swap = [(i * size + j, (i ^ 1) * size + 1 - j) for i in range(nctx) for j in range(size)]
        return lax.ppermute(value, ("ctx", "fsdp"), swap)

    def exchange(value):
        return lax.all_to_all(value, "ctx", 0, 0)

    def to_send(value):
        lead = value.shape[1:-1]
        value = value.reshape((heads,) + lead + (groups, per * tokens))
        value = jnp.moveaxis(value, -2, 1).reshape((nctx // same,) + lead + (per * tokens,))
        return value if same == 1 else jnp.repeat(value, same, axis=0)

    def received(value):
        value = value[::same]
        lead = value.shape[1:-1]
        value = value.reshape((heads, groups) + lead + (per * tokens,))
        return jnp.moveaxis(value, 1, -2).reshape((heads,) + lead + (rows,))

    def quarter_of(weight, first, count):
        size = weight.shape[0] // 2
        return lax.dynamic_slice(weight, (core * size, first), (size, count))

    def halves(value):
        mine = lax.dynamic_index_in_dim(value, at, 0, keepdims=False)
        return mine + over_x(lax.dynamic_index_in_dim(value, 1 - at, 0, keepdims=False))

    vectors = (gain_attn, shift_attn, bias_query, bias_value, bias_merge, gain_mlp, shift_mlp, bias_contract, bias_expand)
    shard = w_contract.shape[0] // nctx
    first, mine = parcel(place, w_heads, w_contract, vectors, shard)
    first_near = over_x(first)
    rest_piece, first_near = lax.optimization_barrier((quarter_of(w_heads, width, 2 * width), first_near))
    query_near = first_near[: half // 2]
    theirs = first_near[half // 2 + shard :]
    contract = (w_contract, lax.all_gather(first_near[half // 2 : half // 2 + shard], "ctx", axis=0))
    query_w = (query_near, over_core(query_near))
    rest_near = over_x(rest_piece)
    merge_near = over_x(after(quarter_of(w_merge, 0, width), rest_near))
    expand_low = over_x(after(quarter_of(w_expand, 0, hidden // 2), rest_near))
    expand_high = over_x(after(quarter_of(w_expand, hidden // 2, hidden // 2), expand_low))

    x = tokens_in.reshape(rows, width)
    dy = cotangent.reshape(rows, width)
    dy_x = over_x(after(dy, expand_high))

    query_rows, normed = front_query(place, x, mine, theirs, w_heads, *query_w)
    query = exchange(to_send(query_rows))
    rest_w = (rest_near, over_core(after(rest_near, query)))
    kv = exchange(to_send(front_rest(place, after(normed, query), mine, theirs, w_heads, *rest_w)))
    normed_all = lax.all_gather(normed, "ctx", axis=0, tiled=False)
    mixed_b, mixed_f, lse = attend(query, kv, per)
    merge_w = (w_merge, merge_near, over_core(after(merge_near, kv)))
    expand_w = (
        w_expand, expand_low, expand_high, over_core(after(expand_low, kv)), over_core(after(expand_high, lse)),
    )
    mixed = received(exchange(mixed_b)).reshape(width, rows)
    x1, normed_two, mixed_rows = merge(place, x, mixed, mine, theirs, merge_w)

    def of_four(value, there):
        return value, there, over_core(value), over_core(there)

    def all_four(value):
        return value, over_x(value), over_core(value), over_both(value)

    def quarter_at(value, at, core):
        return lax.dynamic_slice_in_dim(value, (2 * at + core) * (width // 4), width // 4, 1)

    dy_four = of_four(after(dy, mixed), after(dy_x, mixed))
    normed_four = of_four(normed_two, over_x(normed_two))
    grad_contract, grad_expand = mlp_weights(
        place, nctx // 2, normed_four, dy_four, mine, theirs, expand_w, contract
    )
    chips = [[2 * chip + one for chip in range(nctx // 2)] for one in range(2)]
    grad_contract = grad_contract.reshape(2, ring, -1, width)
    to_line = lax.dynamic_index_in_dim(grad_contract, 1 - line, 0, keepdims=False)
    x1, to_line, grad_expand, normed_all = lax.optimization_barrier((x1, to_line, grad_expand, normed_all))
    reduced = lax.psum_scatter(grad_expand, "ctx", scatter_dimension=0, axis_index_groups=chips)
    contract_line = over_line(to_line)
    block_out, dx1, da, grad_mixed = mlp(
        place, x1, normed_two, dy, mine, theirs, merge_w, expand_w, contract
    )
    grad_out = exchange(to_send(grad_mixed.reshape(heads, HEAD, rows)))

    contract_half = lax.dynamic_index_in_dim(grad_contract, line, 0, keepdims=False).astype(F32)
    contract_half = (contract_half + after(contract_line, da).astype(F32)).astype(BF16)

    def chunk_of(by):
        return lax.dynamic_index_in_dim(contract_half, (ring_at + by) % ring, 0, keepdims=False)

    contract_parts = [on_ring(chunk_of(by), by) for by in range(1, ring)]

    mixed_four = (
        mixed_rows,
        over_x(quarter_at(mixed_rows, 1 - at, core)),
        over_core(quarter_at(mixed_rows, at, 1 - core)),
        over_both(quarter_at(mixed_rows, 1 - at, 1 - core)),
    )
    mixed_four = lax.optimization_barrier((mixed_four, da))[0]
    grads_four = of_four(da, over_x(da))
    grads_four, contract_half = lax.optimization_barrier((grads_four, contract_half))
    grad_merge = merge_weights(place, nctx // 2, mixed_four, grads_four, hidden)
    contract_sum = chunk_of(0).astype(F32)
    contract_parts, grad_merge = lax.optimization_barrier((contract_parts, grad_merge))
    for part in contract_parts:
        contract_sum = contract_sum + part.astype(F32)
    contract_sum = contract_sum.astype(BF16)
    grad_merge, grad_out, contract_sum = lax.optimization_barrier((grad_merge, grad_out, contract_sum))
    grad_merge = grad_merge.reshape((ring, 2) + grad_merge.shape[1:])
    merge_line = over_line(lax.dynamic_index_in_dim(grad_merge, 1 - line, 1, keepdims=False))

    dqkv = attend_back(query, kv, grad_out, mixed_f, lse, per)
    dp = received(exchange(dqkv))

    own_line = [on_ring(contract_sum, by) for by in range(1, ring)]
    own_line, dqkv = lax.optimization_barrier((own_line, dqkv))
    grad_expand = lax.all_gather(after(reduced, dqkv), "ctx", axis=0)
    own_line = jnp.stack([contract_sum] + own_line)
    other_line = over_line(own_line)
    merge_half = lax.dynamic_index_in_dim(grad_merge, line, 1, keepdims=False).astype(F32)
    merge_half = (merge_half + after(merge_line, dqkv).astype(F32)).astype(BF16)
    merge_parts = [
        on_ring(lax.dynamic_index_in_dim(merge_half, (ring_at + by) % ring, 0, keepdims=False), by)
        for by in range(1, ring)
    ]

    if groups > 1:
        normed_all = lax.dynamic_slice_in_dim(normed_all, (ctx // same % groups) * tokens * per, tokens * per, 1)
    grad_heads = heads_gradient(dqkv, normed_all)
    merge_parts = lax.optimization_barrier((merge_parts, grad_heads))[0]
    if groups > 1:
        members = [
            [first + one + same * group for group in range(groups)]
            for first in range(0, nctx, groups * same)
            for one in range(same)
        ]
        grad_heads = lax.psum(grad_heads, "ctx", axis_index_groups=members)
    kept = lax.dynamic_slice_in_dim(grad_heads, at * half, half, 1)
    sent = lax.dynamic_slice_in_dim(grad_heads, (1 - at) * half, half, 1)
    kept = (kept + over_x(sent.astype(BF16)).astype(F32)).astype(BF16)
    if groups * same > 1:
        share = kept.shape[0] // (groups * same)
        kept = lax.dynamic_slice_in_dim(kept, ctx % (groups * same) * share, share, 0)
    rows_here = kept.shape[0] // 2
    kept = jnp.concatenate([kept[:rows_here], kept[rows_here:]], axis=1)
    kept = jnp.pad(kept, ((0, -rows_here % 16), (0, 0)))
    own_merge = lax.dynamic_index_in_dim(merge_half, ring_at, 0, keepdims=False).astype(F32)
    for part in merge_parts:
        own_merge = own_merge + part.astype(F32)
    own_merge = own_merge.astype(BF16)
    spread = jnp.concatenate([kept, own_merge])
    spread, other_line, dp, grad_expand = lax.optimization_barrier((spread, other_line, dp, grad_expand))
    expand_sum = spread_expand(grad_expand, w_expand.shape)
    spread = lax.all_gather(spread, "ctx", axis=0, tiled=False)
    stacks = (own_line, other_line, over_core(own_line), over_core(other_line))
    contract_sum = spread_contract(place, stacks, w_contract.shape)
    begin = kept.shape[0]
    merge_rows = half // nctx
    first = begin + merge_rows
    vectors = spread[:2, first : first + 2].astype(F32)
    if groups * same == 1:
        heads_sum, merge_sum = spread_heads(spread, begin, w_heads.shape, w_merge.shape)
    else:
        by_head = spread[:, :rows_here].reshape(nctx, rows_here, 2, half)
        by_head = jnp.swapaxes(by_head, 1, 2).reshape(heads, 2, -1, half)
        by_head = jnp.swapaxes(by_head, 1, 2).reshape(heads, -1, width)
        merge_sum = spread[:, begin:first].reshape(nctx // 2, 2, merge_rows, width)
        merge_sum = jnp.swapaxes(merge_sum, 0, 1).reshape(heads, -1, width)
        heads_sum, merge_sum = spread_heads(
            jnp.concatenate([by_head, merge_sum], axis=1), by_head.shape[1], w_heads.shape, w_merge.shape
        )

    grad_tokens, sums_attn = back(place, dp, x, dx1, mine, theirs, w_heads, query_w, rest_w)
    last = halves(sums_attn[:4].reshape(4, 2, half).swapaxes(0, 1))
    last = jnp.sum(exchange(jnp.broadcast_to(last, (nctx,) + last.shape)), axis=0)
    return (
        block_out.reshape(tokens_in.shape),
        grad_tokens.reshape(tokens_in.shape),
        last[0],
        last[1],
        heads_sum,
        last[2],
        last[3],
        merge_sum,
        vectors[0, 1, half:],
        vectors[0, 0, half:],
        vectors[0, 1, :half],
        expand_sum,
        vectors[1].reshape(-1),
        contract_sum,
        vectors[0, 0, :half],
    )


def solution(mesh):
    rows, vec, mat = P("fsdp", "ctx", None), P("fsdp"), P("fsdp", None)
    return jax.shard_map(
        functools.partial(per_device, (mesh.shape["ctx"], mesh.shape["fsdp"])),
        mesh=mesh,
        in_specs=(rows, vec, vec, mat, vec, vec, mat, vec, vec, vec, mat, vec, mat, vec, rows),
        out_specs=(rows, rows, vec, vec, mat, vec, vec, mat, vec, vec, vec, mat, vec, mat, vec),
        check_vma=False,
    )
```
